32 devices in a mesh: ctx: 8 (over z, y), fsdp: 4 (over x, core).
Axes of the slice: x: 2, y: 2, z: 4, core: 2. Of those that a mesh axis runs over, the one named last changes fastest.
Arguments:
- inputs: bfloat16 [2, 2048, 1024], P(None, ('ctx', 'fsdp')), may hold values from -6 to 6
- attn_gain: bfloat16 [1024], P('fsdp'), may hold values from 0.5 to 1.5
- attn_proj: bfloat16 [1024, 3072], P('fsdp'), may hold values from -0.1875 to 0.1875
- attn_out: bfloat16 [1024, 1024], P('fsdp'), may hold values from -6 to 6
- mlp_gain: bfloat16 [1024], P('fsdp'), may hold values from 0.5 to 1.5
- mlp_in: bfloat16 [1024, 5248], P('fsdp'), may hold values from -0.1875 to 0.1875
- mlp_out: bfloat16 [2624, 1024], P('fsdp'), may hold values from -0.125 to 0.125
- cotangent: bfloat16 [2, 2048, 1024], P(None, ('ctx', 'fsdp')), may hold values from -6 to 6
Outputs:
- outputs: bfloat16 [2, 2048, 1024], P(None, ('ctx', 'fsdp'))
- input_grad: float32 [2, 2048, 1024], P(None, ('ctx', 'fsdp'))
- attn_gain_grad: float32 [1024], P('fsdp')
- attn_proj_grad: float32 [1024, 3072], P('fsdp')
- attn_out_grad: float32 [1024, 1024], P('fsdp')
- mlp_gain_grad: float32 [1024], P('fsdp')
- mlp_in_grad: float32 [1024, 5248], P('fsdp')
- mlp_out_grad: float32 [2624, 1024], P('fsdp')
The draws below stay inside these ranges and needn't reach their ends.
All inputs are finite; a program needn't handle non-finite values.
Results may differ from the reference program's by a relative error of at most 0.02.
Values may be sent and summed in bfloat16 or wider, within the bound.
A program may use at most 768 MiB of HBM per device.

```python
import jax
import jax.numpy as jnp
from jax import lax

D = 1024
HEADS = 16
HEAD_DIM = 64
FF = 2624
SEQS = 2
LEN = 2048


def block_levels(rng, extent, shards, smallest, top_value):
    gain = 1.0
    for dim, shards_of in shards:
        heights = jax.random.uniform(jax.random.fold_in(jax.random.fold_in(rng, 6), dim), (shards_of,), jnp.float32, smallest / len(shards), top_value / len(shards))
        gain = gain * jnp.repeat(jnp.exp(heights), extent[dim] // shards_of).reshape((-1,) + (1,) * (len(extent) - 1 - dim))
    return gain


def scatter_about(own_key, dims, width, reach, shards=(), kind=jnp.bfloat16):
    entries = jax.random.normal(own_key, dims, jnp.float32) * width
    if len(shards) > 0:
        entries = block_levels(own_key, dims, shards, -0.22, 0.18) * entries
    return jnp.clip(entries, min=-reach, max=reach).astype(kind)


def setup_inputs(seed: int = 0) -> dict:
    key_list = jax.random.split(jax.random.key(seed), 9)
    inputs = scatter_about(key_list[0], (SEQS, LEN, D), 1.0, 6.0, ((1, 32),))
    attn_gain = jnp.clip(1.0 + 0.1 * jax.random.normal(key_list[1], (D,), jnp.float32), 0.5, 1.5).astype(jnp.bfloat16)
    attn_proj = scatter_about(key_list[2], (D, 3 * D), D ** -0.5, 0.1875, ((0, 4),))
    attn_out = scatter_about(key_list[3], (D, D), (max(1, 3 * D // LEN)) ** -0.5, 6.0, ((0, 4),))
    mlp_gain = jnp.clip(1.0 + 0.1 * jax.random.normal(key_list[4], (D,), jnp.float32), 0.5, 1.5).astype(jnp.bfloat16)
    mlp_in = scatter_about(key_list[5], (D, 2 * FF), D ** -0.5, 0.1875, ((0, 4),))
    mlp_out = scatter_about(key_list[6], (FF, D), FF ** -0.5, 0.125, ((0, 4),))
    cotangent = scatter_about(key_list[7], (SEQS, LEN, D), 1.0, 6.0, ((1, 32),))
    return dict(inputs=inputs, attn_gain=attn_gain, attn_proj=attn_proj, attn_out=attn_out, mlp_gain=mlp_gain, mlp_in=mlp_in, mlp_out=mlp_out, cotangent=cotangent)


eps = 1e-05
rope_base = 160000.0
highest = lax.Precision.HIGHEST

@jax.custom_vjp
def low(v):
    return lax.optimization_barrier(v.astype(jnp.bfloat16)).astype(jnp.float32)

@jax.custom_vjp
def low_back(v):
    return v

def low_keep(v):
    return (low(v), None)

def low_pass(kept, grad):
    return (grad,)

def back_keep(v):
    return (v, None)

def back_low(kept, grad):
    return (low(grad),)
low.defvjp(low_keep, low_pass)
low_back.defvjp(back_keep, back_low)

def layer_norm(values, norm_gain):
    center = lax.optimization_barrier(jnp.mean(values, axis=-1, keepdims=True))
    centred = values - center
    spread = lax.optimization_barrier(jnp.mean(centred * centred, axis=-1, keepdims=True))
    return centred * lax.rsqrt(spread + eps) * norm_gain

def rotate(values, cos_table, sin_table):
    halfway = values.shape[-1] // 2
    turned = jnp.concatenate([-values[..., halfway:], values[..., :halfway]], axis=-1)
    return values * cos_table + turned * sin_table

def angles(positions, head_size):
    exponent = jnp.arange(0, head_size, 2, dtype=jnp.float32) / head_size
    inverse = rope_base ** (-exponent)
    phases = positions.astype(jnp.float32)[:, None] * inverse[None, :]
    phases = jnp.concatenate([phases, phases], axis=-1)
    return (jnp.cos(phases)[:, None, :], jnp.sin(phases)[:, None, :])

def attention(queries, key_rows, value_rows):
    group_size, length, head_count, head_size = queries.shape
    block_rows = min(512, length)
    scaling = head_size ** (-0.5)
    blocks = queries.reshape(group_size, length // block_rows, block_rows, head_count, head_size).transpose(1, 0, 2, 3, 4)

    def one_block(query_part):
        scores = low_back(jnp.einsum('gqhd,gkhd->ghqk', query_part, key_rows, precision=highest) * scaling)
        weights = low(jax.nn.softmax(scores, axis=-1))
        return jnp.einsum('ghqk,gkhd->gqhd', weights, value_rows, precision=highest)
    outcome = lax.map(jax.checkpoint(one_block), blocks)
    return outcome.transpose(1, 0, 2, 3, 4).reshape(group_size, length, head_count * head_size)

def forward(states, attn_gain, attn_proj, attn_out, mlp_gain, mlp_in, mlp_out):
    group_size, length, model_width = states.shape
    normed = low(layer_norm(states, attn_gain)).reshape(-1, model_width)
    mixed_rows = low_back(jnp.dot(normed, attn_proj, precision=highest))
    mixed_rows = mixed_rows.reshape(group_size, length, 3, HEADS, HEAD_DIM)
    cos_table, sin_table = angles(jnp.arange(length, dtype=jnp.int32), HEAD_DIM)
    queries = low(rotate(mixed_rows[:, :, 0], cos_table, sin_table))
    key_rows = low(rotate(mixed_rows[:, :, 1], cos_table, sin_table))
    value_rows = low(mixed_rows[:, :, 2])
    context = low(low_back(attention(queries, key_rows, value_rows).reshape(-1, model_width)))
    branch = low_back(jnp.dot(context, attn_out, precision=highest))
    middle = states + branch.reshape(group_size, length, model_width)
    normed_two = low(layer_norm(middle, mlp_gain)).reshape(-1, model_width)
    lifted = low_back(jnp.dot(normed_two, mlp_in, precision=highest))
    gate_out = low(jax.nn.gelu(lifted[:, :FF], approximate=False) * lifted[:, FF:])
    return middle + jnp.dot(gate_out, mlp_out, precision=highest).reshape(group_size, length, model_width)

def reference(inputs, attn_gain, attn_proj, attn_out, mlp_gain, mlp_in, mlp_out, cotangent):
    params = (attn_gain.astype(jnp.float32), attn_proj.astype(jnp.float32), attn_out.astype(jnp.float32), mlp_gain.astype(jnp.float32), mlp_in.astype(jnp.float32), mlp_out.astype(jnp.float32))
    group_size = min(SEQS, max(1, 4096 // LEN))
    group_count = SEQS // group_size
    states = inputs.astype(jnp.float32).reshape(group_count, group_size, LEN, D)
    seed_rows = cotangent.astype(jnp.float32).reshape(group_count, group_size, LEN, D)

    def one_group(totals, paired):
        result, pullback = jax.vjp(forward, paired[0], params[0], params[1], params[2], params[3], params[4], params[5])
        gradients = pullback(paired[1])
        totals = tuple((entry + update for entry, update in zip(totals, gradients[1:])))
        return (totals, (result.astype(jnp.bfloat16), gradients[0]))
    zero_sums = tuple((jnp.zeros_like(entry) for entry in params))
    totals, (outputs, input_grad) = lax.scan(one_group, zero_sums, (states, seed_rows))
    return (outputs.reshape(SEQS, LEN, D), input_grad.reshape(SEQS, LEN, D), totals[0], totals[1], totals[2], totals[3], totals[4], totals[5])
```

```python
import functools

import jax
import jax.numpy as jnp
from jax import lax
from jax.experimental import pallas as pl
from jax.experimental.pallas import tpu as pltpu
from jax.sharding import PartitionSpec as P

HEADS = 16
HEAD_DIM = 64


eps = 1e-05
rope_base = 160000.0


def layer_norm(values, norm_gain):
    center = jnp.mean(values, axis=-1, keepdims=True)
    centred = values - center
    spread = jnp.mean(centred * centred, axis=-1, keepdims=True)
    return centred * lax.rsqrt(spread + eps) * norm_gain


def rotate(values, cos_table, sin_table):
    halfway = values.shape[-1] // 2
    turned = jnp.concatenate([-values[..., halfway:], values[..., :halfway]], axis=-1)
    return values * cos_table + turned * sin_table


def unrotate(gradient, cos_table, sin_table):
    halfway = gradient.shape[-1] // 2
    sined = gradient * sin_table
    return gradient * cos_table + jnp.concatenate(
        [sined[..., halfway:], -sined[..., :halfway]], axis=-1
    )


def angles(positions, head_size):
    exponent = jnp.arange(0, head_size, 2, dtype=jnp.float32) / head_size
    inverse = rope_base ** (-exponent)
    phases = positions.astype(jnp.float32)[:, None] * inverse[None, :]
    phases = jnp.concatenate([phases, phases], axis=-1)
    return (jnp.cos(phases)[:, None, :], jnp.sin(phases)[:, None, :])


def gated_unit(lifted):
    hidden_units = lifted.shape[-1] // 2
    return jax.nn.gelu(lifted[..., :hidden_units], approximate=False) * lifted[..., hidden_units:]


def as_heads(flat_rows, head_size):
    return flat_rows.reshape(flat_rows.shape[0], flat_rows.shape[1], -1, head_size)


def empty_state(seq_count, head_count, query_rows, head_size):
    return (
        jnp.full((seq_count, head_count, query_rows), -jnp.inf, jnp.float32),
        jnp.zeros((seq_count, head_count, query_rows), jnp.float32),
        jnp.zeros((seq_count, head_count, query_rows, head_size), jnp.float32),
    )


def forward_step(queries, scaling, state_now, shard_part):
    running_max, denominator, weighted = state_now
    key_part = as_heads(shard_part[0], queries.shape[3])
    value_part = as_heads(shard_part[1], queries.shape[3])
    scores = (
        jnp.einsum("sqhd,skhd->shqk", queries, key_part, preferred_element_type=jnp.float32)
        * scaling
    )
    new_max = jnp.max(scores, axis=-1)
    fading = jnp.exp(running_max - new_max)
    weights = jnp.exp(scores - new_max[..., None])
    denominator = denominator * fading + jnp.sum(weights, axis=-1)
    weighted = weighted * fading[..., None] + jnp.einsum(
        "shqk,skhd->shqd",
        weights.astype(jnp.bfloat16),
        value_part,
        preferred_element_type=jnp.float32,
    )
    return (new_max, denominator, weighted)


def query_step(queries, grad_out, log_total, inner_heads, scaling, shard_part):
    key_part = as_heads(shard_part[0], queries.shape[3])
    value_part = as_heads(shard_part[1], queries.shape[3])
    scores = (
        jnp.einsum("sqhd,skhd->shqk", queries, key_part, preferred_element_type=jnp.float32)
        * scaling
    )
    weights = jnp.exp(scores - log_total[..., None])
    weight_grad = jnp.einsum(
        "sqhd,skhd->shqk", grad_out, value_part, preferred_element_type=jnp.float32
    )
    score_grad = (weights * (weight_grad - inner_heads[..., None])).astype(jnp.bfloat16)
    return jnp.einsum("shqk,skhd->sqhd", score_grad, key_part, preferred_element_type=jnp.float32)


def key_step(key_heads, value_heads, scaling, shard_part):
    head_size = key_heads.shape[3]
    query_part = as_heads(shard_part[0].astype(jnp.bfloat16), head_size)
    grad_part = as_heads(shard_part[1].astype(jnp.bfloat16), head_size)
    log_part = shard_part[2].transpose(0, 2, 1)
    inner_part = shard_part[3].transpose(0, 2, 1)
    scores = (
        jnp.einsum("sqhd,skhd->shqk", query_part, key_heads, preferred_element_type=jnp.float32)
        * scaling
    )
    weights = jnp.exp(scores - log_part[..., None])
    value_grad = jnp.einsum(
        "shqk,sqhd->skhd",
        weights.astype(jnp.bfloat16),
        grad_part,
        preferred_element_type=jnp.float32,
    )
    weight_grad = jnp.einsum(
        "sqhd,skhd->shqk", grad_part, value_heads, preferred_element_type=jnp.float32
    )
    score_grad = (weights * (weight_grad - inner_part[..., None])).astype(jnp.bfloat16)
    key_grad = jnp.einsum(
        "shqk,sqhd->skhd", score_grad, query_part, preferred_element_type=jnp.float32
    )
    return (key_grad, value_grad)


MESH_ID = pl.DeviceIdType.MESH


def exchange_kernel(ctx_count, fsdp_count, x_ref, o_ref, send_sem, recv_sem, own_sem):
    count = ctx_count * fsdp_count
    me = lax.axis_index("ctx") * fsdp_count + lax.axis_index("fsdp")
    barrier = pltpu.get_barrier_semaphore()

    def target(step):
        place = lax.rem(me + step, count)
        return place, (place // fsdp_count, lax.rem(place, fsdp_count))

    def copy_to(step):
        place, device = target(step)
        return pltpu.make_async_remote_copy(
            src_ref=x_ref.at[place],
            dst_ref=o_ref.at[me],
            send_sem=send_sem.at[step],
            recv_sem=recv_sem.at[step],
            device_id=device,
            device_id_type=MESH_ID,
        )

    @pl.loop(1, count)
    def _(step):
        pl.semaphore_signal(barrier, inc=1, device_id=target(step)[1], device_id_type=MESH_ID)

    pl.semaphore_wait(barrier, count - 1)
    own = pltpu.make_async_copy(x_ref.at[me], o_ref.at[me], own_sem)
    own.start()

    @pl.loop(1, count)
    def _(step):
        copy_to(step).start()

    own.wait()

    @pl.loop(1, count)
    def _(step):
        copy_to(step).wait()


def exchange(blocks, ctx_count, fsdp_count, collective_id):
    count = ctx_count * fsdp_count
    return pl.pallas_call(
        functools.partial(exchange_kernel, ctx_count, fsdp_count),
        out_shape=jax.ShapeDtypeStruct(blocks.shape, blocks.dtype),
        in_specs=[pl.BlockSpec(memory_space=pl.ANY)],
        out_specs=pl.BlockSpec(memory_space=pl.ANY),
        scratch_shapes=[
            pltpu.SemaphoreType.DMA((count,)),
            pltpu.SemaphoreType.DMA((count,)),
            pltpu.SemaphoreType.DMA,
        ],
        compiler_params=pltpu.CompilerParams(collective_id=collective_id, has_side_effects=True),
    )(blocks)


def gather_kernel(spread, chunks, x_ref, o_ref, send_sem, recv_sem, own_sem):
    ctx, place = lax.axis_index("ctx"), lax.axis_index("fsdp")
    across = lax.rem(place + 2, 4)
    beside = place + 1 - 2 * lax.rem(place, 2)
    half = lax.rem(ctx, 2)
    other_ctx = ctx + 1 - 2 * half
    sibling, partner, neighbour = (ctx, beside), (ctx, across), (other_ctx, place)
    width = x_ref.shape[-1] // (2 * chunks if spread else chunks)
    mine = half * chunks if spread else 0
    theirs = (1 - half) * chunks

    def columns(index):
        return pl.ds(pl.multiple_of(index * width, 128), width)

    def send(src, dst, sem, device):
        return pltpu.make_async_remote_copy(
            src_ref=src,
            dst_ref=dst,
            send_sem=send_sem.at[sem],
            recv_sem=recv_sem.at[sem],
            device_id=device,
            device_id_type=MESH_ID,
        )

    def piece(index):
        return o_ref.at[across, :, columns(index)]

    barrier = pltpu.get_barrier_semaphore()
    partners = (sibling, partner, neighbour) if spread else (sibling, partner)
    for device in partners:
        pl.semaphore_signal(barrier, inc=1, device_id=device, device_id_type=MESH_ID)
    pl.semaphore_wait(barrier, len(partners))
    crossing = [
        send(
            x_ref.at[:, columns(mine + c)],
            o_ref.at[place, :, columns(mine + c)],
            c,
            partner,
        )
        for c in range(chunks)
    ]
    for copy in crossing:
        copy.start()
    started = list(crossing)
    whole = send(x_ref, o_ref.at[place], chunks, sibling)
    whole.start()
    own = pltpu.make_async_copy(x_ref, o_ref.at[place], own_sem)
    own.start()
    turned = []
    for c in range(chunks):
        crossing[c].wait_recv()
        if spread:
            turn = send(piece(mine + c), piece(mine + c), chunks + 1 + c, neighbour)
            turn.start()
            turned.append(turn)
        hand = send(piece(mine + c), piece(mine + c), 2 * chunks + 1 + c, sibling)
        hand.start()
        started.append(hand)
    handed = started[chunks:]
    for c in range(len(turned)):
        turned[c].wait_recv()
        hand = send(piece(theirs + c), piece(theirs + c), 3 * chunks + 1 + c, sibling)
        hand.start()
        handed.append(hand)
    whole.wait_recv()
    own.wait()
    for hand in handed:
        hand.wait_recv()
    for copy in crossing + turned + handed + [whole]:
        copy.wait_send()


def gather(block, spread, chunks, collective_id):
    rows, width = block.shape
    count = 4 * chunks + 1
    return pl.pallas_call(
        functools.partial(gather_kernel, spread, chunks),
        out_shape=jax.ShapeDtypeStruct((4, rows, width), block.dtype),
        in_specs=[pl.BlockSpec(memory_space=pl.ANY)],
        out_specs=pl.BlockSpec(memory_space=pl.ANY),
        scratch_shapes=[
            pltpu.SemaphoreType.DMA((count,)),
            pltpu.SemaphoreType.DMA((count,)),
            pltpu.SemaphoreType.DMA,
        ],
        compiler_params=pltpu.CompilerParams(collective_id=collective_id, has_side_effects=True),
    )(block).reshape(4 * rows, width)


TILE = 16
SLICE = 1536


def total_kernel(pair, lone, x_ref, o_ref, y_got, z_got, z_sent, e_got, send_sem, recv_sem):
    ctx, place = lax.axis_index("ctx"), lax.axis_index("fsdp")
    y = lax.rem(ctx, 2)
    z = ctx // 2
    firsts, lasts = 2 * pair, 2 * lone
    every = firsts + lasts

    def send(src, dst, sem, to_ctx):
        return pltpu.make_async_remote_copy(
            src_ref=src,
            dst_ref=dst,
            send_sem=send_sem.at[sem],
            recv_sem=recv_sem.at[sem],
            device_id=(to_ctx, place),
            device_id_type=MESH_ID,
        )

    y_side = ctx + 1 - 2 * y

    def rows(item, side):
        if item < firsts:
            return pl.ds(pl.multiple_of((side * firsts + item) * TILE, TILE), TILE)
        return pl.ds((firsts + item) * TILE, TILE)

    def end_of(item):
        return item // pair if item < firsts else (item - firsts) // lone

    def turn_of(item):
        return item % pair if item < firsts else (item - firsts) % lone

    def add(store, store_rows, terms):
        @pl.loop(0, x_ref.shape[1] // SLICE)
        def _(i):
            columns = pl.ds(pl.multiple_of(i * SLICE, SLICE), SLICE)
            total = terms[0][0][terms[0][1], columns].astype(jnp.float32)
            for ref, place_rows in terms[1:]:
                total += ref[place_rows, columns].astype(jnp.float32)
            store[store_rows, columns] = total.astype(jnp.bfloat16)

    def slot(item):
        return pl.ds(item * TILE, TILE)

    def pair_copy(item):
        return send(x_ref.at[rows(item, 1 - y), :], y_got.at[slot(item), :], item, y_side)

    def up_copy(item, to_z):
        return send(z_sent.at[slot(item), :], z_got.at[slot(item), :], firsts + item, 2 * to_z + y)

    def end_copy(item):
        return send(
            z_sent.at[slot(item), :],
            e_got.at[slot(item - firsts), :],
            firsts + every + item - firsts,
            y_side,
        )

    def down_copy(item, to_z):
        here = rows(item, y)
        return send(
            o_ref.at[here, :], o_ref.at[here, :], firsts + every + lasts + item, 2 * to_z + y
        )

    def back_copy(item):
        here = rows(item, y)
        return send(
            o_ref.at[here, :], o_ref.at[here, :], firsts + 2 * every + lasts + item, y_side
        )

    barrier = pltpu.get_barrier_semaphore()
    pl.semaphore_signal(barrier, inc=1, device_id=(y_side, place), device_id_type=MESH_ID)

    @pl.when(z > 0)
    def _():
        pl.semaphore_signal(barrier, inc=1, device_id=(ctx - 2, place), device_id_type=MESH_ID)

    @pl.when(z < 3)
    def _():
        pl.semaphore_signal(barrier, inc=1, device_id=(ctx + 2, place), device_id_type=MESH_ID)

    @pl.when((z == 0) | (z == 3))
    def _():
        pl.semaphore_wait(barrier, 2)

    @pl.when((z > 0) & (z < 3))
    def _():
        pl.semaphore_wait(barrier, 3)

    for turn in range(pair):
        for end in range(2):
            pair_copy(end * pair + turn).start()

    def steps(my_z):
        depth = lambda item: 3 - my_z if end_of(item) == 0 else my_z
        toward = lambda item: my_z - 1 if end_of(item) == 0 else my_z + 1
        away = lambda item: my_z + 1 if end_of(item) == 0 else my_z - 1
        events = []
        for item in range(every):
            wait = 1 if item < firsts else 0
            late = 0 if item < firsts else 1
            at = 2 * turn_of(item) + depth(item) + wait
            events.append((at, item, "up"))
            if depth(item) == 3 and late:
                events.append((at + 1, item, "meet"))
            if depth(item) < 3:
                events.append(
                    (2 * turn_of(item) + 3 + wait + late + 3 - depth(item), item, "down")
                )
        pending = []

        def start(copy):
            copy.start()
            pending.append(copy)

        def finish(item):
            if depth(item) > 0:
                start(down_copy(item, away(item)))
            if item < firsts:
                start(back_copy(item))

        for _, item, kind in sorted(events):
            if kind == "up":
                terms = [(x_ref, rows(item, y))]
                if item < firsts:
                    pair_copy(item).wait_recv()
                    terms.append((y_got, slot(item)))
                if depth(item) > 0:
                    up_copy(item, away(item)).wait_recv()
                    terms.append((z_got, slot(item)))
                if depth(item) == 3 and item < firsts:
                    add(o_ref, rows(item, y), terms)
                    finish(item)
                else:
                    add(z_sent, slot(item), terms)
                    if depth(item) == 3:
                        start(end_copy(item))
                    else:
                        start(up_copy(item, toward(item)))
            elif kind == "meet":
                end_copy(item).wait_recv()
                add(
                    o_ref,
                    rows(item, y),
                    [(z_sent, slot(item)), (e_got, slot(item - firsts))],
                )
                finish(item)
            else:
                down_copy(item, toward(item)).wait_recv()
                finish(item)
        for copy in pending:
            copy.wait_send()

    for my_z in range(4):
        pl.when(z == my_z)(functools.partial(steps, my_z))

    for item in range(firsts):
        pair_copy(item).wait_send()
        send(
            o_ref.at[rows(item, y), :],
            o_ref.at[rows(item, 1 - y), :],
            firsts + 2 * every + lasts + item,
            y_side,
        ).wait_recv()


def total_over_ctx(grads, collective_id):
    rows, width = grads.shape
    chunks = rows // TILE
    pair, lone = chunks // 8, chunks // 4
    items = 2 * pair + 2 * lone
    sems = 4 * pair + 2 * items + 2 * lone
    low = lambda count: pltpu.VMEM((count * TILE, width), jnp.bfloat16)
    return pl.pallas_call(
        functools.partial(total_kernel, pair, lone),
        out_shape=jax.ShapeDtypeStruct((rows, width), jnp.bfloat16),
        in_specs=[pl.BlockSpec(memory_space=pltpu.VMEM)],
        out_specs=pl.BlockSpec(memory_space=pltpu.VMEM),
        scratch_shapes=[
            low(2 * pair),
            low(items),
            low(items),
            low(2 * lone),
            pltpu.SemaphoreType.DMA((sems,)),
            pltpu.SemaphoreType.DMA((sems,)),
        ],
        compiler_params=pltpu.CompilerParams(
            collective_id=collective_id,
            has_side_effects=True,
            vmem_limit_bytes=48 * 1024 * 1024,
        ),
    )(grads)


def pack(blocks):
    half = blocks.shape[-2] // 2
    return jnp.concatenate([blocks[..., :half, :], blocks[..., half:, :]], axis=-1)


def unpack(blocks):
    half = blocks.shape[-1] // 2
    return jnp.concatenate([blocks[..., :half], blocks[..., half:]], axis=-2)


CONTRACT_LAST = (((1,), (1,)), ((), ()))
CONTRACT_FIRST = (((0,), (0,)), ((), ()))


def attend_kernel(q_ref, k_ref, v_ref, context_ref, log_ref):
    scores = lax.dot_general(
        q_ref[...], k_ref[...], CONTRACT_LAST, preferred_element_type=jnp.float32
    )
    top = jnp.max(scores, axis=-1, keepdims=True)
    weights = jnp.exp(scores - top)
    total = jnp.sum(weights, axis=-1, keepdims=True)
    weighted = jnp.dot(
        weights.astype(jnp.bfloat16), v_ref[...], preferred_element_type=jnp.float32
    )
    context_ref[...] = weighted / total
    log_ref[...] = top + jnp.log(total)


def attend(queries, key_rows, value_rows, block):
    rows, size = queries.shape
    return pl.pallas_call(
        attend_kernel,
        grid=(rows // block,),
        out_shape=(
            jax.ShapeDtypeStruct((rows, size), jnp.float32),
            jax.ShapeDtypeStruct((rows, 1), jnp.float32),
        ),
        in_specs=[
            pl.BlockSpec((block, size), lambda i: (i, 0)),
            pl.BlockSpec((rows, size), lambda i: (0, 0)),
            pl.BlockSpec((rows, size), lambda i: (0, 0)),
        ],
        out_specs=(
            pl.BlockSpec((block, size), lambda i: (i, 0)),
            pl.BlockSpec((block, 1), lambda i: (i, 0)),
        ),
        compiler_params=pltpu.CompilerParams(vmem_limit_bytes=48 * 1024 * 1024),
    )(queries, key_rows, value_rows)


def attend_back_kernel(
    q_ref, k_ref, v_ref, context_ref, log_ref, grad_ref, dq_ref, dk_ref, dv_ref
):
    @pl.when(pl.program_id(0) == 0)
    def _():
        dk_ref[...] = jnp.zeros_like(dk_ref)
        dv_ref[...] = jnp.zeros_like(dv_ref)

    grad = grad_ref[...]
    inner = jnp.sum(grad.astype(jnp.float32) * context_ref[...], axis=-1, keepdims=True)
    scores = lax.dot_general(
        q_ref[...], k_ref[...], CONTRACT_LAST, preferred_element_type=jnp.float32
    )
    probs = jnp.exp(scores - log_ref[...])
    prob_grad = lax.dot_general(
        grad, v_ref[...], CONTRACT_LAST, preferred_element_type=jnp.float32
    )
    score_grad = (probs * (prob_grad - inner)).astype(jnp.bfloat16)
    dv_ref[...] += lax.dot_general(
        probs.astype(jnp.bfloat16), grad, CONTRACT_FIRST, preferred_element_type=jnp.float32
    )
    dk_ref[...] += lax.dot_general(
        score_grad, q_ref[...], CONTRACT_FIRST, preferred_element_type=jnp.float32
    )
    dq_ref[...] = jnp.dot(score_grad, k_ref[...], preferred_element_type=jnp.float32)


def attend_back(queries, key_rows, value_rows, context, log_total, grad, block):
    rows, size = queries.shape
    part = pl.BlockSpec((block, size), lambda i: (i, 0))
    whole = pl.BlockSpec((rows, size), lambda i: (0, 0))
    return pl.pallas_call(
        attend_back_kernel,
        grid=(rows // block,),
        out_shape=(jax.ShapeDtypeStruct((rows, size), jnp.float32),) * 3,
        in_specs=[
            part,
            whole,
            whole,
            part,
            pl.BlockSpec((block, 1), lambda i: (i, 0)),
            part,
        ],
        out_specs=(part, whole, whole),
        compiler_params=pltpu.CompilerParams(vmem_limit_bytes=48 * 1024 * 1024),
    )(queries, key_rows, value_rows, context, log_total, grad)


def by_head_forward(mixed_rows, cos_table, sin_table, scaling):
    seq_count, row_count, _, head_count, head_size = mixed_rows.shape
    ctx_count, fsdp_count = lax.axis_size("ctx"), lax.axis_size("fsdp")
    count = ctx_count * fsdp_count
    queries = rotate(mixed_rows[:, :, 0], cos_table, sin_table).astype(jnp.bfloat16) * scaling
    key_rows = rotate(mixed_rows[:, :, 1], cos_table, sin_table).astype(jnp.bfloat16)
    value_rows = mixed_rows[:, :, 2].astype(jnp.bfloat16)
    to_head = lambda rows: rows.transpose(0, 2, 1, 3).reshape(count, row_count, head_size)
    sent = jnp.concatenate(
        [
            jnp.concatenate([to_head(queries), to_head(key_rows)], axis=-1),
            pack(to_head(value_rows)),
        ],
        axis=1,
    )
    got = exchange(sent, ctx_count, fsdp_count, 1)
    flat = lambda rows: rows.reshape(count * row_count, head_size)
    queries = flat(got[:, :row_count, :head_size])
    key_rows = flat(got[:, :row_count, head_size:])
    value_rows = flat(unpack(got[:, row_count:]))
    context, log_total = attend(queries, key_rows, value_rows, 256)
    back = exchange(
        pack(context.astype(jnp.bfloat16).reshape(count, row_count, head_size)),
        ctx_count,
        fsdp_count,
        2,
    )
    context_low = (
        unpack(back)
        .reshape(seq_count, head_count, row_count, head_size)
        .transpose(0, 2, 1, 3)
        .reshape(seq_count * row_count, head_count * head_size)
    )
    return context_low, (queries, key_rows, value_rows, context, log_total)


def by_head_back(context_grad, saved, scaling, after):
    seq_count, row_count, head_count, head_size = context_grad.shape
    ctx_count, fsdp_count = lax.axis_size("ctx"), lax.axis_size("fsdp")
    count = ctx_count * fsdp_count
    queries, key_rows, value_rows, context, log_total = saved
    sent = pack(context_grad.transpose(0, 2, 1, 3).reshape(count, row_count, head_size))
    grad = unpack(exchange(sent, ctx_count, fsdp_count, 3)).reshape(count * row_count, head_size)
    query_grad, key_grad, value_grad = attend_back(
        queries, key_rows, value_rows, context, log_total, grad, 256
    )
    cos_all, sin_all = angles(jnp.arange(count * row_count, dtype=jnp.int32), head_size)
    cos_all, sin_all = cos_all[:, 0], sin_all[:, 0]
    query_pre = unrotate(query_grad * scaling, cos_all, sin_all).astype(jnp.bfloat16)
    key_pre = unrotate(key_grad, cos_all, sin_all).astype(jnp.bfloat16)
    split = lambda rows: rows.reshape(count, row_count, head_size)
    sent = jnp.concatenate(
        [
            jnp.concatenate([split(query_pre), split(key_pre)], axis=-1),
            pack(split(value_grad.astype(jnp.bfloat16))),
        ],
        axis=1,
    )
    if after:
        sent, after = lax.optimization_barrier((sent, after))
    got = exchange(sent, ctx_count, fsdp_count, 4)
    parts = jnp.stack(
        [got[:, :row_count, :head_size], got[:, :row_count, head_size:], unpack(got[:, row_count:])]
    )
    return (
        parts.reshape(3, seq_count, head_count, row_count, head_size)
        .transpose(1, 3, 0, 2, 4)
        .reshape(seq_count * row_count, 3 * head_count * head_size)
    ), after


def by_block_forward(mixed_rows, cos_table, sin_table, scaling):
    seq_count, row_count, _, head_count, head_size = mixed_rows.shape
    width = head_count * head_size
    queries = rotate(mixed_rows[:, :, 0], cos_table, sin_table).astype(jnp.bfloat16)
    key_flat = (
        rotate(mixed_rows[:, :, 1], cos_table, sin_table)
        .astype(jnp.bfloat16)
        .reshape(seq_count, row_count, width)
    )
    value_flat = mixed_rows[:, :, 2].astype(jnp.bfloat16).reshape(seq_count, row_count, width)
    key_block, value_block = (
        lax.all_gather(key_flat, "fsdp", axis=1, tiled=True),
        lax.all_gather(value_flat, "fsdp", axis=1, tiled=True),
    )
    start_state = empty_state(seq_count, head_count, row_count, head_size)
    running_max, denominator, weighted = forward_step(
        queries,
        scaling,
        start_state,
        (
            lax.all_gather(key_block, "ctx", axis=1, tiled=True),
            lax.all_gather(value_block, "ctx", axis=1, tiled=True),
        ),
    )
    context = (weighted / denominator[..., None]).transpose(0, 2, 1, 3)
    log_total = running_max + jnp.log(denominator)
    context_low = context.reshape(seq_count * row_count, width).astype(jnp.bfloat16)
    return context_low, (queries, key_block, value_block, context, log_total, cos_table, sin_table)


def by_block_back(context_grad, saved, scaling, after):
    seq_count, row_count, head_count, head_size = context_grad.shape
    width = head_count * head_size
    queries, key_block, value_block, context, log_total, cos_table, sin_table = saved
    inner = jnp.sum(context_grad.astype(jnp.float32) * context, axis=-1)
    inner_heads = inner.transpose(0, 2, 1)
    log_rows = log_total.transpose(0, 2, 1)
    query_grad = query_step(
        queries,
        context_grad,
        log_total,
        inner_heads,
        scaling,
        (
            lax.all_gather(key_block, "ctx", axis=1, tiled=True),
            lax.all_gather(value_block, "ctx", axis=1, tiled=True),
        ),
    )
    block_len = key_block.shape[1]
    query_wide = queries.reshape(seq_count, row_count, width).astype(jnp.float32)
    grad_wide = context_grad.reshape(seq_count, row_count, width).astype(jnp.float32)
    key_grad, value_grad = key_step(
        as_heads(key_block, head_size),
        as_heads(value_block, head_size),
        scaling,
        (
            lax.all_gather(query_wide, "ctx", axis=1, tiled=True),
            lax.all_gather(grad_wide, "ctx", axis=1, tiled=True),
            lax.all_gather(log_rows, "ctx", axis=1, tiled=True),
            lax.all_gather(inner, "ctx", axis=1, tiled=True),
        ),
    )
    own = lambda grad: lax.psum_scatter(
        grad.reshape(seq_count, block_len, width), "fsdp", scatter_dimension=1, tiled=True
    ).reshape(seq_count, row_count, head_count, head_size)
    query_pre = unrotate(query_grad * scaling, cos_table, sin_table)
    key_pre = unrotate(own(key_grad) * scaling, cos_table, sin_table)
    return (
        jnp.stack([query_pre, key_pre, own(value_grad)], axis=2)
        .reshape(seq_count * row_count, 3 * width)
        .astype(jnp.bfloat16)
    ), after


def group_rows(rows):
    return lax.all_gather(rows, "fsdp", axis=0, tiled=True)


def group_columns(arrays):
    count = lax.axis_size("fsdp")
    widths = [rows.shape[1] // count for rows in arrays]
    sent = jnp.stack(
        [
            jnp.concatenate(
                [rows[:, f * width : (f + 1) * width] for rows, width in zip(arrays, widths)],
                axis=1,
            )
            for f in range(count)
        ]
    )
    got = lax.all_to_all(sent, "fsdp", split_axis=0, concat_axis=0, tiled=True)
    got = got.reshape(-1, sum(widths))
    edges = [sum(widths[:i]) for i in range(len(widths) + 1)]
    return [got[:, edges[i] : edges[i + 1]] for i in range(len(widths))]


def weight_grad(left, right):
    return jnp.einsum("tw,tf->wf", left, right, preferred_element_type=jnp.float32)


AXES = ("ctx", "fsdp")


def routes(move):
    pairs = []
    for z in range(4):
        for y in range(2):
            for x in range(2):
                for core in range(2):
                    to = move(z, y, x, core)
                    if to is not None:
                        source = ((z * 2 + y) * 2 + x) * 2 + core
                        pairs.append((source, ((to[0] * 2 + to[1]) * 2 + to[2]) * 2 + to[3]))
    return pairs


TO_X = routes(lambda z, y, x, core: (z, y, 1 - x, core))
TO_Y = routes(lambda z, y, x, core: (z, 1 - y, x, core))
TO_CORE = routes(lambda z, y, x, core: (z, y, x, 1 - core))
INWARD = routes(lambda z, y, x, core: {0: (1, y, x, core), 3: (2, y, x, core)}.get(z))
MIDDLE = routes(lambda z, y, x, core: {1: (2, y, x, core), 2: (1, y, x, core)}.get(z))
OUTWARD = routes(lambda z, y, x, core: {1: (0, y, x, core), 2: (3, y, x, core)}.get(z))


def over(array, route):
    return lax.ppermute(array, AXES, route)


def half_of(array, index):
    width = array.shape[1] // 2
    return jnp.where(index == 0, array[:, :width], array[:, width:])


def plane_left(parts, x):
    own = jnp.concatenate([half_of(part, x) for part in parts], axis=1)
    away = jnp.concatenate([half_of(part, 1 - x) for part in parts], axis=1)
    over_x = over(away, TO_X)
    return jnp.concatenate([own, over_x, over(own, TO_Y), over(over_x, TO_Y)], axis=0)


def plane_right(part, y, width):
    first, last = part[:, :width], part[:, part.shape[1] - width :]
    own = jnp.where(y == 0, first, last)
    over_y = over(jnp.where(y == 0, last, first), TO_Y)
    return jnp.concatenate([own, over(own, TO_X), over_y, over(over_y, TO_X)], axis=0)


def core_sum(left, right, core):
    both = weight_grad(left, right).astype(jnp.bfloat16)
    both = both.reshape(2, both.shape[0] // 2, both.shape[1])
    away = jnp.where(core == 0, both[1], both[0])
    own = jnp.where(core == 0, both[0], both[1])
    return added(own, over(away, TO_CORE))


def added(one, other):
    total = (one.astype(jnp.float32) + other.astype(jnp.float32)).astype(jnp.bfloat16)
    return lax.optimization_barrier(total)


def line_sum(part, z):
    part = added(part, over(part, INWARD))
    total = added(part, over(part, MIDDLE))
    outer = over(total, OUTWARD)
    return lax.optimization_barrier(jnp.where((z == 0) | (z == 3), outer, total))


def ctx_sum(part, z, y, full, pieces):
    width = part.shape[1] // pieces
    sums = [line_sum(part[:, i * width : (i + 1) * width], z) for i in range(pieces)]
    swapped = [over(total, TO_Y) for total in sums]
    own, other = jnp.concatenate(sums, axis=1), jnp.concatenate(swapped, axis=1)
    low, high = jnp.where(y == 0, own, other), jnp.where(y == 0, other, own)
    skip = 2 * part.shape[1] - full
    return jnp.concatenate([low, high[:, skip:]], axis=1).astype(jnp.float32)


def on_device(inputs, attn_gain, attn_proj, attn_out, mlp_gain, mlp_in, mlp_out, cotangent):
    seq_count, row_count, model_width = inputs.shape
    head_size = HEAD_DIM
    head_count = HEADS
    scaling = head_size ** (-0.5)
    fsdp_count = lax.axis_size("fsdp")
    fsdp_place = lax.axis_index("fsdp")
    device_count = lax.axis_size("ctx") * fsdp_count
    one_head_each = device_count == seq_count * head_count
    start_row = (lax.axis_index("ctx") * fsdp_count + fsdp_place) * row_count
    cos_table, sin_table = angles(start_row + jnp.arange(row_count, dtype=jnp.int32), head_size)
    tokens = seq_count * row_count
    gain_width = own_rows = attn_gain.shape[0]
    gains = lax.all_gather(jnp.stack([attn_gain, mlp_gain]), "fsdp", axis=1, tiled=True).astype(
        jnp.float32
    )
    gain_one, gain_two = gains[0], gains[1]
    ctx_count = lax.axis_size("ctx")
    small = one_head_each and fsdp_count == 4 and ctx_count == 8
    proj_full, out_full, lift_full, down_full = (
        gather(attn_proj, True, 3, 6)
        if small
        else lax.all_gather(attn_proj, "fsdp", axis=0, tiled=True),
        lax.all_gather(attn_out, "fsdp", axis=0, tiled=True),
        lax.all_gather(mlp_in, "fsdp", axis=0, tiled=True),
        lax.all_gather(mlp_out, "fsdp", axis=0, tiled=True),
    )
    states = inputs.astype(jnp.float32)
    normed, norm_back_one = jax.vjp(layer_norm, states, gain_one)
    normed_low = normed.astype(jnp.bfloat16).reshape(tokens, model_width)
    mixed_rows = jnp.dot(normed_low, proj_full, preferred_element_type=jnp.float32).reshape(
        seq_count, row_count, 3, head_count, head_size
    )
    attention, attention_back = (
        (by_head_forward, by_head_back) if one_head_each else (by_block_forward, by_block_back)
    )
    context_low, saved = attention(mixed_rows, cos_table, sin_table, scaling)
    branch = jnp.dot(context_low, out_full, preferred_element_type=jnp.float32).reshape(
        seq_count, row_count, model_width
    )
    middle = states + branch
    normed_two, norm_back_two = jax.vjp(layer_norm, middle, gain_two)
    normed_two_low = normed_two.astype(jnp.bfloat16).reshape(tokens, model_width)
    lifted = jnp.dot(normed_two_low, lift_full, preferred_element_type=jnp.float32)
    gate_out, gated_back = jax.vjp(gated_unit, lifted)
    gate_low = gate_out.astype(jnp.bfloat16)
    outputs = (
        middle
        + jnp.dot(gate_low, down_full, preferred_element_type=jnp.float32).reshape(
            seq_count, row_count, model_width
        )
    ).astype(jnp.bfloat16)
    seed_rows = cotangent.reshape(tokens, model_width)
    gate_grad = jnp.einsum("td,fd->tf", seed_rows, down_full, preferred_element_type=jnp.float32)
    lifted_grad = gated_back(gate_grad)[0].astype(jnp.bfloat16)
    normed_two_grad = jnp.einsum(
        "tf,wf->tw", lifted_grad, lift_full, preferred_element_type=jnp.float32
    ).reshape(seq_count, row_count, model_width)
    middle_part, gain_two_grad = norm_back_two(normed_two_grad)
    middle_grad = cotangent.astype(jnp.float32) + middle_part
    middle_low = middle_grad.reshape(tokens, model_width).astype(jnp.bfloat16)
    context_grad = (
        jnp.einsum("tv,wv->tw", middle_low, out_full, preferred_element_type=jnp.float32)
        .astype(jnp.bfloat16)
        .reshape(seq_count, row_count, head_count, head_size)
    )
    norms = normed_two_low, context_low, normed_low
    if small:
        z, y = lax.axis_index("ctx") // 2, lax.axis_index("ctx") % 2
        x, core = fsdp_place // 2, fsdp_place % 2
        left = plane_left(norms, x)
        gate_left = plane_left((gate_low,), x)
        seed_right = plane_right(seed_rows, y, model_width // 2)
        lifted_width = lifted_grad.shape[1]
        lift_half = -(-lifted_width // 256) * 128
        lift_right = plane_right(lifted_grad, y, lift_half)
        middle_right = plane_right(middle_low, y, model_width // 2)
        each = left.shape[1] // 3
        down_part = core_sum(gate_left, seed_right, core)
        lift_part = core_sum(left[:, :each], lift_right, core)
        out_part = core_sum(left[:, each : 2 * each], middle_right, core)
        down_sum = ctx_sum(down_part, z, y, model_width, 1)
        lift_sum = ctx_sum(lift_part, z, y, lifted_width, 3)
        out_sum = ctx_sum(out_part, z, y, model_width, 1)
        mixed_grad, _ = attention_back(context_grad, saved, scaling, ())
        mixed_right = plane_right(mixed_grad, y, mixed_grad.shape[1] // 2)
        proj_part = core_sum(left[:, 2 * each :], mixed_right, core)
        proj_sum = ctx_sum(proj_part, z, y, mixed_grad.shape[1], 2)
    else:
        normed_two_part, gate_part, context_part, normed_part = group_columns(
            (normed_two_low, gate_low, context_low, normed_low)
        )
        seed_group = group_rows(seed_rows)
        joined = group_rows(jnp.concatenate([lifted_grad, middle_low], axis=1))
        lift_grad = weight_grad(normed_two_part, joined[:, : lifted_grad.shape[1]])
        out_grad = weight_grad(context_part, joined[:, lifted_grad.shape[1] :])
        down_grad = weight_grad(gate_part, seed_group)
        first_grads = tuple(grad.astype(jnp.bfloat16) for grad in (lift_grad, down_grad, out_grad))
        mixed_grad, first_grads = attention_back(context_grad, saved, scaling, first_grads)
        mixed_group = group_rows(mixed_grad)
        proj_grad = weight_grad(normed_part, mixed_group).astype(jnp.bfloat16)
        lift_sum, down_sum, out_sum, proj_sum = (
            total.astype(jnp.float32) for total in lax.psum((*first_grads, proj_grad), "ctx")
        )
    normed_grad = jnp.einsum(
        "tm,wm->tw", mixed_grad, proj_full, preferred_element_type=jnp.float32
    ).reshape(seq_count, row_count, model_width)
    state_part, gain_one_grad = norm_back_one(normed_grad)
    input_grad = middle_grad + state_part
    gain_grads = jnp.stack([gain_one_grad, gain_two_grad])
    gain_sums = lax.psum(gain_grads, ("ctx", "fsdp"))
    gain_own = lax.dynamic_slice_in_dim(gain_sums, fsdp_place * gain_width, gain_width, axis=1)
    return (
        outputs,
        input_grad,
        gain_own[0],
        proj_sum,
        out_sum,
        gain_own[1],
        lift_sum,
        down_sum,
    )


def solution(mesh):
    in_specs = (
        P(None, ("ctx", "fsdp"), None),
        P("fsdp"),
        P("fsdp", None),
        P("fsdp", None),
        P("fsdp"),
        P("fsdp", None),
        P("fsdp", None),
        P(None, ("ctx", "fsdp"), None),
    )
    out_specs = (
        P(None, ("ctx", "fsdp"), None),
        P(None, ("ctx", "fsdp"), None),
        P("fsdp"),
        P("fsdp", None),
        P("fsdp", None),
        P("fsdp"),
        P("fsdp", None),
        P("fsdp", None),
    )
    return jax.shard_map(
        on_device, mesh=mesh, in_specs=in_specs, out_specs=out_specs, check_vma=False
    )
```

```python
import functools

import jax
import jax.numpy as jnp
from jax import lax
from jax.experimental import pallas as pl
from jax.experimental.pallas import tpu as pltpu
from jax.sharding import PartitionSpec as P

HEADS = 16
HEAD_DIM = 64


eps = 1e-05
rope_base = 160000.0


def layer_norm(values, norm_gain):
    center = jnp.mean(values, axis=-1, keepdims=True)
    centred = values - center
    spread = jnp.mean(centred * centred, axis=-1, keepdims=True)
    return centred * lax.rsqrt(spread + eps) * norm_gain


def rotate(values, cos_table, sin_table):
    halfway = values.shape[-1] // 2
    turned = jnp.concatenate([-values[..., halfway:], values[..., :halfway]], axis=-1)
    return values * cos_table + turned * sin_table


def unrotate(gradient, cos_table, sin_table):
    halfway = gradient.shape[-1] // 2
    sined = gradient * sin_table
    return gradient * cos_table + jnp.concatenate(
        [sined[..., halfway:], -sined[..., :halfway]], axis=-1
    )


def angles(positions, head_size):
    exponent = jnp.arange(0, head_size, 2, dtype=jnp.float32) / head_size
    inverse = rope_base ** (-exponent)
    phases = positions.astype(jnp.float32)[:, None] * inverse[None, :]
    phases = jnp.concatenate([phases, phases], axis=-1)
    return (jnp.cos(phases)[:, None, :], jnp.sin(phases)[:, None, :])


def gated_unit(lifted):
    hidden_units = lifted.shape[-1] // 2
    return jax.nn.gelu(lifted[..., :hidden_units], approximate=False) * lifted[..., hidden_units:]


def as_heads(flat_rows, head_size):
    return flat_rows.reshape(flat_rows.shape[0], flat_rows.shape[1], -1, head_size)


def empty_state(seq_count, head_count, query_rows, head_size):
    return (
        jnp.full((seq_count, head_count, query_rows), -jnp.inf, jnp.float32),
        jnp.zeros((seq_count, head_count, query_rows), jnp.float32),
        jnp.zeros((seq_count, head_count, query_rows, head_size), jnp.float32),
    )


def forward_step(queries, scaling, state_now, shard_part):
    running_max, denominator, weighted = state_now
    key_part = as_heads(shard_part[0], queries.shape[3])
    value_part = as_heads(shard_part[1], queries.shape[3])
    scores = (
        jnp.einsum("sqhd,skhd->shqk", queries, key_part, preferred_element_type=jnp.float32)
        * scaling
    )
    new_max = jnp.max(scores, axis=-1)
    fading = jnp.exp(running_max - new_max)
    weights = jnp.exp(scores - new_max[..., None])
    denominator = denominator * fading + jnp.sum(weights, axis=-1)
    weighted = weighted * fading[..., None] + jnp.einsum(
        "shqk,skhd->shqd",
        weights.astype(jnp.bfloat16),
        value_part,
        preferred_element_type=jnp.float32,
    )
    return (new_max, denominator, weighted)


def query_step(queries, grad_out, log_total, inner_heads, scaling, shard_part):
    key_part = as_heads(shard_part[0], queries.shape[3])
    value_part = as_heads(shard_part[1], queries.shape[3])
    scores = (
        jnp.einsum("sqhd,skhd->shqk", queries, key_part, preferred_element_type=jnp.float32)
        * scaling
    )
    weights = jnp.exp(scores - log_total[..., None])
    weight_grad = jnp.einsum(
        "sqhd,skhd->shqk", grad_out, value_part, preferred_element_type=jnp.float32
    )
    score_grad = (weights * (weight_grad - inner_heads[..., None])).astype(jnp.bfloat16)
    return jnp.einsum("shqk,skhd->sqhd", score_grad, key_part, preferred_element_type=jnp.float32)


def key_step(key_heads, value_heads, scaling, shard_part):
    head_size = key_heads.shape[3]
    query_part = as_heads(shard_part[0].astype(jnp.bfloat16), head_size)
    grad_part = as_heads(shard_part[1].astype(jnp.bfloat16), head_size)
    log_part = shard_part[2].transpose(0, 2, 1)
    inner_part = shard_part[3].transpose(0, 2, 1)
    scores = (
        jnp.einsum("sqhd,skhd->shqk", query_part, key_heads, preferred_element_type=jnp.float32)
        * scaling
    )
    weights = jnp.exp(scores - log_part[..., None])
    value_grad = jnp.einsum(
        "shqk,sqhd->skhd",
        weights.astype(jnp.bfloat16),
        grad_part,
        preferred_element_type=jnp.float32,
    )
    weight_grad = jnp.einsum(
        "sqhd,skhd->shqk", grad_part, value_heads, preferred_element_type=jnp.float32
    )
    score_grad = (weights * (weight_grad - inner_part[..., None])).astype(jnp.bfloat16)
    key_grad = jnp.einsum(
        "shqk,sqhd->skhd", score_grad, query_part, preferred_element_type=jnp.float32
    )
    return (key_grad, value_grad)


MESH_ID = pl.DeviceIdType.MESH


def exchange_kernel(ctx_count, fsdp_count, x_ref, o_ref, send_sem, recv_sem, own_sem):
    count = ctx_count * fsdp_count
    me = lax.axis_index("ctx") * fsdp_count + lax.axis_index("fsdp")
    barrier = pltpu.get_barrier_semaphore()

    def target(step):
        place = lax.rem(me + step, count)
        return place, (place // fsdp_count, lax.rem(place, fsdp_count))

    def copy_to(step):
        place, device = target(step)
        return pltpu.make_async_remote_copy(
            src_ref=x_ref.at[place],
            dst_ref=o_ref.at[me],
            send_sem=send_sem.at[step],
            recv_sem=recv_sem.at[step],
            device_id=device,
            device_id_type=MESH_ID,
        )

    @pl.loop(1, count)
    def _(step):
        pl.semaphore_signal(barrier, inc=1, device_id=target(step)[1], device_id_type=MESH_ID)

    pl.semaphore_wait(barrier, count - 1)
    own = pltpu.make_async_copy(x_ref.at[me], o_ref.at[me], own_sem)
    own.start()

    @pl.loop(1, count)
    def _(step):
        copy_to(step).start()

    own.wait()

    @pl.loop(1, count)
    def _(step):
        copy_to(step).wait()


def exchange(blocks, ctx_count, fsdp_count, collective_id):
    count = ctx_count * fsdp_count
    return pl.pallas_call(
        functools.partial(exchange_kernel, ctx_count, fsdp_count),
        out_shape=jax.ShapeDtypeStruct(blocks.shape, blocks.dtype),
        in_specs=[pl.BlockSpec(memory_space=pl.ANY)],
        out_specs=pl.BlockSpec(memory_space=pl.ANY),
        scratch_shapes=[
            pltpu.SemaphoreType.DMA((count,)),
            pltpu.SemaphoreType.DMA((count,)),
            pltpu.SemaphoreType.DMA,
        ],
        compiler_params=pltpu.CompilerParams(collective_id=collective_id, has_side_effects=True),
    )(blocks)


def gather_kernel(spread, chunks, x_ref, o_ref, send_sem, recv_sem, own_sem):
    ctx, place = lax.axis_index("ctx"), lax.axis_index("fsdp")
    across = lax.rem(place + 2, 4)
    beside = place + 1 - 2 * lax.rem(place, 2)
    half = lax.rem(ctx, 2)
    other_ctx = ctx + 1 - 2 * half
    sibling, partner, neighbour = (ctx, beside), (ctx, across), (other_ctx, place)
    width = x_ref.shape[-1] // (2 * chunks if spread else chunks)
    mine = half * chunks if spread else 0
    theirs = (1 - half) * chunks

    def columns(index):
        return pl.ds(pl.multiple_of(index * width, 128), width)

    def send(src, dst, sem, device):
        return pltpu.make_async_remote_copy(
            src_ref=src,
            dst_ref=dst,
            send_sem=send_sem.at[sem],
            recv_sem=recv_sem.at[sem],
            device_id=device,
            device_id_type=MESH_ID,
        )

    def piece(index):
        return o_ref.at[across, :, columns(index)]

    barrier = pltpu.get_barrier_semaphore()
    partners = (sibling, partner, neighbour) if spread else (sibling, partner)
    for device in partners:
        pl.semaphore_signal(barrier, inc=1, device_id=device, device_id_type=MESH_ID)
    pl.semaphore_wait(barrier, len(partners))
    crossing = [
        send(
            x_ref.at[:, columns(mine + c)],
            o_ref.at[place, :, columns(mine + c)],
            c,
            partner,
        )
        for c in range(chunks)
    ]
    for copy in crossing:
        copy.start()
    started = list(crossing)
    whole = send(x_ref, o_ref.at[place], chunks, sibling)
    whole.start()
    own = pltpu.make_async_copy(x_ref, o_ref.at[place], own_sem)
    own.start()
    turned = []
    for c in range(chunks):
        crossing[c].wait_recv()
        if spread:
            turn = send(piece(mine + c), piece(mine + c), chunks + 1 + c, neighbour)
            turn.start()
            turned.append(turn)
        hand = send(piece(mine + c), piece(mine + c), 2 * chunks + 1 + c, sibling)
        hand.start()
        started.append(hand)
    handed = started[chunks:]
    for c in range(len(turned)):
        turned[c].wait_recv()
        hand = send(piece(theirs + c), piece(theirs + c), 3 * chunks + 1 + c, sibling)
        hand.start()
        handed.append(hand)
    whole.wait_recv()
    own.wait()
    for hand in handed:
        hand.wait_recv()
    for copy in crossing + turned + handed + [whole]:
        copy.wait_send()


def gather(block, spread, chunks, collective_id):
    rows, width = block.shape
    count = 4 * chunks + 1
    return pl.pallas_call(
        functools.partial(gather_kernel, spread, chunks),
        out_shape=jax.ShapeDtypeStruct((4, rows, width), block.dtype),
        in_specs=[pl.BlockSpec(memory_space=pl.ANY)],
        out_specs=pl.BlockSpec(memory_space=pl.ANY),
        scratch_shapes=[
            pltpu.SemaphoreType.DMA((count,)),
            pltpu.SemaphoreType.DMA((count,)),
            pltpu.SemaphoreType.DMA,
        ],
        compiler_params=pltpu.CompilerParams(collective_id=collective_id, has_side_effects=True),
    )(block).reshape(4 * rows, width)


def pack(blocks):
    half = blocks.shape[-2] // 2
    return jnp.concatenate([blocks[..., :half, :], blocks[..., half:, :]], axis=-1)


def unpack(blocks):
    half = blocks.shape[-1] // 2
    return jnp.concatenate([blocks[..., :half], blocks[..., half:]], axis=-2)


CONTRACT_LAST = (((1,), (1,)), ((), ()))
CONTRACT_FIRST = (((0,), (0,)), ((), ()))


def attend_kernel(q_ref, k_ref, v_ref, context_ref, log_ref):
    scores = lax.dot_general(
        q_ref[...], k_ref[...], CONTRACT_LAST, preferred_element_type=jnp.float32
    )
    top = jnp.max(scores, axis=-1, keepdims=True)
    weights = jnp.exp(scores - top)
    total = jnp.sum(weights, axis=-1, keepdims=True)
    weighted = jnp.dot(
        weights.astype(jnp.bfloat16), v_ref[...], preferred_element_type=jnp.float32
    )
    context_ref[...] = weighted / total
    log_ref[...] = top + jnp.log(total)


def attend(queries, key_rows, value_rows, block):
    rows, size = queries.shape
    return pl.pallas_call(
        attend_kernel,
        grid=(rows // block,),
        out_shape=(
            jax.ShapeDtypeStruct((rows, size), jnp.float32),
            jax.ShapeDtypeStruct((rows, 1), jnp.float32),
        ),
        in_specs=[
            pl.BlockSpec((block, size), lambda i: (i, 0)),
            pl.BlockSpec((rows, size), lambda i: (0, 0)),
            pl.BlockSpec((rows, size), lambda i: (0, 0)),
        ],
        out_specs=(
            pl.BlockSpec((block, size), lambda i: (i, 0)),
            pl.BlockSpec((block, 1), lambda i: (i, 0)),
        ),
        compiler_params=pltpu.CompilerParams(vmem_limit_bytes=48 * 1024 * 1024),
    )(queries, key_rows, value_rows)


def attend_back_kernel(
    q_ref, k_ref, v_ref, context_ref, log_ref, grad_ref, dq_ref, dk_ref, dv_ref
):
    @pl.when(pl.program_id(0) == 0)
    def _():
        dk_ref[...] = jnp.zeros_like(dk_ref)
        dv_ref[...] = jnp.zeros_like(dv_ref)

    grad = grad_ref[...]
    inner = jnp.sum(grad.astype(jnp.float32) * context_ref[...], axis=-1, keepdims=True)
    scores = lax.dot_general(
        q_ref[...], k_ref[...], CONTRACT_LAST, preferred_element_type=jnp.float32
    )
    probs = jnp.exp(scores - log_ref[...])
    prob_grad = lax.dot_general(
        grad, v_ref[...], CONTRACT_LAST, preferred_element_type=jnp.float32
    )
    score_grad = (probs * (prob_grad - inner)).astype(jnp.bfloat16)
    dv_ref[...] += lax.dot_general(
        probs.astype(jnp.bfloat16), grad, CONTRACT_FIRST, preferred_element_type=jnp.float32
    )
    dk_ref[...] += lax.dot_general(
        score_grad, q_ref[...], CONTRACT_FIRST, preferred_element_type=jnp.float32
    )
    dq_ref[...] = jnp.dot(score_grad, k_ref[...], preferred_element_type=jnp.float32)


def attend_back(queries, key_rows, value_rows, context, log_total, grad, block):
    rows, size = queries.shape
    part = pl.BlockSpec((block, size), lambda i: (i, 0))
    whole = pl.BlockSpec((rows, size), lambda i: (0, 0))
    return pl.pallas_call(
        attend_back_kernel,
        grid=(rows // block,),
        out_shape=(jax.ShapeDtypeStruct((rows, size), jnp.float32),) * 3,
        in_specs=[
            part,
            whole,
            whole,
            part,
            pl.BlockSpec((block, 1), lambda i: (i, 0)),
            part,
        ],
        out_specs=(part, whole, whole),
        compiler_params=pltpu.CompilerParams(vmem_limit_bytes=48 * 1024 * 1024),
    )(queries, key_rows, value_rows, context, log_total, grad)


def by_head_forward(mixed_rows, cos_table, sin_table, scaling):
    seq_count, row_count, _, head_count, head_size = mixed_rows.shape
    ctx_count, fsdp_count = lax.axis_size("ctx"), lax.axis_size("fsdp")
    count = ctx_count * fsdp_count
    queries = rotate(mixed_rows[:, :, 0], cos_table, sin_table).astype(jnp.bfloat16) * scaling
    key_rows = rotate(mixed_rows[:, :, 1], cos_table, sin_table).astype(jnp.bfloat16)
    value_rows = mixed_rows[:, :, 2].astype(jnp.bfloat16)
    to_head = lambda rows: rows.transpose(0, 2, 1, 3).reshape(count, row_count, head_size)
    sent = jnp.concatenate(
        [
            jnp.concatenate([to_head(queries), to_head(key_rows)], axis=-1),
            pack(to_head(value_rows)),
        ],
        axis=1,
    )
    got = exchange(sent, ctx_count, fsdp_count, 1)
    flat = lambda rows: rows.reshape(count * row_count, head_size)
    queries = flat(got[:, :row_count, :head_size])
    key_rows = flat(got[:, :row_count, head_size:])
    value_rows = flat(unpack(got[:, row_count:]))
    context, log_total = attend(queries, key_rows, value_rows, 256)
    back = exchange(
        pack(context.astype(jnp.bfloat16).reshape(count, row_count, head_size)),
        ctx_count,
        fsdp_count,
        2,
    )
    context_low = (
        unpack(back)
        .reshape(seq_count, head_count, row_count, head_size)
        .transpose(0, 2, 1, 3)
        .reshape(seq_count * row_count, head_count * head_size)
    )
    return context_low, (queries, key_rows, value_rows, context, log_total)


def by_head_back(context_grad, saved, scaling, after):
    seq_count, row_count, head_count, head_size = context_grad.shape
    ctx_count, fsdp_count = lax.axis_size("ctx"), lax.axis_size("fsdp")
    count = ctx_count * fsdp_count
    queries, key_rows, value_rows, context, log_total = saved
    sent = pack(context_grad.transpose(0, 2, 1, 3).reshape(count, row_count, head_size))
    grad = unpack(exchange(sent, ctx_count, fsdp_count, 3)).reshape(count * row_count, head_size)
    query_grad, key_grad, value_grad = attend_back(
        queries, key_rows, value_rows, context, log_total, grad, 256
    )
    cos_all, sin_all = angles(jnp.arange(count * row_count, dtype=jnp.int32), head_size)
    cos_all, sin_all = cos_all[:, 0], sin_all[:, 0]
    query_pre = unrotate(query_grad * scaling, cos_all, sin_all).astype(jnp.bfloat16)
    key_pre = unrotate(key_grad, cos_all, sin_all).astype(jnp.bfloat16)
    split = lambda rows: rows.reshape(count, row_count, head_size)
    sent = jnp.concatenate(
        [
            jnp.concatenate([split(query_pre), split(key_pre)], axis=-1),
            pack(split(value_grad.astype(jnp.bfloat16))),
        ],
        axis=1,
    )
    if after:
        sent, after = lax.optimization_barrier((sent, after))
    got = exchange(sent, ctx_count, fsdp_count, 4)
    parts = jnp.stack(
        [got[:, :row_count, :head_size], got[:, :row_count, head_size:], unpack(got[:, row_count:])]
    )
    return (
        parts.reshape(3, seq_count, head_count, row_count, head_size)
        .transpose(1, 3, 0, 2, 4)
        .reshape(seq_count * row_count, 3 * head_count * head_size)
    ), after


def by_block_forward(mixed_rows, cos_table, sin_table, scaling):
    seq_count, row_count, _, head_count, head_size = mixed_rows.shape
    width = head_count * head_size
    queries = rotate(mixed_rows[:, :, 0], cos_table, sin_table).astype(jnp.bfloat16)
    key_flat = (
        rotate(mixed_rows[:, :, 1], cos_table, sin_table)
        .astype(jnp.bfloat16)
        .reshape(seq_count, row_count, width)
    )
    value_flat = mixed_rows[:, :, 2].astype(jnp.bfloat16).reshape(seq_count, row_count, width)
    key_block, value_block = (
        lax.all_gather(key_flat, "fsdp", axis=1, tiled=True),
        lax.all_gather(value_flat, "fsdp", axis=1, tiled=True),
    )
    start_state = empty_state(seq_count, head_count, row_count, head_size)
    running_max, denominator, weighted = forward_step(
        queries,
        scaling,
        start_state,
        (
            lax.all_gather(key_block, "ctx", axis=1, tiled=True),
            lax.all_gather(value_block, "ctx", axis=1, tiled=True),
        ),
    )
    context = (weighted / denominator[..., None]).transpose(0, 2, 1, 3)
    log_total = running_max + jnp.log(denominator)
    context_low = context.reshape(seq_count * row_count, width).astype(jnp.bfloat16)
    return context_low, (queries, key_block, value_block, context, log_total, cos_table, sin_table)


def by_block_back(context_grad, saved, scaling, after):
    seq_count, row_count, head_count, head_size = context_grad.shape
    width = head_count * head_size
    queries, key_block, value_block, context, log_total, cos_table, sin_table = saved
    inner = jnp.sum(context_grad.astype(jnp.float32) * context, axis=-1)
    inner_heads = inner.transpose(0, 2, 1)
    log_rows = log_total.transpose(0, 2, 1)
    query_grad = query_step(
        queries,
        context_grad,
        log_total,
        inner_heads,
        scaling,
        (
            lax.all_gather(key_block, "ctx", axis=1, tiled=True),
            lax.all_gather(value_block, "ctx", axis=1, tiled=True),
        ),
    )
    block_len = key_block.shape[1]
    query_wide = queries.reshape(seq_count, row_count, width).astype(jnp.float32)
    grad_wide = context_grad.reshape(seq_count, row_count, width).astype(jnp.float32)
    key_grad, value_grad = key_step(
        as_heads(key_block, head_size),
        as_heads(value_block, head_size),
        scaling,
        (
            lax.all_gather(query_wide, "ctx", axis=1, tiled=True),
            lax.all_gather(grad_wide, "ctx", axis=1, tiled=True),
            lax.all_gather(log_rows, "ctx", axis=1, tiled=True),
            lax.all_gather(inner, "ctx", axis=1, tiled=True),
        ),
    )
    own = lambda grad: lax.psum_scatter(
        grad.reshape(seq_count, block_len, width), "fsdp", scatter_dimension=1, tiled=True
    ).reshape(seq_count, row_count, head_count, head_size)
    query_pre = unrotate(query_grad * scaling, cos_table, sin_table)
    key_pre = unrotate(own(key_grad) * scaling, cos_table, sin_table)
    return (
        jnp.stack([query_pre, key_pre, own(value_grad)], axis=2)
        .reshape(seq_count * row_count, 3 * width)
        .astype(jnp.bfloat16)
    ), after


def group_rows(rows):
    return lax.all_gather(rows, "fsdp", axis=0, tiled=True)


def group_columns(arrays):
    count = lax.axis_size("fsdp")
    widths = [rows.shape[1] // count for rows in arrays]
    sent = jnp.stack(
        [
            jnp.concatenate(
                [rows[:, f * width : (f + 1) * width] for rows, width in zip(arrays, widths)],
                axis=1,
            )
            for f in range(count)
        ]
    )
    got = lax.all_to_all(sent, "fsdp", split_axis=0, concat_axis=0, tiled=True)
    got = got.reshape(-1, sum(widths))
    edges = [sum(widths[:i]) for i in range(len(widths) + 1)]
    return [got[:, edges[i] : edges[i + 1]] for i in range(len(widths))]


def weight_grad(left, right):
    return jnp.einsum("tw,tf->wf", left, right, preferred_element_type=jnp.float32)


def mesh_place():
    ctx, place = lax.axis_index("ctx"), lax.axis_index("fsdp")
    return ctx // 2, lax.rem(ctx, 2), place // 2, lax.rem(place, 2)


def device_at(z, y, x, core):
    return (2 * z + y, 2 * x + core)


def greet(barrier, devices):
    for device in devices:
        pl.semaphore_signal(barrier, inc=1, device_id=device, device_id_type=MESH_ID)
    pl.semaphore_wait(barrier, len(devices))


def spans(total, count):
    edges = [total * i // (count * 16) * 16 for i in range(count)] + [total]
    return list(zip(edges[:-1], edges[1:]))


def plane_kernel(kinds, cuts, *refs):
    count = len(kinds)
    ins, outs = refs[:count], refs[count : 2 * count]
    send_sem, recv_sem, own_sem = refs[2 * count :]
    z, y, x, core = mesh_place()
    to_x, to_y = device_at(z, y, 1 - x, core), device_at(z, 1 - y, x, core)
    greet(pltpu.get_barrier_semaphore(), (to_x, to_y))
    serial = iter(range(send_sem.shape[0]))

    def send(src, dst, device):
        sem = next(serial)
        copy = pltpu.make_async_remote_copy(
            src_ref=src,
            dst_ref=dst,
            send_sem=send_sem.at[sem],
            recv_sem=recv_sem.at[sem],
            device_id=device,
            device_id_type=MESH_ID,
        )
        copy.start()
        return copy

    def block(ref, out, index):
        width = out.shape[2]
        if len(ref.shape) == 3:
            return ref.at[index]
        step = ref.shape[1] - width
        return ref.at[:, pl.ds(pl.multiple_of(index * step, 128), width)]

    owns = []
    for i in range(count):
        own = block(ins[i], outs[i], y if kinds[i] else x)
        copy = pltpu.make_async_copy(own, outs[i].at[0], own_sem.at[i])
        copy.start()
        owns.append(copy)
    firsts, seconds = [], []
    for i in range(count):
        own = block(ins[i], outs[i], y if kinds[i] else x)
        away = block(ins[i], outs[i], 1 - y if kinds[i] else 1 - x)
        for low, high in spans(outs[i].shape[1], cuts[i]):
            rows = pl.ds(low, high - low)
            by_x = send((own if kinds[i] else away).at[rows], outs[i].at[1, rows], to_x)
            by_y = send((away if kinds[i] else own).at[rows], outs[i].at[2, rows], to_y)
            firsts.append((i, rows, by_x, by_y))
    for i, rows, by_x, by_y in firsts:
        if kinds[i]:
            by_y.wait_recv()
            seconds.append(send(outs[i].at[2, rows], outs[i].at[3, rows], to_x))
        else:
            by_x.wait_recv()
            seconds.append(send(outs[i].at[1, rows], outs[i].at[3, rows], to_y))
    for i, rows, by_x, by_y in firsts:
        (by_x if kinds[i] else by_y).wait_recv()
        by_x.wait_send()
        by_y.wait_send()
    for copy in seconds:
        copy.wait()
    for copy in owns:
        copy.wait()


def plane(parts, kinds, widths, cuts, collective_id):
    rows = parts[0].shape[-2]
    sems = 3 * sum(cuts)
    outs = pl.pallas_call(
        functools.partial(plane_kernel, kinds, cuts),
        out_shape=[jax.ShapeDtypeStruct((4, rows, width), jnp.bfloat16) for width in widths],
        in_specs=[pl.BlockSpec(memory_space=pl.ANY)] * len(parts),
        out_specs=[pl.BlockSpec(memory_space=pl.ANY)] * len(parts),
        scratch_shapes=[
            pltpu.SemaphoreType.DMA((sems,)),
            pltpu.SemaphoreType.DMA((sems,)),
            pltpu.SemaphoreType.DMA((len(parts),)),
        ],
        compiler_params=pltpu.CompilerParams(collective_id=collective_id, has_side_effects=True),
    )(*parts)
    return [out.reshape(4 * rows, width) for out, width in zip(outs, widths)]


def finish_kernel(chunks, count, *refs):
    parts, gains = refs[:count], refs[count]
    outs, gain_got = refs[count + 1 : 2 * count + 1], refs[2 * count + 1]
    scratch = refs[2 * count + 2 :]
    core_got, z_got, mid_got, z_sent = (scratch[i * count : (i + 1) * count] for i in range(4))
    send_sem, recv_sem, gain_send, gain_recv, own_sem = scratch[4 * count :]
    z, y, x, core = mesh_place()
    me = lax.axis_index("ctx") * 4 + lax.axis_index("fsdp")
    total = len(chunks)
    barrier = pltpu.get_barrier_semaphore()

    def other(step):
        place = lax.rem(me + step, 32)
        return place, (place // 4, lax.rem(place, 4))

    @pl.loop(1, 32)
    def _(step):
        pl.semaphore_signal(barrier, inc=1, device_id=other(step)[1], device_id_type=MESH_ID)

    pl.semaphore_wait(barrier, 31)

    def send(stage, k, src, dst, device):
        return pltpu.make_async_remote_copy(
            src_ref=src,
            dst_ref=dst,
            send_sem=send_sem.at[stage * total + k],
            recv_sem=recv_sem.at[stage * total + k],
            device_id=device,
            device_id_type=MESH_ID,
        )

    def at(k):
        i, low, high = chunks[k]
        return i, pl.ds(low, high - low)

    def core_copy(k):
        i, rows = at(k)
        return send(
            0, k, parts[i].at[1 - core, rows], core_got[i].at[rows], device_at(z, y, x, 1 - core)
        )

    def inward(k):
        i, rows = at(k)
        return send(
            1, k, z_sent[i].at[rows], z_got[i].at[rows], device_at(1 + z // 2, y, x, core)
        )

    def middle(k):
        i, rows = at(k)
        return send(2, k, z_sent[i].at[rows], mid_got[i].at[rows], device_at(3 - z, y, x, core))

    def outward(k):
        i, rows = at(k)
        here = outs[i].at[y, rows]
        return send(3, k, here, here, device_at(3 * (z // 2), y, x, core))

    def across(k):
        i, rows = at(k)
        here = outs[i].at[y, rows]
        return send(4, k, here, here, device_at(z, 1 - y, x, core))

    def gain_copy(step):
        place, device = other(step)
        return pltpu.make_async_remote_copy(
            src_ref=gains.at[lax.rem(place, 4)],
            dst_ref=gain_got.at[me],
            send_sem=gain_send.at[step],
            recv_sem=gain_recv.at[step],
            device_id=device,
            device_id_type=MESH_ID,
        )

    def wide(value):
        return value.astype(jnp.float32)

    for k in range(total):
        core_copy(k).start()
    own = pltpu.make_async_copy(gains.at[lax.rem(me, 4)], gain_got.at[me], own_sem)
    own.start()

    @pl.loop(1, 32)
    def _(step):
        gain_copy(step).start()

    @pl.when((z == 0) | (z == 3))
    def _():
        for k in range(total):
            i, rows = at(k)
            core_copy(k).wait_recv()
            value = wide(parts[i][core, rows]) + wide(core_got[i][rows])
            z_sent[i][rows] = value.astype(jnp.bfloat16)
            inward(k).start()
        for k in range(total):
            outward(k).wait_recv()
            across(k).start()
        for k in range(total):
            inward(k).wait_send()

    @pl.when((z == 1) | (z == 2))
    def _():
        def meet(k):
            i, rows = at(k)
            middle(k).wait_recv()
            value = wide(z_sent[i][rows]) + wide(mid_got[i][rows])
            outs[i][y, rows] = value.astype(jnp.bfloat16)
            outward(k).start()
            across(k).start()

        for k in range(total):
            i, rows = at(k)
            core_copy(k).wait_recv()
            inward(k).wait_recv()
            value = wide(parts[i][core, rows]) + wide(core_got[i][rows]) + wide(z_got[i][rows])
            z_sent[i][rows] = value.astype(jnp.bfloat16)
            middle(k).start()
            if k > 0:
                meet(k - 1)
        meet(total - 1)
        for k in range(total):
            middle(k).wait_send()
            outward(k).wait_send()

    for k in range(total):
        i, rows = at(k)
        there = outs[i].at[1 - y, rows]
        send(4, k, there, there, device_at(z, 1 - y, x, core)).wait_recv()
        across(k).wait_send()
        core_copy(k).wait_send()
    own.wait()

    @pl.loop(1, 32)
    def _(step):
        gain_copy(step).wait()


def finish(parts, gains, cuts, collective_id):
    chunks = [
        (i, low, high) for i, cut in enumerate(cuts) for low, high in spans(parts[i].shape[1], cut)
    ]
    shapes = [part.shape for part in parts]
    buffers = [pltpu.VMEM(shape[1:], jnp.bfloat16) for shape in shapes]
    in_vmem = pl.BlockSpec(memory_space=pltpu.VMEM)
    return pl.pallas_call(
        functools.partial(finish_kernel, chunks, len(parts)),
        out_shape=[jax.ShapeDtypeStruct(shape, jnp.bfloat16) for shape in shapes]
        + [jax.ShapeDtypeStruct((32, 8, gains.shape[2]), jnp.float32)],
        in_specs=[in_vmem] * (len(parts) + 1),
        out_specs=[in_vmem] * (len(parts) + 1),
        scratch_shapes=buffers * 4
        + [
            pltpu.SemaphoreType.DMA((5 * len(chunks),)),
            pltpu.SemaphoreType.DMA((5 * len(chunks),)),
            pltpu.SemaphoreType.DMA((32,)),
            pltpu.SemaphoreType.DMA((32,)),
            pltpu.SemaphoreType.DMA,
        ],
        compiler_params=pltpu.CompilerParams(
            collective_id=collective_id,
            has_side_effects=True,
            vmem_limit_bytes=48 * 1024 * 1024,
        ),
    )(*parts, gains)


def core_blocks(left, right):
    both = weight_grad(left, right).astype(jnp.bfloat16)
    return both.reshape(2, both.shape[0] // 2, both.shape[1])


def joined_halves(out, full):
    skip = 2 * out.shape[2] - full
    return jnp.concatenate([out[0], out[1][:, skip:]], axis=1).astype(jnp.float32)


def on_device(inputs, attn_gain, attn_proj, attn_out, mlp_gain, mlp_in, mlp_out, cotangent):
    seq_count, row_count, model_width = inputs.shape
    head_size = HEAD_DIM
    head_count = HEADS
    scaling = head_size ** (-0.5)
    fsdp_count = lax.axis_size("fsdp")
    fsdp_place = lax.axis_index("fsdp")
    device_count = lax.axis_size("ctx") * fsdp_count
    one_head_each = device_count == seq_count * head_count
    start_row = (lax.axis_index("ctx") * fsdp_count + fsdp_place) * row_count
    cos_table, sin_table = angles(start_row + jnp.arange(row_count, dtype=jnp.int32), head_size)
    tokens = seq_count * row_count
    gain_width = own_rows = attn_gain.shape[0]
    gains = lax.all_gather(jnp.stack([attn_gain, mlp_gain]), "fsdp", axis=1, tiled=True).astype(
        jnp.float32
    )
    gain_one, gain_two = gains[0], gains[1]
    ctx_count = lax.axis_size("ctx")
    small = one_head_each and fsdp_count == 4 and ctx_count == 8
    proj_full, out_full, lift_full, down_full = (
        gather(attn_proj, True, 3, 6)
        if small
        else lax.all_gather(attn_proj, "fsdp", axis=0, tiled=True),
        lax.all_gather(attn_out, "fsdp", axis=0, tiled=True),
        lax.all_gather(mlp_in, "fsdp", axis=0, tiled=True),
        lax.all_gather(mlp_out, "fsdp", axis=0, tiled=True),
    )
    states = inputs.astype(jnp.float32)
    normed, norm_back_one = jax.vjp(layer_norm, states, gain_one)
    normed_low = normed.astype(jnp.bfloat16).reshape(tokens, model_width)
    mixed_rows = jnp.dot(normed_low, proj_full, preferred_element_type=jnp.float32).reshape(
        seq_count, row_count, 3, head_count, head_size
    )
    attention, attention_back = (
        (by_head_forward, by_head_back) if one_head_each else (by_block_forward, by_block_back)
    )
    context_low, saved = attention(mixed_rows, cos_table, sin_table, scaling)
    branch = jnp.dot(context_low, out_full, preferred_element_type=jnp.float32).reshape(
        seq_count, row_count, model_width
    )
    middle = states + branch
    normed_two, norm_back_two = jax.vjp(layer_norm, middle, gain_two)
    normed_two_low = normed_two.astype(jnp.bfloat16).reshape(tokens, model_width)
    lifted = jnp.dot(normed_two_low, lift_full, preferred_element_type=jnp.float32)
    gate_out, gated_back = jax.vjp(gated_unit, lifted)
    gate_low = gate_out.astype(jnp.bfloat16)
    outputs = (
        middle
        + jnp.dot(gate_low, down_full, preferred_element_type=jnp.float32).reshape(
            seq_count, row_count, model_width
        )
    ).astype(jnp.bfloat16)
    seed_rows = cotangent.reshape(tokens, model_width)
    gate_grad = jnp.einsum("td,fd->tf", seed_rows, down_full, preferred_element_type=jnp.float32)
    lifted_grad = gated_back(gate_grad)[0].astype(jnp.bfloat16)
    normed_two_grad = jnp.einsum(
        "tf,wf->tw", lifted_grad, lift_full, preferred_element_type=jnp.float32
    ).reshape(seq_count, row_count, model_width)
    middle_part, gain_two_grad = norm_back_two(normed_two_grad)
    middle_grad = cotangent.astype(jnp.float32) + middle_part
    middle_low = middle_grad.reshape(tokens, model_width).astype(jnp.bfloat16)
    context_grad = (
        jnp.einsum("tv,wv->tw", middle_low, out_full, preferred_element_type=jnp.float32)
        .astype(jnp.bfloat16)
        .reshape(seq_count, row_count, head_count, head_size)
    )
    if small:
        width, lifted_width = model_width // 2, lifted_grad.shape[1]
        hidden = gate_low.shape[1] // 2
        lift_half = -(-lifted_width // 256) * 128
        gate_halves = jnp.stack([gate_low[:, :hidden], gate_low[:, hidden:]])
        normed_two_left, context_left, normed_left, gate_left, seed_right, middle_right, lift_right = (
            plane(
                (normed_two_low, context_low, normed_low, gate_halves, seed_rows, middle_low, lifted_grad),
                (0, 0, 0, 0, 1, 1, 1),
                (width, width, width, hidden, width, width, lift_half),
                (1, 1, 1, 2, 1, 1, 4),
                5,
            )
        )
        mixed_grad, _ = attention_back(context_grad, saved, scaling, ())
        (mixed_right,) = plane((mixed_grad,), (1,), (mixed_grad.shape[1] // 2,), (4,), 7)
        lift_part = core_blocks(normed_two_left, lift_right)
        down_part = core_blocks(gate_left, seed_right)
        out_part = core_blocks(context_left, middle_right)
        proj_part = core_blocks(normed_left, mixed_right)
    else:
        normed_two_part, gate_part, context_part, normed_part = group_columns(
            (normed_two_low, gate_low, context_low, normed_low)
        )
        seed_group = group_rows(seed_rows)
        joined = group_rows(jnp.concatenate([lifted_grad, middle_low], axis=1))
        lift_grad = weight_grad(normed_two_part, joined[:, : lifted_grad.shape[1]])
        out_grad = weight_grad(context_part, joined[:, lifted_grad.shape[1] :])
        down_grad = weight_grad(gate_part, seed_group)
        first_grads = tuple(grad.astype(jnp.bfloat16) for grad in (lift_grad, down_grad, out_grad))
        mixed_grad, first_grads = attention_back(context_grad, saved, scaling, first_grads)
        mixed_group = group_rows(mixed_grad)
        proj_grad = weight_grad(normed_part, mixed_group).astype(jnp.bfloat16)
        lift_sum, down_sum, out_sum, proj_sum = (
            total.astype(jnp.float32) for total in lax.psum((*first_grads, proj_grad), "ctx")
        )
    normed_grad = jnp.einsum(
        "tm,wm->tw", mixed_grad, proj_full, preferred_element_type=jnp.float32
    ).reshape(seq_count, row_count, model_width)
    state_part, gain_one_grad = norm_back_one(normed_grad)
    input_grad = middle_grad + state_part
    gain_grads = jnp.stack([gain_one_grad, gain_two_grad])
    if small:
        shares = gain_grads.reshape(2, fsdp_count, gain_width).transpose(1, 0, 2)
        shares = jnp.concatenate([shares, jnp.zeros((fsdp_count, 6, gain_width))], axis=1)
        lift_sum, down_sum, out_sum, proj_sum, gain_got = finish(
            (lift_part, down_part, out_part, proj_part), shares, (8, 4, 2, 4), 8
        )
        lift_sum = joined_halves(lift_sum, lifted_width)
        down_sum = joined_halves(down_sum, model_width)
        out_sum = joined_halves(out_sum, model_width)
        proj_sum = joined_halves(proj_sum, mixed_grad.shape[1])
        gain_own = jnp.sum(gain_got, axis=0)
    else:
        gain_sums = lax.psum(gain_grads, ("ctx", "fsdp"))
        gain_own = lax.dynamic_slice_in_dim(gain_sums, fsdp_place * gain_width, gain_width, axis=1)
    return (
        outputs,
        input_grad,
        gain_own[0],
        proj_sum,
        out_sum,
        gain_own[1],
        lift_sum,
        down_sum,
    )


def solution(mesh):
    in_specs = (
        P(None, ("ctx", "fsdp"), None),
        P("fsdp"),
        P("fsdp", None),
        P("fsdp", None),
        P("fsdp"),
        P("fsdp", None),
        P("fsdp", None),
        P(None, ("ctx", "fsdp"), None),
    )
    out_specs = (
        P(None, ("ctx", "fsdp"), None),
        P(None, ("ctx", "fsdp"), None),
        P("fsdp"),
        P("fsdp", None),
        P("fsdp", None),
        P("fsdp"),
        P("fsdp", None),
        P("fsdp", None),
    )
    return jax.shard_map(
        on_device, mesh=mesh, in_specs=in_specs, out_specs=out_specs, check_vma=False
    )
```

```python
import functools

import jax
import jax.numpy as jnp
from jax import lax
from jax.experimental import pallas as pl
from jax.experimental.pallas import tpu as pltpu
from jax.sharding import PartitionSpec as P

HEADS = 16
HEAD_DIM = 64


eps = 1e-05
rope_base = 160000.0


def layer_norm(values, norm_gain):
    center = jnp.mean(values, axis=-1, keepdims=True)
    centred = values - center
    spread = jnp.mean(centred * centred, axis=-1, keepdims=True)
    return centred * lax.rsqrt(spread + eps) * norm_gain


def rotate(values, cos_table, sin_table):
    halfway = values.shape[-1] // 2
    turned = jnp.concatenate([-values[..., halfway:], values[..., :halfway]], axis=-1)
    return values * cos_table + turned * sin_table


def unrotate(gradient, cos_table, sin_table):
    halfway = gradient.shape[-1] // 2
    sined = gradient * sin_table
    return gradient * cos_table + jnp.concatenate(
        [sined[..., halfway:], -sined[..., :halfway]], axis=-1
    )


def angles(positions, head_size):
    exponent = jnp.arange(0, head_size, 2, dtype=jnp.float32) / head_size
    inverse = rope_base ** (-exponent)
    phases = positions.astype(jnp.float32)[:, None] * inverse[None, :]
    phases = jnp.concatenate([phases, phases], axis=-1)
    return (jnp.cos(phases)[:, None, :], jnp.sin(phases)[:, None, :])


def gated_unit(lifted):
    hidden_units = lifted.shape[-1] // 2
    return jax.nn.gelu(lifted[..., :hidden_units], approximate=False) * lifted[..., hidden_units:]


def as_heads(flat_rows, head_size):
    return flat_rows.reshape(flat_rows.shape[0], flat_rows.shape[1], -1, head_size)


def empty_state(seq_count, head_count, query_rows, head_size):
    return (
        jnp.full((seq_count, head_count, query_rows), -jnp.inf, jnp.float32),
        jnp.zeros((seq_count, head_count, query_rows), jnp.float32),
        jnp.zeros((seq_count, head_count, query_rows, head_size), jnp.float32),
    )


def forward_step(queries, scaling, state_now, shard_part):
    running_max, denominator, weighted = state_now
    key_part = as_heads(shard_part[0], queries.shape[3])
    value_part = as_heads(shard_part[1], queries.shape[3])
    scores = (
        jnp.einsum("sqhd,skhd->shqk", queries, key_part, preferred_element_type=jnp.float32)
        * scaling
    )
    new_max = jnp.max(scores, axis=-1)
    fading = jnp.exp(running_max - new_max)
    weights = jnp.exp(scores - new_max[..., None])
    denominator = denominator * fading + jnp.sum(weights, axis=-1)
    weighted = weighted * fading[..., None] + jnp.einsum(
        "shqk,skhd->shqd",
        weights.astype(jnp.bfloat16),
        value_part,
        preferred_element_type=jnp.float32,
    )
    return (new_max, denominator, weighted)


def query_step(queries, grad_out, log_total, inner_heads, scaling, shard_part):
    key_part = as_heads(shard_part[0], queries.shape[3])
    value_part = as_heads(shard_part[1], queries.shape[3])
    scores = (
        jnp.einsum("sqhd,skhd->shqk", queries, key_part, preferred_element_type=jnp.float32)
        * scaling
    )
    weights = jnp.exp(scores - log_total[..., None])
    weight_grad = jnp.einsum(
        "sqhd,skhd->shqk", grad_out, value_part, preferred_element_type=jnp.float32
    )
    score_grad = (weights * (weight_grad - inner_heads[..., None])).astype(jnp.bfloat16)
    return jnp.einsum("shqk,skhd->sqhd", score_grad, key_part, preferred_element_type=jnp.float32)


def key_step(key_heads, value_heads, scaling, shard_part):
    head_size = key_heads.shape[3]
    query_part = as_heads(shard_part[0].astype(jnp.bfloat16), head_size)
    grad_part = as_heads(shard_part[1].astype(jnp.bfloat16), head_size)
    log_part = shard_part[2].transpose(0, 2, 1)
    inner_part = shard_part[3].transpose(0, 2, 1)
    scores = (
        jnp.einsum("sqhd,skhd->shqk", query_part, key_heads, preferred_element_type=jnp.float32)
        * scaling
    )
    weights = jnp.exp(scores - log_part[..., None])
    value_grad = jnp.einsum(
        "shqk,sqhd->skhd",
        weights.astype(jnp.bfloat16),
        grad_part,
        preferred_element_type=jnp.float32,
    )
    weight_grad = jnp.einsum(
        "sqhd,skhd->shqk", grad_part, value_heads, preferred_element_type=jnp.float32
    )
    score_grad = (weights * (weight_grad - inner_part[..., None])).astype(jnp.bfloat16)
    key_grad = jnp.einsum(
        "shqk,sqhd->skhd", score_grad, query_part, preferred_element_type=jnp.float32
    )
    return (key_grad, value_grad)


MESH_ID = pl.DeviceIdType.MESH


def exchange_kernel(ctx_count, fsdp_count, x_ref, o_ref, send_sem, recv_sem, own_sem):
    count = ctx_count * fsdp_count
    me = lax.axis_index("ctx") * fsdp_count + lax.axis_index("fsdp")
    barrier = pltpu.get_barrier_semaphore()

    def target(step):
        place = lax.rem(me + step, count)
        return place, (place // fsdp_count, lax.rem(place, fsdp_count))

    def copy_to(step):
        place, device = target(step)
        return pltpu.make_async_remote_copy(
            src_ref=x_ref.at[place],
            dst_ref=o_ref.at[me],
            send_sem=send_sem.at[step],
            recv_sem=recv_sem.at[step],
            device_id=device,
            device_id_type=MESH_ID,
        )

    @pl.loop(1, count)
    def _(step):
        pl.semaphore_signal(barrier, inc=1, device_id=target(step)[1], device_id_type=MESH_ID)

    pl.semaphore_wait(barrier, count - 1)
    own = pltpu.make_async_copy(x_ref.at[me], o_ref.at[me], own_sem)
    own.start()

    @pl.loop(1, count)
    def _(step):
        copy_to(step).start()

    own.wait()

    @pl.loop(1, count)
    def _(step):
        copy_to(step).wait()


def exchange(blocks, ctx_count, fsdp_count, collective_id):
    count = ctx_count * fsdp_count
    return pl.pallas_call(
        functools.partial(exchange_kernel, ctx_count, fsdp_count),
        out_shape=jax.ShapeDtypeStruct(blocks.shape, blocks.dtype),
        in_specs=[pl.BlockSpec(memory_space=pl.ANY)],
        out_specs=pl.BlockSpec(memory_space=pl.ANY),
        scratch_shapes=[
            pltpu.SemaphoreType.DMA((count,)),
            pltpu.SemaphoreType.DMA((count,)),
            pltpu.SemaphoreType.DMA,
        ],
        compiler_params=pltpu.CompilerParams(collective_id=collective_id, has_side_effects=True),
    )(blocks)


def gather_kernel(spread, chunks, x_ref, o_ref, send_sem, recv_sem, own_sem):
    ctx, place = lax.axis_index("ctx"), lax.axis_index("fsdp")
    across = lax.rem(place + 2, 4)
    beside = place + 1 - 2 * lax.rem(place, 2)
    half = lax.rem(ctx, 2)
    other_ctx = ctx + 1 - 2 * half
    sibling, partner, neighbour = (ctx, beside), (ctx, across), (other_ctx, place)
    width = x_ref.shape[-1] // (2 * chunks if spread else chunks)
    mine = half * chunks if spread else 0
    theirs = (1 - half) * chunks

    def columns(index):
        return pl.ds(pl.multiple_of(index * width, 128), width)

    def send(src, dst, sem, device):
        return pltpu.make_async_remote_copy(
            src_ref=src,
            dst_ref=dst,
            send_sem=send_sem.at[sem],
            recv_sem=recv_sem.at[sem],
            device_id=device,
            device_id_type=MESH_ID,
        )

    def piece(index):
        return o_ref.at[across, :, columns(index)]

    barrier = pltpu.get_barrier_semaphore()
    partners = (sibling, partner, neighbour) if spread else (sibling, partner)
    for device in partners:
        pl.semaphore_signal(barrier, inc=1, device_id=device, device_id_type=MESH_ID)
    pl.semaphore_wait(barrier, len(partners))
    crossing = [
        send(
            x_ref.at[:, columns(mine + c)],
            o_ref.at[place, :, columns(mine + c)],
            c,
            partner,
        )
        for c in range(chunks)
    ]
    for copy in crossing:
        copy.start()
    started = list(crossing)
    whole = send(x_ref, o_ref.at[place], chunks, sibling)
    whole.start()
    own = pltpu.make_async_copy(x_ref, o_ref.at[place], own_sem)
    own.start()
    turned = []
    for c in range(chunks):
        crossing[c].wait_recv()
        if spread:
            turn = send(piece(mine + c), piece(mine + c), chunks + 1 + c, neighbour)
            turn.start()
            turned.append(turn)
        hand = send(piece(mine + c), piece(mine + c), 2 * chunks + 1 + c, sibling)
        hand.start()
        started.append(hand)
    handed = started[chunks:]
    for c in range(len(turned)):
        turned[c].wait_recv()
        hand = send(piece(theirs + c), piece(theirs + c), 3 * chunks + 1 + c, sibling)
        hand.start()
        handed.append(hand)
    whole.wait_recv()
    own.wait()
    for hand in handed:
        hand.wait_recv()
    for copy in crossing + turned + handed + [whole]:
        copy.wait_send()


def gather(block, spread, chunks, collective_id):
    rows, width = block.shape
    count = 4 * chunks + 1
    return pl.pallas_call(
        functools.partial(gather_kernel, spread, chunks),
        out_shape=jax.ShapeDtypeStruct((4, rows, width), block.dtype),
        in_specs=[pl.BlockSpec(memory_space=pl.ANY)],
        out_specs=pl.BlockSpec(memory_space=pl.ANY),
        scratch_shapes=[
            pltpu.SemaphoreType.DMA((count,)),
            pltpu.SemaphoreType.DMA((count,)),
            pltpu.SemaphoreType.DMA,
        ],
        compiler_params=pltpu.CompilerParams(collective_id=collective_id, has_side_effects=True),
    )(block).reshape(4 * rows, width)


def pack(blocks):
    half = blocks.shape[-2] // 2
    return jnp.concatenate([blocks[..., :half, :], blocks[..., half:, :]], axis=-1)


def unpack(blocks):
    half = blocks.shape[-1] // 2
    return jnp.concatenate([blocks[..., :half], blocks[..., half:]], axis=-2)


CUTS = ((False, 1), (True, 4), (False, 2))
CONTRACT_LAST = (((1,), (1,)), ((), ()))
CONTRACT_FIRST = (((0,), (0,)), ((), ()))


def attend_kernel(q_ref, k_ref, v_ref, context_ref, log_ref):
    scores = lax.dot_general(
        q_ref[...], k_ref[...], CONTRACT_LAST, preferred_element_type=jnp.float32
    )
    top = jnp.max(scores, axis=-1, keepdims=True)
    weights = jnp.exp(scores - top)
    total = jnp.sum(weights, axis=-1, keepdims=True)
    weighted = jnp.dot(
        weights.astype(jnp.bfloat16), v_ref[...], preferred_element_type=jnp.float32
    )
    context_ref[...] = weighted / total
    log_ref[...] = top + jnp.log(total)


def attend(queries, key_rows, value_rows, block):
    rows, size = queries.shape
    return pl.pallas_call(
        attend_kernel,
        grid=(rows // block,),
        out_shape=(
            jax.ShapeDtypeStruct((rows, size), jnp.float32),
            jax.ShapeDtypeStruct((rows, 1), jnp.float32),
        ),
        in_specs=[
            pl.BlockSpec((block, size), lambda i: (i, 0)),
            pl.BlockSpec((rows, size), lambda i: (0, 0)),
            pl.BlockSpec((rows, size), lambda i: (0, 0)),
        ],
        out_specs=(
            pl.BlockSpec((block, size), lambda i: (i, 0)),
            pl.BlockSpec((block, 1), lambda i: (i, 0)),
        ),
        compiler_params=pltpu.CompilerParams(vmem_limit_bytes=48 * 1024 * 1024),
    )(queries, key_rows, value_rows)


def attend_back_kernel(
    q_ref, k_ref, v_ref, context_ref, log_ref, grad_ref, dq_ref, dk_ref, dv_ref
):
    @pl.when(pl.program_id(0) == 0)
    def _():
        dk_ref[...] = jnp.zeros_like(dk_ref)
        dv_ref[...] = jnp.zeros_like(dv_ref)

    grad = grad_ref[...]
    inner = jnp.sum(grad.astype(jnp.float32) * context_ref[...], axis=-1, keepdims=True)
    scores = lax.dot_general(
        q_ref[...], k_ref[...], CONTRACT_LAST, preferred_element_type=jnp.float32
    )
    probs = jnp.exp(scores - log_ref[...])
    prob_grad = lax.dot_general(
        grad, v_ref[...], CONTRACT_LAST, preferred_element_type=jnp.float32
    )
    score_grad = (probs * (prob_grad - inner)).astype(jnp.bfloat16)
    dv_ref[...] += lax.dot_general(
        probs.astype(jnp.bfloat16), grad, CONTRACT_FIRST, preferred_element_type=jnp.float32
    )
    dk_ref[...] += lax.dot_general(
        score_grad, q_ref[...], CONTRACT_FIRST, preferred_element_type=jnp.float32
    )
    dq_ref[...] = jnp.dot(score_grad, k_ref[...], preferred_element_type=jnp.float32)


def attend_back(queries, key_rows, value_rows, context, log_total, grad, block):
    rows, size = queries.shape
    part = pl.BlockSpec((block, size), lambda i: (i, 0))
    whole = pl.BlockSpec((rows, size), lambda i: (0, 0))
    return pl.pallas_call(
        attend_back_kernel,
        grid=(rows // block,),
        out_shape=(jax.ShapeDtypeStruct((rows, size), jnp.float32),) * 3,
        in_specs=[
            part,
            whole,
            whole,
            part,
            pl.BlockSpec((block, 1), lambda i: (i, 0)),
            part,
        ],
        out_specs=(part, whole, whole),
        compiler_params=pltpu.CompilerParams(vmem_limit_bytes=48 * 1024 * 1024),
    )(queries, key_rows, value_rows, context, log_total, grad)


def whole_mesh(me):
    def other(step):
        place = lax.rem(me + step, 32)
        return place, (place // 4, lax.rem(place, 4))

    return other


def greet_all(other):
    barrier = pltpu.get_barrier_semaphore()

    @pl.loop(1, 32)
    def _(step):
        pl.semaphore_signal(barrier, inc=1, device_id=other(step)[1], device_id_type=MESH_ID)

    pl.semaphore_wait(barrier, 31)


def swap_lanes(value):
    return pltpu.roll(value.astype(jnp.float32), 64, 1)


def low_lanes(value):
    return lax.broadcasted_iota(jnp.int32, value.shape, 1) < 64


def weight_piece(ref, by_rows, half, index, count):
    if by_rows:
        size = ref.shape[0] // (2 * count)
        start = pl.multiple_of((half * count + index) * size, 16)
        return ref.at[pl.ds(start, size), :]
    size = ref.shape[1] // (2 * count)
    start = pl.multiple_of((half * count + index) * size, 128)
    return ref.at[:, pl.ds(start, size)]


def forward_kernel(cuts, *refs):
    count = len(cuts)
    sent, shards = refs[0], refs[1 : 1 + count]
    got, context, log_ref, back = refs[1 + count : 5 + count]
    fulls = refs[5 + count : 5 + 2 * count]
    (keys, values, packed, head_send, head_recv, back_send, back_recv, own_sem) = refs[
        5 + 2 * count : 13 + 2 * count
    ]
    w_send, w_recv = refs[13 + 2 * count :]
    z, y, x, core = mesh_place()
    place = 2 * x + core
    me = 4 * (2 * z + y) + place
    across = lax.rem(place + 2, 4)
    other = whole_mesh(me)
    sibling, partner = device_at(z, y, x, 1 - core), device_at(z, y, 1 - x, core)
    neighbour = device_at(z, 1 - y, x, core)
    greet_all(other)

    def head_copy(step):
        to, device = other(step)
        return pltpu.make_async_remote_copy(
            src_ref=sent.at[to],
            dst_ref=got.at[me],
            send_sem=head_send.at[step],
            recv_sem=head_recv.at[step],
            device_id=device,
            device_id_type=MESH_ID,
        )

    def back_copy(to):
        step = lax.rem(to - me + 32, 32)
        return pltpu.make_async_remote_copy(
            src_ref=packed.at[to],
            dst_ref=back.at[me],
            send_sem=back_send.at[step],
            recv_sem=back_recv.at[step],
            device_id=(to // 4, lax.rem(to, 4)),
            device_id_type=MESH_ID,
        )

    serial = iter(range(w_send.shape[0]))

    def send(src, dst, device):
        sem = next(serial)
        copy = pltpu.make_async_remote_copy(
            src_ref=src,
            dst_ref=dst,
            send_sem=w_send.at[sem],
            recv_sem=w_recv.at[sem],
            device_id=device,
            device_id_type=MESH_ID,
        )
        copy.start()
        return copy

    @pl.loop(1, 32)
    def _(step):
        head_copy(step).start()

    own = [pltpu.make_async_copy(sent.at[me], got.at[me], own_sem.at[count])]
    own[0].start()
    crossing, handed, turned = [], [], []
    for i, (by_rows, pieces) in enumerate(cuts):
        for c in range(pieces):
            src = weight_piece(shards[i], by_rows, y, c, pieces)
            dst = weight_piece(fulls[i].at[place], by_rows, y, c, pieces)
            crossing.append((i, c, send(src, dst, partner)))
    for i in range(count):
        copy = pltpu.make_async_copy(shards[i], fulls[i].at[place], own_sem.at[i])
        copy.start()
        own.append(copy)
        handed.append(send(shards[i], fulls[i].at[place], sibling))

    def turn(entry):
        i, c, copy = entry
        copy.wait_recv()
        here = weight_piece(fulls[i].at[across], cuts[i][0], y, c, cuts[i][1])
        turned.append((i, c, send(here, here, neighbour)))
        handed.append(send(here, here, sibling))

    def hand(entry):
        i, c, copy = entry
        copy.wait_recv()
        here = weight_piece(fulls[i].at[across], cuts[i][0], 1 - y, c, cuts[i][1])
        handed.append(send(here, here, sibling))

    turn(crossing[0])
    own[0].wait()

    @pl.loop(1, 32)
    def _(step):
        head_copy(step).wait()

    keys[0:1024] = got[:, 0:32, :].reshape(1024, 128)
    keys[1024:2048] = got[:, 32:64, :].reshape(1024, 128)
    values[...] = got[:, 64:96, :].reshape(1024, 128)

    def attend_block(b):
        block = lax.rem(b + me // 4, 8)
        low_rows = pl.ds(pl.multiple_of(block * 128, 128), 128)
        high_rows = pl.ds(pl.multiple_of(1024 + block * 128, 128), 128)
        queries = swap_lanes(jnp.concatenate([keys[low_rows], keys[high_rows]], axis=0))
        queries = jnp.where(low_lanes(queries), 0.0, queries).astype(jnp.bfloat16)
        scores = lax.dot_general(
            queries, keys[...], CONTRACT_LAST, preferred_element_type=jnp.float32
        )
        top = jnp.max(scores, axis=-1, keepdims=True)
        weights = jnp.exp(scores - top)
        total = jnp.sum(weights, axis=-1, keepdims=True)
        weights = weights.astype(jnp.bfloat16)
        first = jnp.dot(weights[:, :1024], values[...], preferred_element_type=jnp.float32)
        second = jnp.dot(weights[:, 1024:], values[...], preferred_element_type=jnp.float32)
        outcome = (first + pltpu.roll(second, 64, 1)) / total
        side = pltpu.roll(outcome[128:], 64, 1)
        outcome = jnp.where(low_lanes(side), outcome[:128], side)
        context[low_rows] = outcome
        log_total = top + jnp.log(total)
        log_ref[0, low_rows] = log_total[:128]
        log_ref[1, low_rows] = log_total[128:]
        packed[pl.ds(4 * block, 4)] = outcome.astype(jnp.bfloat16).reshape(4, 32, 128)

        @pl.loop(4 * block, 4 * block + 4)
        def _(to):
            @pl.when(to != me)
            def _():
                back_copy(to).start()

    @pl.loop(0, 8)
    def _(b):
        attend_block(b)

    mine = pltpu.make_async_copy(packed.at[me], back.at[me], own_sem.at[count + 1])
    mine.start()
    own.append(mine)
    for index in range(1, len(crossing)):
        turn(crossing[index])
        hand(turned[index - 1])
    hand(turned[-1])

    @pl.loop(1, 32)
    def _(step):
        back_copy(lax.rem(me + step, 32)).wait()

    for copy in handed:
        copy.wait()
    for _, _, copy in crossing + turned:
        copy.wait_send()
    for copy in own[1:]:
        copy.wait()


def forward_heads(sent, shards, cuts, collective_id):
    in_vmem, anywhere = pl.BlockSpec(memory_space=pltpu.VMEM), pl.BlockSpec(memory_space=pl.ANY)
    copies = len(shards) + sum(4 * pieces for _, pieces in cuts)
    low, full = jnp.bfloat16, jnp.float32
    sems = [pltpu.SemaphoreType.DMA((32,))] * 4
    return pl.pallas_call(
        functools.partial(forward_kernel, cuts),
        out_shape=[
            jax.ShapeDtypeStruct((32, 96, 128), low),
            jax.ShapeDtypeStruct((1024, 128), full),
            jax.ShapeDtypeStruct((2, 1024, 1), full),
            jax.ShapeDtypeStruct((32, 32, 128), low),
        ]
        + [jax.ShapeDtypeStruct((4, *shard.shape), low) for shard in shards],
        in_specs=[in_vmem] + [anywhere] * len(shards),
        out_specs=[in_vmem] * 4 + [anywhere] * len(shards),
        scratch_shapes=[
            pltpu.VMEM((2048, 128), low),
            pltpu.VMEM((1024, 128), low),
            pltpu.VMEM((32, 32, 128), low),
            *sems,
            pltpu.SemaphoreType.DMA((len(shards) + 2,)),
            pltpu.SemaphoreType.DMA((copies,)),
            pltpu.SemaphoreType.DMA((copies,)),
        ],
        compiler_params=pltpu.CompilerParams(
            collective_id=collective_id,
            has_side_effects=True,
            vmem_limit_bytes=48 * 1024 * 1024,
        ),
    )(sent, *shards)


def by_head_forward(mixed_rows, cos_table, sin_table, scaling, shards=()):
    seq_count, row_count, _, head_count, head_size = mixed_rows.shape
    ctx_count, fsdp_count = lax.axis_size("ctx"), lax.axis_size("fsdp")
    count = ctx_count * fsdp_count
    queries = rotate(mixed_rows[:, :, 0], cos_table, sin_table).astype(jnp.bfloat16) * scaling
    key_rows = rotate(mixed_rows[:, :, 1], cos_table, sin_table).astype(jnp.bfloat16)
    value_rows = mixed_rows[:, :, 2].astype(jnp.bfloat16)
    to_head = lambda rows: rows.transpose(0, 2, 1, 3).reshape(count, row_count, head_size)
    sent = jnp.concatenate(
        [
            jnp.concatenate([to_head(queries), to_head(key_rows)], axis=-1),
            pack(to_head(value_rows)),
        ],
        axis=1,
    )
    if shards:
        got, context, log_total, back, *fulls = forward_heads(sent, shards, CUTS, 1)
        context_low = (
            unpack(back)
            .reshape(seq_count, head_count, row_count, head_size)
            .transpose(0, 2, 1, 3)
            .reshape(seq_count * row_count, head_count * head_size)
        )
        flat = lambda rows: rows.reshape(count * row_count, head_size)
        queries = flat(got[:, :row_count, :head_size])
        key_rows = flat(got[:, :row_count, head_size:])
        value_rows = flat(unpack(got[:, row_count:]))
        context = flat(unpack(context.reshape(32, 32, 128)))
        log_total = log_total.reshape(2, 32, 32).transpose(1, 0, 2).reshape(2048, 1)
        return context_low, (queries, key_rows, value_rows, context, log_total), fulls
    got = exchange(sent, ctx_count, fsdp_count, 1)
    flat = lambda rows: rows.reshape(count * row_count, head_size)
    queries = flat(got[:, :row_count, :head_size])
    key_rows = flat(got[:, :row_count, head_size:])
    value_rows = flat(unpack(got[:, row_count:]))
    context, log_total = attend(queries, key_rows, value_rows, 256)
    back = exchange(
        pack(context.astype(jnp.bfloat16).reshape(count, row_count, head_size)),
        ctx_count,
        fsdp_count,
        2,
    )
    context_low = (
        unpack(back)
        .reshape(seq_count, head_count, row_count, head_size)
        .transpose(0, 2, 1, 3)
        .reshape(seq_count * row_count, head_count * head_size)
    )
    return context_low, (queries, key_rows, value_rows, context, log_total), ()


def by_head_back(context_grad, saved, scaling, after):
    seq_count, row_count, head_count, head_size = context_grad.shape
    ctx_count, fsdp_count = lax.axis_size("ctx"), lax.axis_size("fsdp")
    count = ctx_count * fsdp_count
    queries, key_rows, value_rows, context, log_total = saved
    sent = pack(context_grad.transpose(0, 2, 1, 3).reshape(count, row_count, head_size))
    grad = unpack(exchange(sent, ctx_count, fsdp_count, 3)).reshape(count * row_count, head_size)
    query_grad, key_grad, value_grad = attend_back(
        queries, key_rows, value_rows, context, log_total, grad, 256
    )
    cos_all, sin_all = angles(jnp.arange(count * row_count, dtype=jnp.int32), head_size)
    cos_all, sin_all = cos_all[:, 0], sin_all[:, 0]
    query_pre = unrotate(query_grad * scaling, cos_all, sin_all).astype(jnp.bfloat16)
    key_pre = unrotate(key_grad, cos_all, sin_all).astype(jnp.bfloat16)
    split = lambda rows: rows.reshape(count, row_count, head_size)
    sent = jnp.concatenate(
        [
            jnp.concatenate([split(query_pre), split(key_pre)], axis=-1),
            pack(split(value_grad.astype(jnp.bfloat16))),
        ],
        axis=1,
    )
    if after:
        sent, after = lax.optimization_barrier((sent, after))
    got = exchange(sent, ctx_count, fsdp_count, 4)
    parts = jnp.stack(
        [got[:, :row_count, :head_size], got[:, :row_count, head_size:], unpack(got[:, row_count:])]
    )
    return (
        parts.reshape(3, seq_count, head_count, row_count, head_size)
        .transpose(1, 3, 0, 2, 4)
        .reshape(seq_count * row_count, 3 * head_count * head_size)
    ), after


def by_block_forward(mixed_rows, cos_table, sin_table, scaling, shards=()):
    seq_count, row_count, _, head_count, head_size = mixed_rows.shape
    width = head_count * head_size
    queries = rotate(mixed_rows[:, :, 0], cos_table, sin_table).astype(jnp.bfloat16)
    key_flat = (
        rotate(mixed_rows[:, :, 1], cos_table, sin_table)
        .astype(jnp.bfloat16)
        .reshape(seq_count, row_count, width)
    )
    value_flat = mixed_rows[:, :, 2].astype(jnp.bfloat16).reshape(seq_count, row_count, width)
    key_block, value_block = (
        lax.all_gather(key_flat, "fsdp", axis=1, tiled=True),
        lax.all_gather(value_flat, "fsdp", axis=1, tiled=True),
    )
    start_state = empty_state(seq_count, head_count, row_count, head_size)
    running_max, denominator, weighted = forward_step(
        queries,
        scaling,
        start_state,
        (
            lax.all_gather(key_block, "ctx", axis=1, tiled=True),
            lax.all_gather(value_block, "ctx", axis=1, tiled=True),
        ),
    )
    context = (weighted / denominator[..., None]).transpose(0, 2, 1, 3)
    log_total = running_max + jnp.log(denominator)
    context_low = context.reshape(seq_count * row_count, width).astype(jnp.bfloat16)
    saved = queries, key_block, value_block, context, log_total, cos_table, sin_table
    return context_low, saved, ()


def by_block_back(context_grad, saved, scaling, after):
    seq_count, row_count, head_count, head_size = context_grad.shape
    width = head_count * head_size
    queries, key_block, value_block, context, log_total, cos_table, sin_table = saved
    inner = jnp.sum(context_grad.astype(jnp.float32) * context, axis=-1)
    inner_heads = inner.transpose(0, 2, 1)
    log_rows = log_total.transpose(0, 2, 1)
    query_grad = query_step(
        queries,
        context_grad,
        log_total,
        inner_heads,
        scaling,
        (
            lax.all_gather(key_block, "ctx", axis=1, tiled=True),
            lax.all_gather(value_block, "ctx", axis=1, tiled=True),
        ),
    )
    block_len = key_block.shape[1]
    query_wide = queries.reshape(seq_count, row_count, width).astype(jnp.float32)
    grad_wide = context_grad.reshape(seq_count, row_count, width).astype(jnp.float32)
    key_grad, value_grad = key_step(
        as_heads(key_block, head_size),
        as_heads(value_block, head_size),
        scaling,
        (
            lax.all_gather(query_wide, "ctx", axis=1, tiled=True),
            lax.all_gather(grad_wide, "ctx", axis=1, tiled=True),
            lax.all_gather(log_rows, "ctx", axis=1, tiled=True),
            lax.all_gather(inner, "ctx", axis=1, tiled=True),
        ),
    )
    own = lambda grad: lax.psum_scatter(
        grad.reshape(seq_count, block_len, width), "fsdp", scatter_dimension=1, tiled=True
    ).reshape(seq_count, row_count, head_count, head_size)
    query_pre = unrotate(query_grad * scaling, cos_table, sin_table)
    key_pre = unrotate(own(key_grad) * scaling, cos_table, sin_table)
    return (
        jnp.stack([query_pre, key_pre, own(value_grad)], axis=2)
        .reshape(seq_count * row_count, 3 * width)
        .astype(jnp.bfloat16)
    ), after


def group_rows(rows):
    return lax.all_gather(rows, "fsdp", axis=0, tiled=True)


def group_columns(arrays):
    count = lax.axis_size("fsdp")
    widths = [rows.shape[1] // count for rows in arrays]
    sent = jnp.stack(
        [
            jnp.concatenate(
                [rows[:, f * width : (f + 1) * width] for rows, width in zip(arrays, widths)],
                axis=1,
            )
            for f in range(count)
        ]
    )
    got = lax.all_to_all(sent, "fsdp", split_axis=0, concat_axis=0, tiled=True)
    got = got.reshape(-1, sum(widths))
    edges = [sum(widths[:i]) for i in range(len(widths) + 1)]
    return [got[:, edges[i] : edges[i + 1]] for i in range(len(widths))]


def weight_grad(left, right):
    return jnp.einsum("tw,tf->wf", left, right, preferred_element_type=jnp.float32)


def mesh_place():
    ctx, place = lax.axis_index("ctx"), lax.axis_index("fsdp")
    return ctx // 2, lax.rem(ctx, 2), place // 2, lax.rem(place, 2)


def device_at(z, y, x, core):
    return (2 * z + y, 2 * x + core)


def greet(barrier, devices):
    for device in devices:
        pl.semaphore_signal(barrier, inc=1, device_id=device, device_id_type=MESH_ID)
    pl.semaphore_wait(barrier, len(devices))


def spans(total, count):
    edges = [total * i // (count * 16) * 16 for i in range(count)] + [total]
    return list(zip(edges[:-1], edges[1:]))


def plane_kernel(kinds, cuts, *refs):
    count = len(kinds)
    ins, outs = refs[:count], refs[count : 2 * count]
    send_sem, recv_sem, own_sem = refs[2 * count :]
    z, y, x, core = mesh_place()
    to_x, to_y = device_at(z, y, 1 - x, core), device_at(z, 1 - y, x, core)
    greet(pltpu.get_barrier_semaphore(), (to_x, to_y))
    serial = iter(range(send_sem.shape[0]))

    def send(src, dst, device):
        sem = next(serial)
        copy = pltpu.make_async_remote_copy(
            src_ref=src,
            dst_ref=dst,
            send_sem=send_sem.at[sem],
            recv_sem=recv_sem.at[sem],
            device_id=device,
            device_id_type=MESH_ID,
        )
        copy.start()
        return copy

    def block(ref, out, index):
        width = out.shape[2]
        if len(ref.shape) == 3:
            return ref.at[index]
        step = ref.shape[1] - width
        return ref.at[:, pl.ds(pl.multiple_of(index * step, 128), width)]

    owns = []
    for i in range(count):
        own = block(ins[i], outs[i], y if kinds[i] else x)
        copy = pltpu.make_async_copy(own, outs[i].at[0], own_sem.at[i])
        copy.start()
        owns.append(copy)
    firsts, seconds = [], []
    for i in range(count):
        own = block(ins[i], outs[i], y if kinds[i] else x)
        away = block(ins[i], outs[i], 1 - y if kinds[i] else 1 - x)
        for low, high in spans(outs[i].shape[1], cuts[i]):
            rows = pl.ds(low, high - low)
            by_x = send((own if kinds[i] else away).at[rows], outs[i].at[1, rows], to_x)
            by_y = send((away if kinds[i] else own).at[rows], outs[i].at[2, rows], to_y)
            firsts.append((i, rows, by_x, by_y))
    for i, rows, by_x, by_y in firsts:
        if kinds[i]:
            by_y.wait_recv()
            seconds.append(send(outs[i].at[2, rows], outs[i].at[3, rows], to_x))
        else:
            by_x.wait_recv()
            seconds.append(send(outs[i].at[1, rows], outs[i].at[3, rows], to_y))
    for i, rows, by_x, by_y in firsts:
        (by_x if kinds[i] else by_y).wait_recv()
        by_x.wait_send()
        by_y.wait_send()
    for copy in seconds:
        copy.wait()
    for copy in owns:
        copy.wait()


def plane(parts, kinds, widths, cuts, collective_id):
    rows = parts[0].shape[-2]
    sems = 3 * sum(cuts)
    outs = pl.pallas_call(
        functools.partial(plane_kernel, kinds, cuts),
        out_shape=[jax.ShapeDtypeStruct((4, rows, width), jnp.bfloat16) for width in widths],
        in_specs=[pl.BlockSpec(memory_space=pl.ANY)] * len(parts),
        out_specs=[pl.BlockSpec(memory_space=pl.ANY)] * len(parts),
        scratch_shapes=[
            pltpu.SemaphoreType.DMA((sems,)),
            pltpu.SemaphoreType.DMA((sems,)),
            pltpu.SemaphoreType.DMA((len(parts),)),
        ],
        compiler_params=pltpu.CompilerParams(collective_id=collective_id, has_side_effects=True),
    )(*parts)
    return [out.reshape(4 * rows, width) for out, width in zip(outs, widths)]


def finish_kernel(chunks, count, *refs):
    parts, gains = refs[:count], refs[count]
    outs, gain_got = refs[count + 1 : 2 * count + 1], refs[2 * count + 1]
    scratch = refs[2 * count + 2 :]
    core_got, z_got, mid_got, z_sent = (scratch[i * count : (i + 1) * count] for i in range(4))
    send_sem, recv_sem, gain_send, gain_recv, own_sem = scratch[4 * count :]
    z, y, x, core = mesh_place()
    me = lax.axis_index("ctx") * 4 + lax.axis_index("fsdp")
    total = len(chunks)
    barrier = pltpu.get_barrier_semaphore()

    def other(step):
        place = lax.rem(me + step, 32)
        return place, (place // 4, lax.rem(place, 4))

    @pl.loop(1, 32)
    def _(step):
        pl.semaphore_signal(barrier, inc=1, device_id=other(step)[1], device_id_type=MESH_ID)

    pl.semaphore_wait(barrier, 31)

    def send(stage, k, src, dst, device):
        return pltpu.make_async_remote_copy(
            src_ref=src,
            dst_ref=dst,
            send_sem=send_sem.at[stage * total + k],
            recv_sem=recv_sem.at[stage * total + k],
            device_id=device,
            device_id_type=MESH_ID,
        )

    def at(k):
        i, low, high = chunks[k]
        return i, pl.ds(low, high - low)

    def core_copy(k):
        i, rows = at(k)
        return send(
            0, k, parts[i].at[1 - core, rows], core_got[i].at[rows], device_at(z, y, x, 1 - core)
        )

    def inward(k):
        i, rows = at(k)
        return send(
            1, k, z_sent[i].at[rows], z_got[i].at[rows], device_at(1 + z // 2, y, x, core)
        )

    def middle(k):
        i, rows = at(k)
        return send(2, k, z_sent[i].at[rows], mid_got[i].at[rows], device_at(3 - z, y, x, core))

    def outward(k):
        i, rows = at(k)
        here = outs[i].at[y, rows]
        return send(3, k, here, here, device_at(3 * (z // 2), y, x, core))

    def across(k):
        i, rows = at(k)
        here = outs[i].at[y, rows]
        return send(4, k, here, here, device_at(z, 1 - y, x, core))

    def gain_copy(step):
        place, device = other(step)
        return pltpu.make_async_remote_copy(
            src_ref=gains.at[lax.rem(place, 4)],
            dst_ref=gain_got.at[me],
            send_sem=gain_send.at[step],
            recv_sem=gain_recv.at[step],
            device_id=device,
            device_id_type=MESH_ID,
        )

    def wide(value):
        return value.astype(jnp.float32)

    for k in range(total):
        core_copy(k).start()
    own = pltpu.make_async_copy(gains.at[lax.rem(me, 4)], gain_got.at[me], own_sem)
    own.start()

    @pl.loop(1, 32)
    def _(step):
        gain_copy(step).start()

    @pl.when((z == 0) | (z == 3))
    def _():
        for k in range(total):
            i, rows = at(k)
            core_copy(k).wait_recv()
            value = wide(parts[i][core, rows]) + wide(core_got[i][rows])
            z_sent[i][rows] = value.astype(jnp.bfloat16)
            inward(k).start()
        for k in range(total):
            outward(k).wait_recv()
            across(k).start()
        for k in range(total):
            inward(k).wait_send()

    @pl.when((z == 1) | (z == 2))
    def _():
        def meet(k):
            i, rows = at(k)
            middle(k).wait_recv()
            value = wide(z_sent[i][rows]) + wide(mid_got[i][rows])
            outs[i][y, rows] = value.astype(jnp.bfloat16)
            outward(k).start()
            across(k).start()

        for k in range(total):
            i, rows = at(k)
            core_copy(k).wait_recv()
            inward(k).wait_recv()
            value = wide(parts[i][core, rows]) + wide(core_got[i][rows]) + wide(z_got[i][rows])
            z_sent[i][rows] = value.astype(jnp.bfloat16)
            middle(k).start()
            if k > 0:
                meet(k - 1)
        meet(total - 1)
        for k in range(total):
            middle(k).wait_send()
            outward(k).wait_send()

    for k in range(total):
        i, rows = at(k)
        there = outs[i].at[1 - y, rows]
        send(4, k, there, there, device_at(z, 1 - y, x, core)).wait_recv()
        across(k).wait_send()
        core_copy(k).wait_send()
    own.wait()

    @pl.loop(1, 32)
    def _(step):
        gain_copy(step).wait()


def finish(parts, gains, cuts, collective_id):
    chunks = [
        (i, low, high) for i, cut in enumerate(cuts) for low, high in spans(parts[i].shape[1], cut)
    ]
    shapes = [part.shape for part in parts]
    buffers = [pltpu.VMEM(shape[1:], jnp.bfloat16) for shape in shapes]
    in_vmem = pl.BlockSpec(memory_space=pltpu.VMEM)
    return pl.pallas_call(
        functools.partial(finish_kernel, chunks, len(parts)),
        out_shape=[jax.ShapeDtypeStruct(shape, jnp.bfloat16) for shape in shapes]
        + [jax.ShapeDtypeStruct((32, 8, gains.shape[2]), jnp.float32)],
        in_specs=[in_vmem] * (len(parts) + 1),
        out_specs=[in_vmem] * (len(parts) + 1),
        scratch_shapes=buffers * 4
        + [
            pltpu.SemaphoreType.DMA((5 * len(chunks),)),
            pltpu.SemaphoreType.DMA((5 * len(chunks),)),
            pltpu.SemaphoreType.DMA((32,)),
            pltpu.SemaphoreType.DMA((32,)),
            pltpu.SemaphoreType.DMA,
        ],
        compiler_params=pltpu.CompilerParams(
            collective_id=collective_id,
            has_side_effects=True,
            vmem_limit_bytes=48 * 1024 * 1024,
        ),
    )(*parts, gains)


def core_blocks(left, right):
    both = weight_grad(left, right).astype(jnp.bfloat16)
    return both.reshape(2, both.shape[0] // 2, both.shape[1])


def joined_halves(out, full):
    skip = 2 * out.shape[2] - full
    return jnp.concatenate([out[0], out[1][:, skip:]], axis=1).astype(jnp.float32)


def on_device(inputs, attn_gain, attn_proj, attn_out, mlp_gain, mlp_in, mlp_out, cotangent):
    seq_count, row_count, model_width = inputs.shape
    head_size = HEAD_DIM
    head_count = HEADS
    scaling = head_size ** (-0.5)
    fsdp_count = lax.axis_size("fsdp")
    fsdp_place = lax.axis_index("fsdp")
    device_count = lax.axis_size("ctx") * fsdp_count
    one_head_each = device_count == seq_count * head_count
    start_row = (lax.axis_index("ctx") * fsdp_count + fsdp_place) * row_count
    cos_table, sin_table = angles(start_row + jnp.arange(row_count, dtype=jnp.int32), head_size)
    tokens = seq_count * row_count
    gain_width = own_rows = attn_gain.shape[0]
    gains = lax.all_gather(jnp.stack([attn_gain, mlp_gain]), "fsdp", axis=1, tiled=True).astype(
        jnp.float32
    )
    gain_one, gain_two = gains[0], gains[1]
    ctx_count = lax.axis_size("ctx")
    small = one_head_each and fsdp_count == 4 and ctx_count == 8
    if small:
        proj_full = gather(attn_proj, True, 3, 6)
        shards = attn_out, mlp_in, mlp_out
    else:
        shards = ()
        proj_full, out_full, lift_full, down_full = (
            lax.all_gather(rows, "fsdp", axis=0, tiled=True)
            for rows in (attn_proj, attn_out, mlp_in, mlp_out)
        )
    states = inputs.astype(jnp.float32)
    normed, norm_back_one = jax.vjp(layer_norm, states, gain_one)
    normed_low = normed.astype(jnp.bfloat16).reshape(tokens, model_width)
    mixed_rows = jnp.dot(normed_low, proj_full, preferred_element_type=jnp.float32).reshape(
        seq_count, row_count, 3, head_count, head_size
    )
    attention, attention_back = (
        (by_head_forward, by_head_back) if one_head_each else (by_block_forward, by_block_back)
    )
    context_low, saved, fulls = attention(mixed_rows, cos_table, sin_table, scaling, shards)
    if small:
        out_full, lift_full, down_full = (
            full.reshape(4 * full.shape[1], full.shape[2]) for full in fulls
        )
    branch = jnp.dot(context_low, out_full, preferred_element_type=jnp.float32).reshape(
        seq_count, row_count, model_width
    )
    middle = states + branch
    normed_two, norm_back_two = jax.vjp(layer_norm, middle, gain_two)
    normed_two_low = normed_two.astype(jnp.bfloat16).reshape(tokens, model_width)
    lifted = jnp.dot(normed_two_low, lift_full, preferred_element_type=jnp.float32)
    gate_out, gated_back = jax.vjp(gated_unit, lifted)
    gate_low = gate_out.astype(jnp.bfloat16)
    outputs = (
        middle
        + jnp.dot(gate_low, down_full, preferred_element_type=jnp.float32).reshape(
            seq_count, row_count, model_width
        )
    ).astype(jnp.bfloat16)
    seed_rows = cotangent.reshape(tokens, model_width)
    gate_grad = jnp.einsum("td,fd->tf", seed_rows, down_full, preferred_element_type=jnp.float32)
    lifted_grad = gated_back(gate_grad)[0].astype(jnp.bfloat16)
    normed_two_grad = jnp.einsum(
        "tf,wf->tw", lifted_grad, lift_full, preferred_element_type=jnp.float32
    ).reshape(seq_count, row_count, model_width)
    middle_part, gain_two_grad = norm_back_two(normed_two_grad)
    middle_grad = cotangent.astype(jnp.float32) + middle_part
    middle_low = middle_grad.reshape(tokens, model_width).astype(jnp.bfloat16)
    context_grad = (
        jnp.einsum("tv,wv->tw", middle_low, out_full, preferred_element_type=jnp.float32)
        .astype(jnp.bfloat16)
        .reshape(seq_count, row_count, head_count, head_size)
    )
    if small:
        width, lifted_width = model_width // 2, lifted_grad.shape[1]
        hidden = gate_low.shape[1] // 2
        lift_half = -(-lifted_width // 256) * 128
        gate_halves = jnp.stack([gate_low[:, :hidden], gate_low[:, hidden:]])
        normed_two_left, context_left, normed_left, gate_left, seed_right, middle_right, lift_right = (
            plane(
                (normed_two_low, context_low, normed_low, gate_halves, seed_rows, middle_low, lifted_grad),
                (0, 0, 0, 0, 1, 1, 1),
                (width, width, width, hidden, width, width, lift_half),
                (1, 1, 1, 2, 1, 1, 4),
                5,
            )
        )
        mixed_grad, _ = attention_back(context_grad, saved, scaling, ())
        (mixed_right,) = plane((mixed_grad,), (1,), (mixed_grad.shape[1] // 2,), (4,), 7)
        lift_part = core_blocks(normed_two_left, lift_right)
        down_part = core_blocks(gate_left, seed_right)
        out_part = core_blocks(context_left, middle_right)
        proj_part = core_blocks(normed_left, mixed_right)
    else:
        normed_two_part, gate_part, context_part, normed_part = group_columns(
            (normed_two_low, gate_low, context_low, normed_low)
        )
        seed_group = group_rows(seed_rows)
        joined = group_rows(jnp.concatenate([lifted_grad, middle_low], axis=1))
        lift_grad = weight_grad(normed_two_part, joined[:, : lifted_grad.shape[1]])
        out_grad = weight_grad(context_part, joined[:, lifted_grad.shape[1] :])
        down_grad = weight_grad(gate_part, seed_group)
        first_grads = tuple(grad.astype(jnp.bfloat16) for grad in (lift_grad, down_grad, out_grad))
        mixed_grad, first_grads = attention_back(context_grad, saved, scaling, first_grads)
        mixed_group = group_rows(mixed_grad)
        proj_grad = weight_grad(normed_part, mixed_group).astype(jnp.bfloat16)
        lift_sum, down_sum, out_sum, proj_sum = (
            total.astype(jnp.float32) for total in lax.psum((*first_grads, proj_grad), "ctx")
        )
    normed_grad = jnp.einsum(
        "tm,wm->tw", mixed_grad, proj_full, preferred_element_type=jnp.float32
    ).reshape(seq_count, row_count, model_width)
    state_part, gain_one_grad = norm_back_one(normed_grad)
    input_grad = middle_grad + state_part
    gain_grads = jnp.stack([gain_one_grad, gain_two_grad])
    if small:
        shares = gain_grads.reshape(2, fsdp_count, gain_width).transpose(1, 0, 2)
        shares = jnp.concatenate([shares, jnp.zeros((fsdp_count, 6, gain_width))], axis=1)
        lift_sum, down_sum, out_sum, proj_sum, gain_got = finish(
            (lift_part, down_part, out_part, proj_part), shares, (8, 4, 2, 4), 8
        )
        lift_sum = joined_halves(lift_sum, lifted_width)
        down_sum = joined_halves(down_sum, model_width)
        out_sum = joined_halves(out_sum, model_width)
        proj_sum = joined_halves(proj_sum, mixed_grad.shape[1])
        gain_own = jnp.sum(gain_got, axis=0)
    else:
        gain_sums = lax.psum(gain_grads, ("ctx", "fsdp"))
        gain_own = lax.dynamic_slice_in_dim(gain_sums, fsdp_place * gain_width, gain_width, axis=1)
    return (
        outputs,
        input_grad,
        gain_own[0],
        proj_sum,
        out_sum,
        gain_own[1],
        lift_sum,
        down_sum,
    )


def solution(mesh):
    in_specs = (
        P(None, ("ctx", "fsdp"), None),
        P("fsdp"),
        P("fsdp", None),
        P("fsdp", None),
        P("fsdp"),
        P("fsdp", None),
        P("fsdp", None),
        P(None, ("ctx", "fsdp"), None),
    )
    out_specs = (
        P(None, ("ctx", "fsdp"), None),
        P(None, ("ctx", "fsdp"), None),
        P("fsdp"),
        P("fsdp", None),
        P("fsdp", None),
        P("fsdp"),
        P("fsdp", None),
        P("fsdp", None),
    )
    return jax.shard_map(
        on_device, mesh=mesh, in_specs=in_specs, out_specs=out_specs, check_vma=False
    )
```

```python
import functools

import jax
import jax.numpy as jnp
from jax import lax
from jax.experimental import pallas as pl
from jax.experimental.pallas import tpu as pltpu
from jax.sharding import PartitionSpec as P

HEADS = 16
HEAD_DIM = 64


eps = 1e-05
rope_base = 160000.0


def layer_norm(values, norm_gain):
    center = jnp.mean(values, axis=-1, keepdims=True)
    centred = values - center
    spread = jnp.mean(centred * centred, axis=-1, keepdims=True)
    return centred * lax.rsqrt(spread + eps) * norm_gain


def rotate(values, cos_table, sin_table):
    halfway = values.shape[-1] // 2
    turned = jnp.concatenate([-values[..., halfway:], values[..., :halfway]], axis=-1)
    return values * cos_table + turned * sin_table


def unrotate(gradient, cos_table, sin_table):
    halfway = gradient.shape[-1] // 2
    sined = gradient * sin_table
    return gradient * cos_table + jnp.concatenate(
        [sined[..., halfway:], -sined[..., :halfway]], axis=-1
    )


def angles(positions, head_size):
    exponent = jnp.arange(0, head_size, 2, dtype=jnp.float32) / head_size
    inverse = rope_base ** (-exponent)
    phases = positions.astype(jnp.float32)[:, None] * inverse[None, :]
    phases = jnp.concatenate([phases, phases], axis=-1)
    return (jnp.cos(phases)[:, None, :], jnp.sin(phases)[:, None, :])


def gated_unit(lifted):
    hidden_units = lifted.shape[-1] // 2
    return jax.nn.gelu(lifted[..., :hidden_units], approximate=False) * lifted[..., hidden_units:]


def as_heads(flat_rows, head_size):
    return flat_rows.reshape(flat_rows.shape[0], flat_rows.shape[1], -1, head_size)


def empty_state(seq_count, head_count, query_rows, head_size):
    return (
        jnp.full((seq_count, head_count, query_rows), -jnp.inf, jnp.float32),
        jnp.zeros((seq_count, head_count, query_rows), jnp.float32),
        jnp.zeros((seq_count, head_count, query_rows, head_size), jnp.float32),
    )


def forward_step(queries, scaling, state_now, shard_part):
    running_max, denominator, weighted = state_now
    key_part = as_heads(shard_part[0], queries.shape[3])
    value_part = as_heads(shard_part[1], queries.shape[3])
    scores = (
        jnp.einsum("sqhd,skhd->shqk", queries, key_part, preferred_element_type=jnp.float32)
        * scaling
    )
    new_max = jnp.max(scores, axis=-1)
    fading = jnp.exp(running_max - new_max)
    weights = jnp.exp(scores - new_max[..., None])
    denominator = denominator * fading + jnp.sum(weights, axis=-1)
    weighted = weighted * fading[..., None] + jnp.einsum(
        "shqk,skhd->shqd",
        weights.astype(jnp.bfloat16),
        value_part,
        preferred_element_type=jnp.float32,
    )
    return (new_max, denominator, weighted)


def query_step(queries, grad_out, log_total, inner_heads, scaling, shard_part):
    key_part = as_heads(shard_part[0], queries.shape[3])
    value_part = as_heads(shard_part[1], queries.shape[3])
    scores = (
        jnp.einsum("sqhd,skhd->shqk", queries, key_part, preferred_element_type=jnp.float32)
        * scaling
    )
    weights = jnp.exp(scores - log_total[..., None])
    weight_grad = jnp.einsum(
        "sqhd,skhd->shqk", grad_out, value_part, preferred_element_type=jnp.float32
    )
    score_grad = (weights * (weight_grad - inner_heads[..., None])).astype(jnp.bfloat16)
    return jnp.einsum("shqk,skhd->sqhd", score_grad, key_part, preferred_element_type=jnp.float32)


def key_step(key_heads, value_heads, scaling, shard_part):
    head_size = key_heads.shape[3]
    query_part = as_heads(shard_part[0].astype(jnp.bfloat16), head_size)
    grad_part = as_heads(shard_part[1].astype(jnp.bfloat16), head_size)
    log_part = shard_part[2].transpose(0, 2, 1)
    inner_part = shard_part[3].transpose(0, 2, 1)
    scores = (
        jnp.einsum("sqhd,skhd->shqk", query_part, key_heads, preferred_element_type=jnp.float32)
        * scaling
    )
    weights = jnp.exp(scores - log_part[..., None])
    value_grad = jnp.einsum(
        "shqk,sqhd->skhd",
        weights.astype(jnp.bfloat16),
        grad_part,
        preferred_element_type=jnp.float32,
    )
    weight_grad = jnp.einsum(
        "sqhd,skhd->shqk", grad_part, value_heads, preferred_element_type=jnp.float32
    )
    score_grad = (weights * (weight_grad - inner_part[..., None])).astype(jnp.bfloat16)
    key_grad = jnp.einsum(
        "shqk,sqhd->skhd", score_grad, query_part, preferred_element_type=jnp.float32
    )
    return (key_grad, value_grad)


MESH_ID = pl.DeviceIdType.MESH


def exchange_kernel(ctx_count, fsdp_count, x_ref, o_ref, send_sem, recv_sem, own_sem):
    count = ctx_count * fsdp_count
    me = lax.axis_index("ctx") * fsdp_count + lax.axis_index("fsdp")
    barrier = pltpu.get_barrier_semaphore()

    def target(step):
        place = lax.rem(me + step, count)
        return place, (place // fsdp_count, lax.rem(place, fsdp_count))

    def copy_to(step):
        place, device = target(step)
        return pltpu.make_async_remote_copy(
            src_ref=x_ref.at[place],
            dst_ref=o_ref.at[me],
            send_sem=send_sem.at[step],
            recv_sem=recv_sem.at[step],
            device_id=device,
            device_id_type=MESH_ID,
        )

    @pl.loop(1, count)
    def _(step):
        pl.semaphore_signal(barrier, inc=1, device_id=target(step)[1], device_id_type=MESH_ID)

    pl.semaphore_wait(barrier, count - 1)
    own = pltpu.make_async_copy(x_ref.at[me], o_ref.at[me], own_sem)
    own.start()

    @pl.loop(1, count)
    def _(step):
        copy_to(step).start()

    own.wait()

    @pl.loop(1, count)
    def _(step):
        copy_to(step).wait()


def exchange(blocks, ctx_count, fsdp_count, collective_id):
    count = ctx_count * fsdp_count
    return pl.pallas_call(
        functools.partial(exchange_kernel, ctx_count, fsdp_count),
        out_shape=jax.ShapeDtypeStruct(blocks.shape, blocks.dtype),
        in_specs=[pl.BlockSpec(memory_space=pl.ANY)],
        out_specs=pl.BlockSpec(memory_space=pl.ANY),
        scratch_shapes=[
            pltpu.SemaphoreType.DMA((count,)),
            pltpu.SemaphoreType.DMA((count,)),
            pltpu.SemaphoreType.DMA,
        ],
        compiler_params=pltpu.CompilerParams(collective_id=collective_id, has_side_effects=True),
    )(blocks)


def gather_kernel(spread, chunks, x_ref, o_ref, send_sem, recv_sem, own_sem):
    ctx, place = lax.axis_index("ctx"), lax.axis_index("fsdp")
    across = lax.rem(place + 2, 4)
    beside = place + 1 - 2 * lax.rem(place, 2)
    half = lax.rem(ctx, 2)
    other_ctx = ctx + 1 - 2 * half
    sibling, partner, neighbour = (ctx, beside), (ctx, across), (other_ctx, place)
    width = x_ref.shape[-1] // (2 * chunks if spread else chunks)
    mine = half * chunks if spread else 0
    theirs = (1 - half) * chunks

    def columns(index):
        return pl.ds(pl.multiple_of(index * width, 128), width)

    def send(src, dst, sem, device):
        return pltpu.make_async_remote_copy(
            src_ref=src,
            dst_ref=dst,
            send_sem=send_sem.at[sem],
            recv_sem=recv_sem.at[sem],
            device_id=device,
            device_id_type=MESH_ID,
        )

    def piece(index):
        return o_ref.at[across, :, columns(index)]

    barrier = pltpu.get_barrier_semaphore()
    partners = (sibling, partner, neighbour) if spread else (sibling, partner)
    for device in partners:
        pl.semaphore_signal(barrier, inc=1, device_id=device, device_id_type=MESH_ID)
    pl.semaphore_wait(barrier, len(partners))
    crossing = [
        send(
            x_ref.at[:, columns(mine + c)],
            o_ref.at[place, :, columns(mine + c)],
            c,
            partner,
        )
        for c in range(chunks)
    ]
    for copy in crossing:
        copy.start()
    started = list(crossing)
    whole = send(x_ref, o_ref.at[place], chunks, sibling)
    whole.start()
    own = pltpu.make_async_copy(x_ref, o_ref.at[place], own_sem)
    own.start()
    turned = []
    for c in range(chunks):
        crossing[c].wait_recv()
        if spread:
            turn = send(piece(mine + c), piece(mine + c), chunks + 1 + c, neighbour)
            turn.start()
            turned.append(turn)
        hand = send(piece(mine + c), piece(mine + c), 2 * chunks + 1 + c, sibling)
        hand.start()
        started.append(hand)
    handed = started[chunks:]
    for c in range(len(turned)):
        turned[c].wait_recv()
        hand = send(piece(theirs + c), piece(theirs + c), 3 * chunks + 1 + c, sibling)
        hand.start()
        handed.append(hand)
    whole.wait_recv()
    own.wait()
    for hand in handed:
        hand.wait_recv()
    for copy in crossing + turned + handed + [whole]:
        copy.wait_send()


def gather(block, spread, chunks, collective_id):
    rows, width = block.shape
    count = 4 * chunks + 1
    return pl.pallas_call(
        functools.partial(gather_kernel, spread, chunks),
        out_shape=jax.ShapeDtypeStruct((4, rows, width), block.dtype),
        in_specs=[pl.BlockSpec(memory_space=pltpu.VMEM)],
        out_specs=pl.BlockSpec(memory_space=pl.ANY),
        scratch_shapes=[
            pltpu.SemaphoreType.DMA((count,)),
            pltpu.SemaphoreType.DMA((count,)),
            pltpu.SemaphoreType.DMA,
        ],
        compiler_params=pltpu.CompilerParams(collective_id=collective_id, has_side_effects=True),
    )(block).reshape(4 * rows, width)


def pack(blocks):
    half = blocks.shape[-2] // 2
    return jnp.concatenate([blocks[..., :half, :], blocks[..., half:, :]], axis=-1)


def unpack(blocks):
    half = blocks.shape[-1] // 2
    return jnp.concatenate([blocks[..., :half], blocks[..., half:]], axis=-2)


CUTS = ((False, 1), (True, 4), (False, 4))
CONTRACT_LAST = (((1,), (1,)), ((), ()))
CONTRACT_FIRST = (((0,), (0,)), ((), ()))


def attend_kernel(q_ref, k_ref, v_ref, context_ref, log_ref):
    scores = lax.dot_general(
        q_ref[...], k_ref[...], CONTRACT_LAST, preferred_element_type=jnp.float32
    )
    top = jnp.max(scores, axis=-1, keepdims=True)
    weights = jnp.exp(scores - top)
    total = jnp.sum(weights, axis=-1, keepdims=True)
    weighted = jnp.dot(
        weights.astype(jnp.bfloat16), v_ref[...], preferred_element_type=jnp.float32
    )
    context_ref[...] = weighted / total
    log_ref[...] = top + jnp.log(total)


def attend(queries, key_rows, value_rows, block):
    rows, size = queries.shape
    return pl.pallas_call(
        attend_kernel,
        grid=(rows // block,),
        out_shape=(
            jax.ShapeDtypeStruct((rows, size), jnp.float32),
            jax.ShapeDtypeStruct((rows, 1), jnp.float32),
        ),
        in_specs=[
            pl.BlockSpec((block, size), lambda i: (i, 0)),
            pl.BlockSpec((rows, size), lambda i: (0, 0)),
            pl.BlockSpec((rows, size), lambda i: (0, 0)),
        ],
        out_specs=(
            pl.BlockSpec((block, size), lambda i: (i, 0)),
            pl.BlockSpec((block, 1), lambda i: (i, 0)),
        ),
        compiler_params=pltpu.CompilerParams(vmem_limit_bytes=48 * 1024 * 1024),
    )(queries, key_rows, value_rows)


def attend_back_kernel(
    q_ref, k_ref, v_ref, context_ref, log_ref, grad_ref, dq_ref, dk_ref, dv_ref
):
    @pl.when(pl.program_id(0) == 0)
    def _():
        dk_ref[...] = jnp.zeros_like(dk_ref)
        dv_ref[...] = jnp.zeros_like(dv_ref)

    grad = grad_ref[...]
    inner = jnp.sum(grad.astype(jnp.float32) * context_ref[...], axis=-1, keepdims=True)
    scores = lax.dot_general(
        q_ref[...], k_ref[...], CONTRACT_LAST, preferred_element_type=jnp.float32
    )
    probs = jnp.exp(scores - log_ref[...])
    prob_grad = lax.dot_general(
        grad, v_ref[...], CONTRACT_LAST, preferred_element_type=jnp.float32
    )
    score_grad = (probs * (prob_grad - inner)).astype(jnp.bfloat16)
    dv_ref[...] += lax.dot_general(
        probs.astype(jnp.bfloat16), grad, CONTRACT_FIRST, preferred_element_type=jnp.float32
    )
    dk_ref[...] += lax.dot_general(
        score_grad, q_ref[...], CONTRACT_FIRST, preferred_element_type=jnp.float32
    )
    dq_ref[...] = jnp.dot(score_grad, k_ref[...], preferred_element_type=jnp.float32)


def attend_back(queries, key_rows, value_rows, context, log_total, grad, block):
    rows, size = queries.shape
    part = pl.BlockSpec((block, size), lambda i: (i, 0))
    whole = pl.BlockSpec((rows, size), lambda i: (0, 0))
    return pl.pallas_call(
        attend_back_kernel,
        grid=(rows // block,),
        out_shape=(jax.ShapeDtypeStruct((rows, size), jnp.float32),) * 3,
        in_specs=[
            part,
            whole,
            whole,
            part,
            pl.BlockSpec((block, 1), lambda i: (i, 0)),
            part,
        ],
        out_specs=(part, whole, whole),
        compiler_params=pltpu.CompilerParams(vmem_limit_bytes=48 * 1024 * 1024),
    )(queries, key_rows, value_rows, context, log_total, grad)


def whole_mesh(me):
    def other(step):
        place = lax.rem(me + step, 32)
        return place, (place // 4, lax.rem(place, 4))

    return other


def greet_all(other):
    barrier = pltpu.get_barrier_semaphore()

    @pl.loop(1, 32)
    def _(step):
        pl.semaphore_signal(barrier, inc=1, device_id=other(step)[1], device_id_type=MESH_ID)

    pl.semaphore_wait(barrier, 31)


def swap_lanes(value):
    return pltpu.roll(value.astype(jnp.float32), 64, 1)


def low_lanes(value):
    return lax.broadcasted_iota(jnp.int32, value.shape, 1) < 64


def weight_piece(ref, by_rows, half, index, count):
    if by_rows:
        size = ref.shape[0] // (2 * count)
        start = pl.multiple_of((half * count + index) * size, 16)
        return ref.at[pl.ds(start, size), :]
    size = ref.shape[1] // (2 * count)
    start = pl.multiple_of((half * count + index) * size, 128)
    return ref.at[:, pl.ds(start, size)]


def forward_kernel(cuts, *refs):
    count = len(cuts)
    sent, shards = refs[0], refs[1 : 1 + count]
    got, context, log_ref, back = refs[1 + count : 5 + count]
    fulls = refs[5 + count : 5 + 2 * count]
    (keys, values, packed, head_send, head_recv, back_send, back_recv, own_sem) = refs[
        5 + 2 * count : 13 + 2 * count
    ]
    w_send, w_recv = refs[13 + 2 * count :]
    z, y, x, core = mesh_place()
    place = 2 * x + core
    me = 4 * (2 * z + y) + place
    across = lax.rem(place + 2, 4)
    other = whole_mesh(me)
    sibling, partner = device_at(z, y, x, 1 - core), device_at(z, y, 1 - x, core)
    neighbour = device_at(z, 1 - y, x, core)
    greet_all(other)

    def head_copy(step):
        to, device = other(step)
        return pltpu.make_async_remote_copy(
            src_ref=sent.at[to],
            dst_ref=got.at[me],
            send_sem=head_send.at[step],
            recv_sem=head_recv.at[step],
            device_id=device,
            device_id_type=MESH_ID,
        )

    def back_copy(to):
        step = lax.rem(to - me + 32, 32)
        return pltpu.make_async_remote_copy(
            src_ref=packed.at[to],
            dst_ref=back.at[me],
            send_sem=back_send.at[step],
            recv_sem=back_recv.at[step],
            device_id=(to // 4, lax.rem(to, 4)),
            device_id_type=MESH_ID,
        )

    serial = iter(range(w_send.shape[0]))

    def send(src, dst, device):
        sem = next(serial)
        copy = pltpu.make_async_remote_copy(
            src_ref=src,
            dst_ref=dst,
            send_sem=w_send.at[sem],
            recv_sem=w_recv.at[sem],
            device_id=device,
            device_id_type=MESH_ID,
        )
        copy.start()
        return copy

    @pl.loop(1, 32)
    def _(step):
        head_copy(step).start()

    own = [pltpu.make_async_copy(sent.at[me], got.at[me], own_sem.at[count])]
    own[0].start()
    crossing, handed, turned = [], [], []
    for i, (by_rows, pieces) in enumerate(cuts):
        for c in range(pieces):
            src = weight_piece(shards[i], by_rows, y, c, pieces)
            dst = weight_piece(fulls[i].at[place], by_rows, y, c, pieces)
            crossing.append((i, c, send(src, dst, partner)))
    for i in range(count):
        copy = pltpu.make_async_copy(shards[i], fulls[i].at[place], own_sem.at[i])
        copy.start()
        own.append(copy)
        handed.append(send(shards[i], fulls[i].at[place], sibling))

    def turn(entry):
        i, c, copy = entry
        copy.wait_recv()
        here = weight_piece(fulls[i].at[across], cuts[i][0], y, c, cuts[i][1])
        turned.append((i, c, send(here, here, neighbour)))
        handed.append(send(here, here, sibling))

    def hand(entry):
        i, c, copy = entry
        copy.wait_recv()
        here = weight_piece(fulls[i].at[across], cuts[i][0], 1 - y, c, cuts[i][1])
        handed.append(send(here, here, sibling))

    turn(crossing[0])
    turn(crossing[1])
    own[0].wait()

    @pl.loop(1, 32)
    def _(step):
        head_copy(step).wait()

    keys[0:1024] = got[:, 0:32, :].reshape(1024, 128)
    keys[1024:2048] = got[:, 32:64, :].reshape(1024, 128)
    values[...] = got[:, 64:96, :].reshape(1024, 128)

    def attend_block(b):
        block = lax.rem(b + me // 4, 8)
        low_rows = pl.ds(pl.multiple_of(block * 128, 128), 128)
        high_rows = pl.ds(pl.multiple_of(1024 + block * 128, 128), 128)
        queries = swap_lanes(jnp.concatenate([keys[low_rows], keys[high_rows]], axis=0))
        queries = jnp.where(low_lanes(queries), 0.0, queries).astype(jnp.bfloat16)
        scores = lax.dot_general(
            queries, keys[...], CONTRACT_LAST, preferred_element_type=jnp.float32
        )
        top = jnp.max(scores, axis=-1, keepdims=True)
        weights = jnp.exp(scores - top)
        total = jnp.sum(weights, axis=-1, keepdims=True)
        weights = weights.astype(jnp.bfloat16)
        first = jnp.dot(weights[:, :1024], values[...], preferred_element_type=jnp.float32)
        second = jnp.dot(weights[:, 1024:], values[...], preferred_element_type=jnp.float32)
        outcome = (first + pltpu.roll(second, 64, 1)) / total
        side = pltpu.roll(outcome[128:], 64, 1)
        outcome = jnp.where(low_lanes(side), outcome[:128], side)
        context[low_rows] = outcome
        log_total = top + jnp.log(total)
        log_ref[0, low_rows] = log_total[:128]
        log_ref[1, low_rows] = log_total[128:]
        packed[pl.ds(4 * block, 4)] = outcome.astype(jnp.bfloat16).reshape(4, 32, 128)

        @pl.loop(4 * block, 4 * block + 4)
        def _(to):
            @pl.when(to != me)
            def _():
                back_copy(to).start()

    turn(crossing[2])
    hand(turned[0])

    @pl.loop(0, 4)
    def _(b):
        attend_block(b)

    turn(crossing[3])
    hand(turned[1])

    @pl.loop(4, 8)
    def _(b):
        attend_block(b)

    mine = pltpu.make_async_copy(packed.at[me], back.at[me], own_sem.at[count + 1])
    mine.start()
    own.append(mine)
    for index in range(4, len(crossing)):
        turn(crossing[index])
        hand(turned[index - 2])
    hand(turned[-2])
    hand(turned[-1])

    @pl.loop(1, 32)
    def _(step):
        back_copy(lax.rem(me + step, 32)).wait()

    for copy in handed:
        copy.wait()
    for _, _, copy in crossing + turned:
        copy.wait_send()
    for copy in own[1:]:
        copy.wait()


def forward_heads(sent, shards, cuts, collective_id):
    in_vmem, anywhere = pl.BlockSpec(memory_space=pltpu.VMEM), pl.BlockSpec(memory_space=pl.ANY)
    copies = len(shards) + sum(4 * pieces for _, pieces in cuts)
    low, full = jnp.bfloat16, jnp.float32
    sems = [pltpu.SemaphoreType.DMA((32,))] * 4
    return pl.pallas_call(
        functools.partial(forward_kernel, cuts),
        out_shape=[
            jax.ShapeDtypeStruct((32, 96, 128), low),
            jax.ShapeDtypeStruct((1024, 128), full),
            jax.ShapeDtypeStruct((2, 1024, 1), full),
            jax.ShapeDtypeStruct((32, 32, 128), low),
        ]
        + [jax.ShapeDtypeStruct((4, *shard.shape), low) for shard in shards],
        in_specs=[in_vmem] * (1 + len(shards)),
        out_specs=[in_vmem] * 4 + [anywhere] * len(shards),
        scratch_shapes=[
            pltpu.VMEM((2048, 128), low),
            pltpu.VMEM((1024, 128), low),
            pltpu.VMEM((32, 32, 128), low),
            *sems,
            pltpu.SemaphoreType.DMA((len(shards) + 2,)),
            pltpu.SemaphoreType.DMA((copies,)),
            pltpu.SemaphoreType.DMA((copies,)),
        ],
        compiler_params=pltpu.CompilerParams(
            collective_id=collective_id,
            has_side_effects=True,
            vmem_limit_bytes=48 * 1024 * 1024,
        ),
    )(sent, *shards)


def back_kernel(kinds, cuts, scaling, *refs):
    count = len(kinds)
    sent, got, context, log_ref, cos_ref, sin_ref = refs[:6]
    parts, result = refs[6 : 6 + count], refs[6 + count]
    outs = refs[7 + count : 7 + 2 * count]
    (grads, keys, values, dq, dk, dv, packed, go_send, go_recv, back_send, back_recv, mine_sem) = refs[
        7 + 2 * count : 19 + 2 * count
    ]
    me = lax.axis_index("ctx") * 4 + lax.axis_index("fsdp")
    other = whole_mesh(me)
    greet_all(other)

    def go_copy(step):
        to, device = other(step)
        return pltpu.make_async_remote_copy(
            src_ref=sent.at[to],
            dst_ref=grads.at[me],
            send_sem=go_send.at[step],
            recv_sem=go_recv.at[step],
            device_id=device,
            device_id_type=MESH_ID,
        )

    def back_copy(to):
        step = lax.rem(to - me + 32, 32)
        return pltpu.make_async_remote_copy(
            src_ref=packed.at[to],
            dst_ref=result.at[me],
            send_sem=back_send.at[step],
            recv_sem=back_recv.at[step],
            device_id=(to // 4, lax.rem(to, 4)),
            device_id_type=MESH_ID,
        )

    @pl.loop(1, 32)
    def _(step):
        go_copy(step).start()

    mine = pltpu.make_async_copy(sent.at[me], grads.at[me], mine_sem.at[0])
    mine.start()
    start, turn, end = plane_moves(kinds, cuts, parts, outs, *refs[19 + 2 * count :])
    start()
    keys[0:1024] = got[:, 0:32, :].reshape(1024, 128)
    keys[1024:2048] = got[:, 32:64, :].reshape(1024, 128)
    values[...] = got[:, 64:96, :].reshape(1024, 128)
    dk[...] = jnp.zeros_like(dk)
    dv[...] = jnp.zeros_like(dv)
    mine.wait()

    @pl.loop(1, 32)
    def _(step):
        go_copy(step).wait()

    def rows_of(block):
        return (
            pl.ds(pl.multiple_of(block * 128, 128), 128),
            pl.ds(pl.multiple_of(1024 + block * 128, 128), 128),
        )

    def grad_block(block):
        low_rows, high_rows = rows_of(block)
        queries = swap_lanes(jnp.concatenate([keys[low_rows], keys[high_rows]], axis=0))
        queries = jnp.where(low_lanes(queries), 0.0, queries).astype(jnp.bfloat16)
        pair = grads[pl.ds(4 * block, 4)].reshape(128, 128).astype(jnp.float32)
        side = pltpu.roll(pair, 64, 1)
        first = low_lanes(pair)
        grad = jnp.concatenate([jnp.where(first, pair, 0.0), jnp.where(first, side, 0.0)], axis=0)
        above = jnp.concatenate([jnp.where(first, 0.0, side), jnp.where(first, 0.0, pair)], axis=0)
        grad, above = grad.astype(jnp.bfloat16), above.astype(jnp.bfloat16)
        product = pair * context[low_rows]
        inner = jnp.concatenate(
            [
                jnp.sum(jnp.where(first, product, 0.0), axis=-1, keepdims=True),
                jnp.sum(jnp.where(first, 0.0, product), axis=-1, keepdims=True),
            ],
            axis=0,
        )
        log_total = jnp.concatenate([log_ref[0, low_rows], log_ref[1, low_rows]], axis=0)
        scores = lax.dot_general(
            queries, keys[...], CONTRACT_LAST, preferred_element_type=jnp.float32
        )
        probs = jnp.exp(scores - log_total)
        prob_grad = jnp.concatenate(
            [
                lax.dot_general(
                    side_grad, values[...], CONTRACT_LAST, preferred_element_type=jnp.float32
                )
                for side_grad in (grad, above)
            ],
            axis=1,
        )
        score_grad = (probs * (prob_grad - inner)).astype(jnp.bfloat16)
        dv[...] += lax.dot_general(
            probs.astype(jnp.bfloat16), grad, CONTRACT_FIRST, preferred_element_type=jnp.float32
        )
        dk[...] += lax.dot_general(
            score_grad, queries, CONTRACT_FIRST, preferred_element_type=jnp.float32
        )
        query_grad = jnp.dot(score_grad, keys[...], preferred_element_type=jnp.float32)
        dq[low_rows] = query_grad[:128]
        dq[high_rows] = query_grad[128:]

    @pl.loop(0, 4)
    def _(block):
        grad_block(block)

    turn(4)

    @pl.loop(4, 8)
    def _(block):
        grad_block(block)

    turn(3)

    def unrotated(rows):
        both = jnp.where(
            low_lanes(dk[rows]), pltpu.roll(dq[rows] * scaling, 64, 1), dk[rows]
        )
        sined = both * sin_ref[rows]
        lane = lax.rem(lax.broadcasted_iota(jnp.int32, both.shape, 1), 64)
        turned = jnp.where(lane < 32, pltpu.roll(sined, 96, 1), -pltpu.roll(sined, 32, 1))
        return (both * cos_ref[rows] + turned).astype(jnp.bfloat16).reshape(4, 32, 128)

    @pl.loop(0, 8)
    def _(b):
        block = lax.rem(b + me // 4, 8)
        low_rows, high_rows = rows_of(block)
        places = pl.ds(4 * block, 4)
        packed[places, 0:32, :] = unrotated(low_rows)
        packed[places, 32:64, :] = unrotated(high_rows)
        side = pltpu.roll(dv[high_rows], 64, 1)
        value_pair = jnp.where(low_lanes(side), dv[low_rows], side)
        packed[places, 64:96, :] = value_pair.astype(jnp.bfloat16).reshape(4, 32, 128)

        @pl.loop(4 * block, 4 * block + 4)
        def _(to):
            @pl.when(to != me)
            def _():
                back_copy(to).start()

    own = pltpu.make_async_copy(packed.at[me], result.at[me], mine_sem.at[1])
    own.start()
    turn(64)

    @pl.loop(1, 32)
    def _(step):
        back_copy(lax.rem(me + step, 32)).wait()

    own.wait()
    end()


def back_heads(sent, saved, tables, parts, kinds, widths, cuts, scaling, collective_id):
    in_vmem, anywhere = pl.BlockSpec(memory_space=pltpu.VMEM), pl.BlockSpec(memory_space=pl.ANY)
    low, full, rows = jnp.bfloat16, jnp.float32, parts[0].shape[-2]
    result, *outs = pl.pallas_call(
        functools.partial(back_kernel, kinds, cuts, scaling),
        out_shape=[jax.ShapeDtypeStruct((32, 96, 128), low)]
        + [jax.ShapeDtypeStruct((4, rows, width), low) for width in widths],
        in_specs=[in_vmem] * (6 + len(parts)),
        out_specs=[in_vmem] + [anywhere] * len(parts),
        scratch_shapes=[
            pltpu.VMEM((32, 32, 128), low),
            pltpu.VMEM((2048, 128), low),
            pltpu.VMEM((1024, 128), low),
            pltpu.VMEM((2048, 128), full),
            pltpu.VMEM((2048, 128), full),
            pltpu.VMEM((2048, 128), full),
            pltpu.VMEM((32, 96, 128), low),
            *[pltpu.SemaphoreType.DMA((32,))] * 4,
            pltpu.SemaphoreType.DMA((2,)),
            pltpu.SemaphoreType.DMA((3 * sum(cuts),)),
            pltpu.SemaphoreType.DMA((3 * sum(cuts),)),
            pltpu.SemaphoreType.DMA((len(parts),)),
        ],
        compiler_params=pltpu.CompilerParams(
            collective_id=collective_id,
            has_side_effects=True,
            vmem_limit_bytes=56 * 1024 * 1024,
        ),
    )(sent, *saved, *tables, *parts)
    return result, [out.reshape(4 * rows, width) for out, width in zip(outs, widths)]


def by_head_forward(mixed_rows, cos_table, sin_table, scaling, shards=()):
    seq_count, row_count, _, head_count, head_size = mixed_rows.shape
    ctx_count, fsdp_count = lax.axis_size("ctx"), lax.axis_size("fsdp")
    count = ctx_count * fsdp_count
    queries = rotate(mixed_rows[:, :, 0], cos_table, sin_table).astype(jnp.bfloat16) * scaling
    key_rows = rotate(mixed_rows[:, :, 1], cos_table, sin_table).astype(jnp.bfloat16)
    value_rows = mixed_rows[:, :, 2].astype(jnp.bfloat16)
    to_head = lambda rows: rows.transpose(0, 2, 1, 3).reshape(count, row_count, head_size)
    sent = jnp.concatenate(
        [
            jnp.concatenate([to_head(queries), to_head(key_rows)], axis=-1),
            pack(to_head(value_rows)),
        ],
        axis=1,
    )
    if shards:
        got, context, log_total, back, *fulls = forward_heads(sent, shards, CUTS, 1)
        context_low = (
            unpack(back)
            .reshape(seq_count, head_count, row_count, head_size)
            .transpose(0, 2, 1, 3)
            .reshape(seq_count * row_count, head_count * head_size)
        )
        return context_low, (got, context, log_total), fulls
    got = exchange(sent, ctx_count, fsdp_count, 1)
    flat = lambda rows: rows.reshape(count * row_count, head_size)
    queries = flat(got[:, :row_count, :head_size])
    key_rows = flat(got[:, :row_count, head_size:])
    value_rows = flat(unpack(got[:, row_count:]))
    context, log_total = attend(queries, key_rows, value_rows, 256)
    back = exchange(
        pack(context.astype(jnp.bfloat16).reshape(count, row_count, head_size)),
        ctx_count,
        fsdp_count,
        2,
    )
    context_low = (
        unpack(back)
        .reshape(seq_count, head_count, row_count, head_size)
        .transpose(0, 2, 1, 3)
        .reshape(seq_count * row_count, head_count * head_size)
    )
    return context_low, (queries, key_rows, value_rows, context, log_total), ()


def by_head_back(context_grad, saved, scaling, after, planes=()):
    seq_count, row_count, head_count, head_size = context_grad.shape
    ctx_count, fsdp_count = lax.axis_size("ctx"), lax.axis_size("fsdp")
    count = ctx_count * fsdp_count
    if planes:
        sent = pack(context_grad.transpose(0, 2, 1, 3).reshape(count, row_count, head_size))
        order = jnp.arange(count * row_count, dtype=jnp.int32)
        order = order.reshape(count, 2, row_count // 2).transpose(1, 0, 2).reshape(-1)
        tables = [jnp.tile(table[:, 0], (1, 2)) for table in angles(order, head_size)]
        got, lefts = back_heads(sent, saved, tables, *planes, scaling, 2)
        parts = jnp.stack(
            [
                got[:, :row_count, :head_size],
                got[:, :row_count, head_size:],
                unpack(got[:, row_count:]),
            ]
        )
        return (
            parts.reshape(3, seq_count, head_count, row_count, head_size)
            .transpose(1, 3, 0, 2, 4)
            .reshape(seq_count * row_count, 3 * head_count * head_size)
        ), lefts
    queries, key_rows, value_rows, context, log_total = saved
    sent = pack(context_grad.transpose(0, 2, 1, 3).reshape(count, row_count, head_size))
    grad = unpack(exchange(sent, ctx_count, fsdp_count, 3)).reshape(count * row_count, head_size)
    query_grad, key_grad, value_grad = attend_back(
        queries, key_rows, value_rows, context, log_total, grad, 256
    )
    cos_all, sin_all = angles(jnp.arange(count * row_count, dtype=jnp.int32), head_size)
    cos_all, sin_all = cos_all[:, 0], sin_all[:, 0]
    query_pre = unrotate(query_grad * scaling, cos_all, sin_all).astype(jnp.bfloat16)
    key_pre = unrotate(key_grad, cos_all, sin_all).astype(jnp.bfloat16)
    split = lambda rows: rows.reshape(count, row_count, head_size)
    sent = jnp.concatenate(
        [
            jnp.concatenate([split(query_pre), split(key_pre)], axis=-1),
            pack(split(value_grad.astype(jnp.bfloat16))),
        ],
        axis=1,
    )
    if after:
        sent, after = lax.optimization_barrier((sent, after))
    got = exchange(sent, ctx_count, fsdp_count, 4)
    parts = jnp.stack(
        [got[:, :row_count, :head_size], got[:, :row_count, head_size:], unpack(got[:, row_count:])]
    )
    return (
        parts.reshape(3, seq_count, head_count, row_count, head_size)
        .transpose(1, 3, 0, 2, 4)
        .reshape(seq_count * row_count, 3 * head_count * head_size)
    ), after


def by_block_forward(mixed_rows, cos_table, sin_table, scaling, shards=()):
    seq_count, row_count, _, head_count, head_size = mixed_rows.shape
    width = head_count * head_size
    queries = rotate(mixed_rows[:, :, 0], cos_table, sin_table).astype(jnp.bfloat16)
    key_flat = (
        rotate(mixed_rows[:, :, 1], cos_table, sin_table)
        .astype(jnp.bfloat16)
        .reshape(seq_count, row_count, width)
    )
    value_flat = mixed_rows[:, :, 2].astype(jnp.bfloat16).reshape(seq_count, row_count, width)
    key_block, value_block = (
        lax.all_gather(key_flat, "fsdp", axis=1, tiled=True),
        lax.all_gather(value_flat, "fsdp", axis=1, tiled=True),
    )
    start_state = empty_state(seq_count, head_count, row_count, head_size)
    running_max, denominator, weighted = forward_step(
        queries,
        scaling,
        start_state,
        (
            lax.all_gather(key_block, "ctx", axis=1, tiled=True),
            lax.all_gather(value_block, "ctx", axis=1, tiled=True),
        ),
    )
    context = (weighted / denominator[..., None]).transpose(0, 2, 1, 3)
    log_total = running_max + jnp.log(denominator)
    context_low = context.reshape(seq_count * row_count, width).astype(jnp.bfloat16)
    saved = queries, key_block, value_block, context, log_total, cos_table, sin_table
    return context_low, saved, ()


def by_block_back(context_grad, saved, scaling, after, planes=()):
    seq_count, row_count, head_count, head_size = context_grad.shape
    width = head_count * head_size
    queries, key_block, value_block, context, log_total, cos_table, sin_table = saved
    inner = jnp.sum(context_grad.astype(jnp.float32) * context, axis=-1)
    inner_heads = inner.transpose(0, 2, 1)
    log_rows = log_total.transpose(0, 2, 1)
    query_grad = query_step(
        queries,
        context_grad,
        log_total,
        inner_heads,
        scaling,
        (
            lax.all_gather(key_block, "ctx", axis=1, tiled=True),
            lax.all_gather(value_block, "ctx", axis=1, tiled=True),
        ),
    )
    block_len = key_block.shape[1]
    query_wide = queries.reshape(seq_count, row_count, width).astype(jnp.float32)
    grad_wide = context_grad.reshape(seq_count, row_count, width).astype(jnp.float32)
    key_grad, value_grad = key_step(
        as_heads(key_block, head_size),
        as_heads(value_block, head_size),
        scaling,
        (
            lax.all_gather(query_wide, "ctx", axis=1, tiled=True),
            lax.all_gather(grad_wide, "ctx", axis=1, tiled=True),
            lax.all_gather(log_rows, "ctx", axis=1, tiled=True),
            lax.all_gather(inner, "ctx", axis=1, tiled=True),
        ),
    )
    own = lambda grad: lax.psum_scatter(
        grad.reshape(seq_count, block_len, width), "fsdp", scatter_dimension=1, tiled=True
    ).reshape(seq_count, row_count, head_count, head_size)
    query_pre = unrotate(query_grad * scaling, cos_table, sin_table)
    key_pre = unrotate(own(key_grad) * scaling, cos_table, sin_table)
    return (
        jnp.stack([query_pre, key_pre, own(value_grad)], axis=2)
        .reshape(seq_count * row_count, 3 * width)
        .astype(jnp.bfloat16)
    ), after


def group_rows(rows):
    return lax.all_gather(rows, "fsdp", axis=0, tiled=True)


def group_columns(arrays):
    count = lax.axis_size("fsdp")
    widths = [rows.shape[1] // count for rows in arrays]
    sent = jnp.stack(
        [
            jnp.concatenate(
                [rows[:, f * width : (f + 1) * width] for rows, width in zip(arrays, widths)],
                axis=1,
            )
            for f in range(count)
        ]
    )
    got = lax.all_to_all(sent, "fsdp", split_axis=0, concat_axis=0, tiled=True)
    got = got.reshape(-1, sum(widths))
    edges = [sum(widths[:i]) for i in range(len(widths) + 1)]
    return [got[:, edges[i] : edges[i + 1]] for i in range(len(widths))]


def weight_grad(left, right):
    return jnp.einsum("tw,tf->wf", left, right, preferred_element_type=jnp.float32)


def mesh_place():
    ctx, place = lax.axis_index("ctx"), lax.axis_index("fsdp")
    return ctx // 2, lax.rem(ctx, 2), place // 2, lax.rem(place, 2)


def device_at(z, y, x, core):
    return (2 * z + y, 2 * x + core)


def greet(barrier, devices):
    for device in devices:
        pl.semaphore_signal(barrier, inc=1, device_id=device, device_id_type=MESH_ID)
    pl.semaphore_wait(barrier, len(devices))


def spans(total, count):
    edges = [total * i // (count * 16) * 16 for i in range(count)] + [total]
    return list(zip(edges[:-1], edges[1:]))


def sender(send_sem, recv_sem):
    serial = iter(range(send_sem.shape[0]))

    def send(src, dst, device):
        sem = next(serial)
        copy = pltpu.make_async_remote_copy(
            src_ref=src,
            dst_ref=dst,
            send_sem=send_sem.at[sem],
            recv_sem=recv_sem.at[sem],
            device_id=device,
            device_id_type=MESH_ID,
        )
        copy.start()
        return copy

    return send


def plane_moves(kinds, cuts, ins, outs, send_sem, recv_sem, own_sem):
    z, y, x, core = mesh_place()
    to_x, to_y = device_at(z, y, 1 - x, core), device_at(z, 1 - y, x, core)
    send = sender(send_sem, recv_sem)
    firsts, seconds, owns = [], [], []

    def block(i, index):
        ref, width = ins[i], outs[i].shape[2]
        if len(ref.shape) == 3:
            return ref.at[index]
        step = ref.shape[1] - width
        return ref.at[:, pl.ds(pl.multiple_of(index * step, 128), width)]

    def start():
        for i, kind in enumerate(kinds):
            own = block(i, y if kind else x)
            away = block(i, 1 - y if kind else 1 - x)
            for low, high in spans(outs[i].shape[1], cuts[i]):
                rows = pl.ds(low, high - low)
                by_x = send((own if kind else away).at[rows], outs[i].at[1, rows], to_x)
                by_y = send((away if kind else own).at[rows], outs[i].at[2, rows], to_y)
                firsts.append((i, rows, by_x, by_y))
        for i, kind in enumerate(kinds):
            own = block(i, y if kind else x)
            copy = pltpu.make_async_copy(own, outs[i].at[0], own_sem.at[i])
            copy.start()
            owns.append(copy)

    def turn(count):
        for i, rows, by_x, by_y in firsts[len(seconds) :][:count]:
            if kinds[i]:
                by_y.wait_recv()
                seconds.append(send(outs[i].at[2, rows], outs[i].at[3, rows], to_x))
            else:
                by_x.wait_recv()
                seconds.append(send(outs[i].at[1, rows], outs[i].at[3, rows], to_y))

    def end():
        turn(len(firsts))
        for i, rows, by_x, by_y in firsts:
            (by_x if kinds[i] else by_y).wait_recv()
            by_x.wait_send()
            by_y.wait_send()
        for copy in seconds:
            copy.wait()
        for copy in owns:
            copy.wait()

    return start, turn, end


def plane_kernel(kinds, cuts, *refs):
    count = len(kinds)
    z, y, x, core = mesh_place()
    greet(
        pltpu.get_barrier_semaphore(),
        (device_at(z, y, 1 - x, core), device_at(z, 1 - y, x, core)),
    )
    start, turn, end = plane_moves(
        kinds, cuts, refs[:count], refs[count : 2 * count], *refs[2 * count :]
    )
    start()
    end()


def plane(parts, kinds, widths, cuts, collective_id):
    rows = parts[0].shape[-2]
    sems = 3 * sum(cuts)
    outs = pl.pallas_call(
        functools.partial(plane_kernel, kinds, cuts),
        out_shape=[jax.ShapeDtypeStruct((4, rows, width), jnp.bfloat16) for width in widths],
        in_specs=[pl.BlockSpec(memory_space=pltpu.VMEM)] * len(parts),
        out_specs=[pl.BlockSpec(memory_space=pl.ANY)] * len(parts),
        scratch_shapes=[
            pltpu.SemaphoreType.DMA((sems,)),
            pltpu.SemaphoreType.DMA((sems,)),
            pltpu.SemaphoreType.DMA((len(parts),)),
        ],
        compiler_params=pltpu.CompilerParams(collective_id=collective_id, has_side_effects=True),
    )(*parts)
    return [out.reshape(4 * rows, width) for out, width in zip(outs, widths)]


def finish_kernel(chunks, count, *refs):
    parts, gains = refs[:count], refs[count]
    outs, gain_got = refs[count + 1 : 2 * count + 1], refs[2 * count + 1]
    scratch = refs[2 * count + 2 :]
    core_got, z_got, mid_got, z_sent = (scratch[i * count : (i + 1) * count] for i in range(4))
    send_sem, recv_sem, gain_send, gain_recv, own_sem = scratch[4 * count :]
    z, y, x, core = mesh_place()
    me = lax.axis_index("ctx") * 4 + lax.axis_index("fsdp")
    total = len(chunks)
    barrier = pltpu.get_barrier_semaphore()

    def other(step):
        place = lax.rem(me + step, 32)
        return place, (place // 4, lax.rem(place, 4))

    @pl.loop(1, 32)
    def _(step):
        pl.semaphore_signal(barrier, inc=1, device_id=other(step)[1], device_id_type=MESH_ID)

    pl.semaphore_wait(barrier, 31)

    def send(stage, k, src, dst, device):
        return pltpu.make_async_remote_copy(
            src_ref=src,
            dst_ref=dst,
            send_sem=send_sem.at[stage * total + k],
            recv_sem=recv_sem.at[stage * total + k],
            device_id=device,
            device_id_type=MESH_ID,
        )

    def at(k):
        i, low, high = chunks[k]
        return i, pl.ds(low, high - low)

    def core_copy(k):
        i, rows = at(k)
        return send(
            0, k, parts[i].at[1 - core, rows], core_got[i].at[rows], device_at(z, y, x, 1 - core)
        )

    def inward(k):
        i, rows = at(k)
        return send(
            1, k, z_sent[i].at[rows], z_got[i].at[rows], device_at(1 + z // 2, y, x, core)
        )

    def middle(k):
        i, rows = at(k)
        return send(2, k, z_sent[i].at[rows], mid_got[i].at[rows], device_at(3 - z, y, x, core))

    def outward(k):
        i, rows = at(k)
        here = outs[i].at[y, rows]
        return send(3, k, here, here, device_at(3 * (z // 2), y, x, core))

    def across(k):
        i, rows = at(k)
        here = outs[i].at[y, rows]
        return send(4, k, here, here, device_at(z, 1 - y, x, core))

    def gain_copy(step):
        place, device = other(step)
        return pltpu.make_async_remote_copy(
            src_ref=gains.at[lax.rem(place, 4)],
            dst_ref=gain_got.at[me],
            send_sem=gain_send.at[step],
            recv_sem=gain_recv.at[step],
            device_id=device,
            device_id_type=MESH_ID,
        )

    def wide(value):
        return value.astype(jnp.float32)

    for k in range(total):
        core_copy(k).start()
    own = pltpu.make_async_copy(gains.at[lax.rem(me, 4)], gain_got.at[me], own_sem)
    own.start()

    @pl.loop(1, 32)
    def _(step):
        gain_copy(step).start()

    @pl.when((z == 0) | (z == 3))
    def _():
        for k in range(total):
            i, rows = at(k)
            core_copy(k).wait_recv()
            value = wide(parts[i][core, rows]) + wide(core_got[i][rows])
            z_sent[i][rows] = value.astype(jnp.bfloat16)
            inward(k).start()
        for k in range(total):
            outward(k).wait_recv()
            across(k).start()
        for k in range(total):
            inward(k).wait_send()

    @pl.when((z == 1) | (z == 2))
    def _():
        def meet(k):
            i, rows = at(k)
            middle(k).wait_recv()
            value = wide(z_sent[i][rows]) + wide(mid_got[i][rows])
            outs[i][y, rows] = value.astype(jnp.bfloat16)
            outward(k).start()
            across(k).start()

        for k in range(total):
            i, rows = at(k)
            core_copy(k).wait_recv()
            inward(k).wait_recv()
            value = wide(parts[i][core, rows]) + wide(core_got[i][rows]) + wide(z_got[i][rows])
            z_sent[i][rows] = value.astype(jnp.bfloat16)
            middle(k).start()
            if k > 0:
                meet(k - 1)
        meet(total - 1)
        for k in range(total):
            middle(k).wait_send()
            outward(k).wait_send()

    for k in range(total):
        i, rows = at(k)
        there = outs[i].at[1 - y, rows]
        send(4, k, there, there, device_at(z, 1 - y, x, core)).wait_recv()
        across(k).wait_send()
        core_copy(k).wait_send()
    own.wait()

    @pl.loop(1, 32)
    def _(step):
        gain_copy(step).wait()


def finish(parts, gains, cuts, collective_id):
    chunks = [
        (i, low, high) for i, cut in enumerate(cuts) for low, high in spans(parts[i].shape[1], cut)
    ]
    shapes = [part.shape for part in parts]
    buffers = [pltpu.VMEM(shape[1:], jnp.bfloat16) for shape in shapes]
    in_vmem = pl.BlockSpec(memory_space=pltpu.VMEM)
    return pl.pallas_call(
        functools.partial(finish_kernel, chunks, len(parts)),
        out_shape=[jax.ShapeDtypeStruct(shape, jnp.bfloat16) for shape in shapes]
        + [jax.ShapeDtypeStruct((32, 8, gains.shape[2]), jnp.float32)],
        in_specs=[in_vmem] * (len(parts) + 1),
        out_specs=[in_vmem] * (len(parts) + 1),
        scratch_shapes=buffers * 4
        + [
            pltpu.SemaphoreType.DMA((5 * len(chunks),)),
            pltpu.SemaphoreType.DMA((5 * len(chunks),)),
            pltpu.SemaphoreType.DMA((32,)),
            pltpu.SemaphoreType.DMA((32,)),
            pltpu.SemaphoreType.DMA,
        ],
        compiler_params=pltpu.CompilerParams(
            collective_id=collective_id,
            has_side_effects=True,
            vmem_limit_bytes=48 * 1024 * 1024,
        ),
    )(*parts, gains)


def core_blocks(left, right):
    both = weight_grad(left, right).astype(jnp.bfloat16)
    return both.reshape(2, both.shape[0] // 2, both.shape[1])


def joined_halves(out, full):
    skip = 2 * out.shape[2] - full
    return jnp.concatenate([out[0], out[1][:, skip:]], axis=1).astype(jnp.float32)


def on_device(inputs, attn_gain, attn_proj, attn_out, mlp_gain, mlp_in, mlp_out, cotangent):
    seq_count, row_count, model_width = inputs.shape
    head_size = HEAD_DIM
    head_count = HEADS
    scaling = head_size ** (-0.5)
    fsdp_count = lax.axis_size("fsdp")
    fsdp_place = lax.axis_index("fsdp")
    device_count = lax.axis_size("ctx") * fsdp_count
    one_head_each = device_count == seq_count * head_count
    start_row = (lax.axis_index("ctx") * fsdp_count + fsdp_place) * row_count
    cos_table, sin_table = angles(start_row + jnp.arange(row_count, dtype=jnp.int32), head_size)
    tokens = seq_count * row_count
    gain_width = own_rows = attn_gain.shape[0]
    gains = lax.all_gather(jnp.stack([attn_gain, mlp_gain]), "fsdp", axis=1, tiled=True).astype(
        jnp.float32
    )
    gain_one, gain_two = gains[0], gains[1]
    ctx_count = lax.axis_size("ctx")
    small = one_head_each and fsdp_count == 4 and ctx_count == 8
    if small:
        proj_full = gather(attn_proj, True, 6, 6)
        shards = attn_out, mlp_in, mlp_out
    else:
        shards = ()
        proj_full, out_full, lift_full, down_full = (
            lax.all_gather(rows, "fsdp", axis=0, tiled=True)
            for rows in (attn_proj, attn_out, mlp_in, mlp_out)
        )
    states = inputs.astype(jnp.float32)
    normed, norm_back_one = jax.vjp(layer_norm, states, gain_one)
    normed_low = normed.astype(jnp.bfloat16).reshape(tokens, model_width)
    mixed_rows = jnp.dot(normed_low, proj_full, preferred_element_type=jnp.float32).reshape(
        seq_count, row_count, 3, head_count, head_size
    )
    attention, attention_back = (
        (by_head_forward, by_head_back) if one_head_each else (by_block_forward, by_block_back)
    )
    context_low, saved, fulls = attention(mixed_rows, cos_table, sin_table, scaling, shards)
    if small:
        out_full, lift_full, down_full = (
            full.reshape(4 * full.shape[1], full.shape[2]) for full in fulls
        )
    branch = jnp.dot(context_low, out_full, preferred_element_type=jnp.float32).reshape(
        seq_count, row_count, model_width
    )
    middle = states + branch
    normed_two, norm_back_two = jax.vjp(layer_norm, middle, gain_two)
    normed_two_low = normed_two.astype(jnp.bfloat16).reshape(tokens, model_width)
    lifted = jnp.dot(normed_two_low, lift_full, preferred_element_type=jnp.float32)
    gate_out, gated_back = jax.vjp(gated_unit, lifted)
    gate_low = gate_out.astype(jnp.bfloat16)
    outputs = (
        middle
        + jnp.dot(gate_low, down_full, preferred_element_type=jnp.float32).reshape(
            seq_count, row_count, model_width
        )
    ).astype(jnp.bfloat16)
    seed_rows = cotangent.reshape(tokens, model_width)
    gate_grad = jnp.einsum("td,fd->tf", seed_rows, down_full, preferred_element_type=jnp.float32)
    lifted_grad = gated_back(gate_grad)[0].astype(jnp.bfloat16)
    normed_two_grad = jnp.einsum(
        "tf,wf->tw", lifted_grad, lift_full, preferred_element_type=jnp.float32
    ).reshape(seq_count, row_count, model_width)
    middle_part, gain_two_grad = norm_back_two(normed_two_grad)
    middle_grad = cotangent.astype(jnp.float32) + middle_part
    middle_low = middle_grad.reshape(tokens, model_width).astype(jnp.bfloat16)
    context_grad = (
        jnp.einsum("tv,wv->tw", middle_low, out_full, preferred_element_type=jnp.float32)
        .astype(jnp.bfloat16)
        .reshape(seq_count, row_count, head_count, head_size)
    )
    if small:
        width, lifted_width = model_width // 2, lifted_grad.shape[1]
        hidden = gate_low.shape[1] // 2
        lift_half = -(-lifted_width // 256) * 128
        gate_halves = jnp.stack([gate_low[:, :hidden], gate_low[:, hidden:]])
        planes = (
            (lifted_grad, normed_two_low, gate_halves, context_low, normed_low, seed_rows, middle_low),
            (1, 0, 0, 0, 0, 1, 1),
            (lift_half, width, hidden, width, width, width, width),
            (4, 1, 2, 1, 1, 1, 1),
        )
        mixed_grad, sides = attention_back(context_grad, saved, scaling, (), planes)
        lift_right, normed_two_left, gate_left, context_left, normed_left, seed_right, middle_right = (
            sides
        )
        (mixed_right,) = plane((mixed_grad,), (1,), (mixed_grad.shape[1] // 2,), (4,), 7)
        lift_part = core_blocks(normed_two_left, lift_right)
        down_part = core_blocks(gate_left, seed_right)
        out_part = core_blocks(context_left, middle_right)
        proj_part = core_blocks(normed_left, mixed_right)
    else:
        normed_two_part, gate_part, context_part, normed_part = group_columns(
            (normed_two_low, gate_low, context_low, normed_low)
        )
        seed_group = group_rows(seed_rows)
        joined = group_rows(jnp.concatenate([lifted_grad, middle_low], axis=1))
        lift_grad = weight_grad(normed_two_part, joined[:, : lifted_grad.shape[1]])
        out_grad = weight_grad(context_part, joined[:, lifted_grad.shape[1] :])
        down_grad = weight_grad(gate_part, seed_group)
        first_grads = tuple(grad.astype(jnp.bfloat16) for grad in (lift_grad, down_grad, out_grad))
        mixed_grad, first_grads = attention_back(context_grad, saved, scaling, first_grads)
        mixed_group = group_rows(mixed_grad)
        proj_grad = weight_grad(normed_part, mixed_group).astype(jnp.bfloat16)
        lift_sum, down_sum, out_sum, proj_sum = (
            total.astype(jnp.float32) for total in lax.psum((*first_grads, proj_grad), "ctx")
        )
    normed_grad = jnp.einsum(
        "tm,wm->tw", mixed_grad, proj_full, preferred_element_type=jnp.float32
    ).reshape(seq_count, row_count, model_width)
    state_part, gain_one_grad = norm_back_one(normed_grad)
    input_grad = middle_grad + state_part
    gain_grads = jnp.stack([gain_one_grad, gain_two_grad])
    if small:
        shares = gain_grads.reshape(2, fsdp_count, gain_width).transpose(1, 0, 2)
        shares = jnp.concatenate([shares, jnp.zeros((fsdp_count, 6, gain_width))], axis=1)
        lift_sum, down_sum, out_sum, proj_sum, gain_got = finish(
            (lift_part, down_part, out_part, proj_part), shares, (8, 4, 2, 4), 8
        )
        lift_sum = joined_halves(lift_sum, lifted_width)
        down_sum = joined_halves(down_sum, model_width)
        out_sum = joined_halves(out_sum, model_width)
        proj_sum = joined_halves(proj_sum, mixed_grad.shape[1])
        gain_own = jnp.sum(gain_got, axis=0)
    else:
        gain_sums = lax.psum(gain_grads, ("ctx", "fsdp"))
        gain_own = lax.dynamic_slice_in_dim(gain_sums, fsdp_place * gain_width, gain_width, axis=1)
    return (
        outputs,
        input_grad,
        gain_own[0],
        proj_sum,
        out_sum,
        gain_own[1],
        lift_sum,
        down_sum,
    )


def solution(mesh):
    in_specs = (
        P(None, ("ctx", "fsdp"), None),
        P("fsdp"),
        P("fsdp", None),
        P("fsdp", None),
        P("fsdp"),
        P("fsdp", None),
        P("fsdp", None),
        P(None, ("ctx", "fsdp"), None),
    )
    out_specs = (
        P(None, ("ctx", "fsdp"), None),
        P(None, ("ctx", "fsdp"), None),
        P("fsdp"),
        P("fsdp", None),
        P("fsdp", None),
        P("fsdp"),
        P("fsdp", None),
        P("fsdp", None),
    )
    return jax.shard_map(
        on_device, mesh=mesh, in_specs=in_specs, out_specs=out_specs, check_vma=False
    )
```

```python
import functools

import jax
import jax.numpy as jnp
from jax import lax
from jax.experimental import pallas as pl
from jax.experimental.pallas import tpu as pltpu
from jax.sharding import PartitionSpec as P

HEADS = 16
HEAD_DIM = 64


eps = 1e-05
rope_base = 160000.0


def layer_norm(values, norm_gain):
    center = jnp.mean(values, axis=-1, keepdims=True)
    centred = values - center
    spread = jnp.mean(centred * centred, axis=-1, keepdims=True)
    return centred * lax.rsqrt(spread + eps) * norm_gain


def rotate(values, cos_table, sin_table):
    halfway = values.shape[-1] // 2
    turned = jnp.concatenate([-values[..., halfway:], values[..., :halfway]], axis=-1)
    return values * cos_table + turned * sin_table


def unrotate(gradient, cos_table, sin_table):
    halfway = gradient.shape[-1] // 2
    sined = gradient * sin_table
    return gradient * cos_table + jnp.concatenate(
        [sined[..., halfway:], -sined[..., :halfway]], axis=-1
    )


def angles(positions, head_size):
    exponent = jnp.arange(0, head_size, 2, dtype=jnp.float32) / head_size
    inverse = rope_base ** (-exponent)
    phases = positions.astype(jnp.float32)[:, None] * inverse[None, :]
    phases = jnp.concatenate([phases, phases], axis=-1)
    return (jnp.cos(phases)[:, None, :], jnp.sin(phases)[:, None, :])


def gated_unit(lifted):
    hidden_units = lifted.shape[-1] // 2
    return jax.nn.gelu(lifted[..., :hidden_units], approximate=False) * lifted[..., hidden_units:]


def as_heads(flat_rows, head_size):
    return flat_rows.reshape(flat_rows.shape[0], flat_rows.shape[1], -1, head_size)


def empty_state(seq_count, head_count, query_rows, head_size):
    return (
        jnp.full((seq_count, head_count, query_rows), -jnp.inf, jnp.float32),
        jnp.zeros((seq_count, head_count, query_rows), jnp.float32),
        jnp.zeros((seq_count, head_count, query_rows, head_size), jnp.float32),
    )


def forward_step(queries, scaling, state_now, shard_part):
    running_max, denominator, weighted = state_now
    key_part = as_heads(shard_part[0], queries.shape[3])
    value_part = as_heads(shard_part[1], queries.shape[3])
    scores = (
        jnp.einsum("sqhd,skhd->shqk", queries, key_part, preferred_element_type=jnp.float32)
        * scaling
    )
    new_max = jnp.max(scores, axis=-1)
    fading = jnp.exp(running_max - new_max)
    weights = jnp.exp(scores - new_max[..., None])
    denominator = denominator * fading + jnp.sum(weights, axis=-1)
    weighted = weighted * fading[..., None] + jnp.einsum(
        "shqk,skhd->shqd",
        weights.astype(jnp.bfloat16),
        value_part,
        preferred_element_type=jnp.float32,
    )
    return (new_max, denominator, weighted)


def query_step(queries, grad_out, log_total, inner_heads, scaling, shard_part):
    key_part = as_heads(shard_part[0], queries.shape[3])
    value_part = as_heads(shard_part[1], queries.shape[3])
    scores = (
        jnp.einsum("sqhd,skhd->shqk", queries, key_part, preferred_element_type=jnp.float32)
        * scaling
    )
    weights = jnp.exp(scores - log_total[..., None])
    weight_grad = jnp.einsum(
        "sqhd,skhd->shqk", grad_out, value_part, preferred_element_type=jnp.float32
    )
    score_grad = (weights * (weight_grad - inner_heads[..., None])).astype(jnp.bfloat16)
    return jnp.einsum("shqk,skhd->sqhd", score_grad, key_part, preferred_element_type=jnp.float32)


def key_step(key_heads, value_heads, scaling, shard_part):
    head_size = key_heads.shape[3]
    query_part = as_heads(shard_part[0].astype(jnp.bfloat16), head_size)
    grad_part = as_heads(shard_part[1].astype(jnp.bfloat16), head_size)
    log_part = shard_part[2].transpose(0, 2, 1)
    inner_part = shard_part[3].transpose(0, 2, 1)
    scores = (
        jnp.einsum("sqhd,skhd->shqk", query_part, key_heads, preferred_element_type=jnp.float32)
        * scaling
    )
    weights = jnp.exp(scores - log_part[..., None])
    value_grad = jnp.einsum(
        "shqk,sqhd->skhd",
        weights.astype(jnp.bfloat16),
        grad_part,
        preferred_element_type=jnp.float32,
    )
    weight_grad = jnp.einsum(
        "sqhd,skhd->shqk", grad_part, value_heads, preferred_element_type=jnp.float32
    )
    score_grad = (weights * (weight_grad - inner_part[..., None])).astype(jnp.bfloat16)
    key_grad = jnp.einsum(
        "shqk,sqhd->skhd", score_grad, query_part, preferred_element_type=jnp.float32
    )
    return (key_grad, value_grad)


MESH_ID = pl.DeviceIdType.MESH


def exchange_kernel(ctx_count, fsdp_count, x_ref, o_ref, send_sem, recv_sem, own_sem):
    count = ctx_count * fsdp_count
    me = lax.axis_index("ctx") * fsdp_count + lax.axis_index("fsdp")
    barrier = pltpu.get_barrier_semaphore()

    def target(step):
        place = lax.rem(me + step, count)
        return place, (place // fsdp_count, lax.rem(place, fsdp_count))

    def copy_to(step):
        place, device = target(step)
        return pltpu.make_async_remote_copy(
            src_ref=x_ref.at[place],
            dst_ref=o_ref.at[me],
            send_sem=send_sem.at[step],
            recv_sem=recv_sem.at[step],
            device_id=device,
            device_id_type=MESH_ID,
        )

    @pl.loop(1, count)
    def _(step):
        pl.semaphore_signal(barrier, inc=1, device_id=target(step)[1], device_id_type=MESH_ID)

    pl.semaphore_wait(barrier, count - 1)
    own = pltpu.make_async_copy(x_ref.at[me], o_ref.at[me], own_sem)
    own.start()

    @pl.loop(1, count)
    def _(step):
        copy_to(step).start()

    own.wait()

    @pl.loop(1, count)
    def _(step):
        copy_to(step).wait()


def exchange(blocks, ctx_count, fsdp_count, collective_id):
    count = ctx_count * fsdp_count
    return pl.pallas_call(
        functools.partial(exchange_kernel, ctx_count, fsdp_count),
        out_shape=jax.ShapeDtypeStruct(blocks.shape, blocks.dtype),
        in_specs=[pl.BlockSpec(memory_space=pl.ANY)],
        out_specs=pl.BlockSpec(memory_space=pl.ANY),
        scratch_shapes=[
            pltpu.SemaphoreType.DMA((count,)),
            pltpu.SemaphoreType.DMA((count,)),
            pltpu.SemaphoreType.DMA,
        ],
        compiler_params=pltpu.CompilerParams(collective_id=collective_id, has_side_effects=True),
    )(blocks)


def pack(blocks):
    half = blocks.shape[-2] // 2
    return jnp.concatenate([blocks[..., :half, :], blocks[..., half:, :]], axis=-1)


def unpack(blocks):
    half = blocks.shape[-1] // 2
    return jnp.concatenate([blocks[..., :half], blocks[..., half:]], axis=-2)


AHEAD = 3
CUTS = ((False, 6), (False, 1), (True, 4), (False, 4))
CONTRACT_LAST = (((1,), (1,)), ((), ()))
CONTRACT_FIRST = (((0,), (0,)), ((), ()))


def attend_kernel(q_ref, k_ref, v_ref, context_ref, log_ref):
    scores = lax.dot_general(
        q_ref[...], k_ref[...], CONTRACT_LAST, preferred_element_type=jnp.float32
    )
    top = jnp.max(scores, axis=-1, keepdims=True)
    weights = jnp.exp(scores - top)
    total = jnp.sum(weights, axis=-1, keepdims=True)
    weighted = jnp.dot(
        weights.astype(jnp.bfloat16), v_ref[...], preferred_element_type=jnp.float32
    )
    context_ref[...] = weighted / total
    log_ref[...] = top + jnp.log(total)


def attend(queries, key_rows, value_rows, block):
    rows, size = queries.shape
    return pl.pallas_call(
        attend_kernel,
        grid=(rows // block,),
        out_shape=(
            jax.ShapeDtypeStruct((rows, size), jnp.float32),
            jax.ShapeDtypeStruct((rows, 1), jnp.float32),
        ),
        in_specs=[
            pl.BlockSpec((block, size), lambda i: (i, 0)),
            pl.BlockSpec((rows, size), lambda i: (0, 0)),
            pl.BlockSpec((rows, size), lambda i: (0, 0)),
        ],
        out_specs=(
            pl.BlockSpec((block, size), lambda i: (i, 0)),
            pl.BlockSpec((block, 1), lambda i: (i, 0)),
        ),
        compiler_params=pltpu.CompilerParams(vmem_limit_bytes=48 * 1024 * 1024),
    )(queries, key_rows, value_rows)


def attend_back_kernel(
    q_ref, k_ref, v_ref, context_ref, log_ref, grad_ref, dq_ref, dk_ref, dv_ref
):
    @pl.when(pl.program_id(0) == 0)
    def _():
        dk_ref[...] = jnp.zeros_like(dk_ref)
        dv_ref[...] = jnp.zeros_like(dv_ref)

    grad = grad_ref[...]
    inner = jnp.sum(grad.astype(jnp.float32) * context_ref[...], axis=-1, keepdims=True)
    scores = lax.dot_general(
        q_ref[...], k_ref[...], CONTRACT_LAST, preferred_element_type=jnp.float32
    )
    probs = jnp.exp(scores - log_ref[...])
    prob_grad = lax.dot_general(
        grad, v_ref[...], CONTRACT_LAST, preferred_element_type=jnp.float32
    )
    score_grad = (probs * (prob_grad - inner)).astype(jnp.bfloat16)
    dv_ref[...] += lax.dot_general(
        probs.astype(jnp.bfloat16), grad, CONTRACT_FIRST, preferred_element_type=jnp.float32
    )
    dk_ref[...] += lax.dot_general(
        score_grad, q_ref[...], CONTRACT_FIRST, preferred_element_type=jnp.float32
    )
    dq_ref[...] = jnp.dot(score_grad, k_ref[...], preferred_element_type=jnp.float32)


def attend_back(queries, key_rows, value_rows, context, log_total, grad, block):
    rows, size = queries.shape
    part = pl.BlockSpec((block, size), lambda i: (i, 0))
    whole = pl.BlockSpec((rows, size), lambda i: (0, 0))
    return pl.pallas_call(
        attend_back_kernel,
        grid=(rows // block,),
        out_shape=(jax.ShapeDtypeStruct((rows, size), jnp.float32),) * 3,
        in_specs=[
            part,
            whole,
            whole,
            part,
            pl.BlockSpec((block, 1), lambda i: (i, 0)),
            part,
        ],
        out_specs=(part, whole, whole),
        compiler_params=pltpu.CompilerParams(vmem_limit_bytes=48 * 1024 * 1024),
    )(queries, key_rows, value_rows, context, log_total, grad)


def whole_mesh(me):
    def other(step):
        place = lax.rem(me + step, 32)
        return place, (place // 4, lax.rem(place, 4))

    return other


def greet_all(other):
    barrier = pltpu.get_barrier_semaphore()

    @pl.loop(1, 32)
    def _(step):
        pl.semaphore_signal(barrier, inc=1, device_id=other(step)[1], device_id_type=MESH_ID)

    pl.semaphore_wait(barrier, 31)


def swap_lanes(value):
    return pltpu.roll(value.astype(jnp.float32), 64, 1)


def low_lanes(value):
    return lax.broadcasted_iota(jnp.int32, value.shape, 1) < 64


def weight_piece(ref, by_rows, half, index, count):
    if by_rows:
        size = ref.shape[0] // (2 * count)
        start = pl.multiple_of((half * count + index) * size, 16)
        return ref.at[pl.ds(start, size), :]
    size = ref.shape[1] // (2 * count)
    start = pl.multiple_of((half * count + index) * size, 128)
    return ref.at[:, pl.ds(start, size)]


def forward_kernel(cuts, scaling, *refs):
    count = len(cuts)
    x_ref, cos_ref, sin_ref, gain_ref = refs[:4]
    shards = refs[4 : 4 + count]
    normed_ref, gains, got, context, log_ref, back = refs[4 + count : 10 + count]
    fulls = refs[10 + count : 10 + 2 * count]
    (sent, keys, values, packed, head_send, head_recv, back_send, back_recv, own_sem) = refs[
        10 + 2 * count : 19 + 2 * count
    ]
    w_send, w_recv = refs[19 + 2 * count :]
    targets, proj = fulls, fulls[0]
    z, y, x, core = mesh_place()
    place = 2 * x + core
    me = 4 * (2 * z + y) + place
    across = lax.rem(place + 2, 4)
    other = whole_mesh(me)
    sibling, partner = device_at(z, y, x, 1 - core), device_at(z, y, 1 - x, core)
    corner = device_at(z, y, 1 - x, 1 - core)
    neighbour = device_at(z, 1 - y, x, core)
    greet_all(other)

    def head_copy(step):
        to, device = other(step)
        return pltpu.make_async_remote_copy(
            src_ref=sent.at[to],
            dst_ref=got.at[me],
            send_sem=head_send.at[step],
            recv_sem=head_recv.at[step],
            device_id=device,
            device_id_type=MESH_ID,
        )

    def back_copy(to):
        step = lax.rem(to - me + 32, 32)
        return pltpu.make_async_remote_copy(
            src_ref=packed.at[to],
            dst_ref=back.at[me],
            send_sem=back_send.at[step],
            recv_sem=back_recv.at[step],
            device_id=(to // 4, lax.rem(to, 4)),
            device_id_type=MESH_ID,
        )

    send = sender(w_send, w_recv)
    crossing, handed, turned = [], [], []

    todo = [(i, c) for i in range(count) for c in range(cuts[i][1])]
    first = cuts[0][1]

    def cross(pieces=1):
        for i, c in todo[len(crossing) :][:pieces]:
            src = weight_piece(shards[i], cuts[i][0], y, c, cuts[i][1])
            dst = weight_piece(targets[i].at[place], cuts[i][0], y, c, cuts[i][1])
            crossing.append((i, c, send(src, dst, partner)))

    def keep(i):
        copy = pltpu.make_async_copy(shards[i], targets[i].at[place], own_sem.at[i])
        copy.start()
        return copy

    def turn(entry):
        i, c, copy = entry
        copy.wait_recv()
        here = weight_piece(targets[i].at[across], cuts[i][0], y, c, cuts[i][1])
        turned.append((i, c, send(here, here, neighbour)))
        cross()
        handed.append(send(here, here, sibling))

    def hand(entry):
        i, c, copy = entry
        copy.wait_recv()
        here = weight_piece(targets[i].at[across], cuts[i][0], 1 - y, c, cuts[i][1])
        handed.append(send(here, here, sibling))

    gain_moves = [
        send(gain_ref, gains.at[place], device) for device in (sibling, partner, corner)
    ]
    cross(AHEAD)
    handed.append(send(shards[0], proj.at[place], sibling))
    kept = pltpu.make_async_copy(gain_ref, gains.at[place], own_sem.at[count])
    kept.start()
    owns = [keep(0)]
    states = x_ref[...].astype(jnp.float32)
    centred = states - jnp.mean(states, axis=-1, keepdims=True)
    spread = jnp.mean(centred * centred, axis=-1, keepdims=True)
    centred = centred * lax.rsqrt(spread + eps)
    kept.wait()
    for copy in gain_moves:
        copy.wait()
    for f in range(4):
        part = centred[:, f * 256 : (f + 1) * 256] * gains[f, 0:1, :].astype(jnp.float32)
        normed_ref[:, f * 256 : (f + 1) * 256] = part.astype(jnp.bfloat16)
    for c in range(first):
        turn(crossing[c])
    for c in range(first):
        hand(turned[c])
    owns[0].wait()
    for copy in handed[: 1 + 2 * first]:
        copy.wait_recv()
    cos = jnp.concatenate([cos_ref[...]] * 2, axis=1)
    sin = jnp.concatenate([sin_ref[...]] * 2, axis=1)

    def turn_heads(value):
        lane = lax.rem(lax.broadcasted_iota(jnp.int32, value.shape, 1), 64)
        turned_lanes = jnp.where(lane < 32, -pltpu.roll(value, 224, 1), pltpu.roll(value, 32, 1))
        return value * cos + turned_lanes * sin

    @pl.loop(0, 4)
    def _(quad):
        def product(start):
            columns = pl.ds(pl.multiple_of(start + quad * 256, 128), 256)
            total = jnp.dot(
                normed_ref[:, :256], proj[0, :, columns], preferred_element_type=jnp.float32
            )
            for f in range(1, 4):
                total += jnp.dot(
                    normed_ref[:, f * 256 : (f + 1) * 256],
                    proj[f, :, columns],
                    preferred_element_type=jnp.float32,
                )
            return total

        queries = turn_heads(product(0)).astype(jnp.bfloat16).astype(jnp.float32) * scaling
        key_rows = turn_heads(product(1024))
        value_rows = product(2048)
        for pair in range(2):
            lanes = slice(pair * 128, (pair + 1) * 128)
            q, k, v = queries[:, lanes], key_rows[:, lanes], value_rows[:, lanes]
            swapped_q, swapped_k = pltpu.roll(q, 64, 1), pltpu.roll(k, 64, 1)
            even = jnp.where(low_lanes(q), q, swapped_k).astype(jnp.bfloat16)
            odd = jnp.where(low_lanes(q), swapped_q, k).astype(jnp.bfloat16)
            swapped_v = pltpu.roll(v, 64, 1)
            for seq in range(2):
                head = seq * 16 + quad * 4 + pair * 2
                low, mid, high = seq * 64, seq * 64 + 32, seq * 64 + 64
                sent[head, 0:64] = even[low:high]
                sent[head + 1, 0:64] = odd[low:high]
                mask = low_lanes(v[low:mid])
                sent[head, 64:96] = jnp.where(mask, v[low:mid], swapped_v[mid:high]).astype(
                    jnp.bfloat16
                )
                sent[head + 1, 64:96] = jnp.where(mask, swapped_v[low:mid], v[mid:high]).astype(
                    jnp.bfloat16
                )

    @pl.loop(1, 32)
    def _(step):
        head_copy(step).start()

    own_head = pltpu.make_async_copy(sent.at[me], got.at[me], own_sem.at[count + 1])
    own_head.start()
    for i in range(1, count):
        owns.append(keep(i))
        handed.append(send(shards[i], targets[i].at[place], sibling))
    for c in range(first, first + 3):
        turn(crossing[c])
    hand(turned[first])
    own_head.wait()

    @pl.loop(1, 32)
    def _(step):
        head_copy(step).wait()

    keys[0:1024] = got[:, 0:32, :].reshape(1024, 128)
    keys[1024:2048] = got[:, 32:64, :].reshape(1024, 128)
    values[...] = got[:, 64:96, :].reshape(1024, 128)

    def attend_block(b):
        block = lax.rem(b + me // 4, 8)
        low_rows = pl.ds(pl.multiple_of(block * 128, 128), 128)
        high_rows = pl.ds(pl.multiple_of(1024 + block * 128, 128), 128)
        queries = swap_lanes(jnp.concatenate([keys[low_rows], keys[high_rows]], axis=0))
        queries = jnp.where(low_lanes(queries), 0.0, queries).astype(jnp.bfloat16)
        scores = lax.dot_general(
            queries, keys[...], CONTRACT_LAST, preferred_element_type=jnp.float32
        )
        top = jnp.max(scores, axis=-1, keepdims=True)
        weights = jnp.exp(scores - top)
        total = jnp.sum(weights, axis=-1, keepdims=True)
        weights = weights.astype(jnp.bfloat16)
        first = jnp.dot(weights[:, :1024], values[...], preferred_element_type=jnp.float32)
        second = jnp.dot(weights[:, 1024:], values[...], preferred_element_type=jnp.float32)
        outcome = (first + pltpu.roll(second, 64, 1)) / total
        side = pltpu.roll(outcome[128:], 64, 1)
        outcome = jnp.where(low_lanes(side), outcome[:128], side)
        context[low_rows] = outcome
        log_total = top + jnp.log(total)
        log_ref[0, low_rows] = log_total[:128]
        log_ref[1, low_rows] = log_total[128:]
        packed[pl.ds(4 * block, 4)] = outcome.astype(jnp.bfloat16).reshape(4, 32, 128)

        @pl.loop(4 * block, 4 * block + 4)
        def _(to):
            @pl.when(to != me)
            def _():
                back_copy(to).start()

    turn(crossing[first + 3])
    hand(turned[first + 1])

    @pl.loop(0, 4)
    def _(b):
        attend_block(b)

    turn(crossing[first + 4])
    hand(turned[first + 2])

    @pl.loop(4, 8)
    def _(b):
        attend_block(b)

    mine = pltpu.make_async_copy(packed.at[me], back.at[me], own_sem.at[count + 2])
    mine.start()
    owns.append(mine)
    for index in range(first + 5, len(todo)):
        turn(crossing[index])
        hand(turned[index - 2])
    hand(turned[-2])
    hand(turned[-1])

    @pl.loop(1, 32)
    def _(step):
        back_copy(lax.rem(me + step, 32)).wait()

    for copy in handed[1 + 2 * first :]:
        copy.wait_recv()
    for copy in handed:
        copy.wait_send()
    for _, _, copy in crossing + turned:
        copy.wait_send()
    for copy in owns[1:]:
        copy.wait()


def forward_heads(rows, cos_table, sin_table, gain, shards, cuts, scaling, collective_id):
    in_vmem, anywhere = pl.BlockSpec(memory_space=pltpu.VMEM), pl.BlockSpec(memory_space=pl.ANY)
    copies = 3 + len(shards) + sum(4 * pieces for _, pieces in cuts)
    low, full = jnp.bfloat16, jnp.float32
    sems = [pltpu.SemaphoreType.DMA((32,))] * 4
    proj, *rest = shards
    return pl.pallas_call(
        functools.partial(forward_kernel, cuts, scaling),
        out_shape=[
            jax.ShapeDtypeStruct(rows.shape, low),
            jax.ShapeDtypeStruct((4, *gain.shape), low),
            jax.ShapeDtypeStruct((32, 96, 128), low),
            jax.ShapeDtypeStruct((1024, 128), full),
            jax.ShapeDtypeStruct((2, 1024, 1), full),
            jax.ShapeDtypeStruct((32, 32, 128), low),
        ]
        + [jax.ShapeDtypeStruct((4, *shard.shape), low) for shard in shards],
        in_specs=[in_vmem] * (4 + len(shards)),
        out_specs=[in_vmem] * 7 + [anywhere] * len(rest),
        scratch_shapes=[
            pltpu.VMEM((32, 96, 128), low),
            pltpu.VMEM((2048, 128), low),
            pltpu.VMEM((1024, 128), low),
            pltpu.VMEM((32, 32, 128), low),
            *sems,
            pltpu.SemaphoreType.DMA((len(shards) + 3,)),
            pltpu.SemaphoreType.DMA((copies,)),
            pltpu.SemaphoreType.DMA((copies,)),
        ],
        compiler_params=pltpu.CompilerParams(
            collective_id=collective_id,
            has_side_effects=True,
            vmem_limit_bytes=56 * 1024 * 1024,
        ),
    )(rows, cos_table, sin_table, gain, *shards)


def back_kernel(kinds, cuts, scaling, *refs):
    count = len(kinds)
    sent, got, context, log_ref, cos_ref, sin_ref = refs[:6]
    parts, result = refs[6 : 6 + count], refs[6 + count]
    outs = refs[7 + count : 7 + 2 * count]
    (grads, keys, values, dq, dk, dv, packed, go_send, go_recv, back_send, back_recv, mine_sem) = refs[
        7 + 2 * count : 19 + 2 * count
    ]
    me = lax.axis_index("ctx") * 4 + lax.axis_index("fsdp")
    other = whole_mesh(me)
    greet_all(other)

    def go_copy(step):
        to, device = other(step)
        return pltpu.make_async_remote_copy(
            src_ref=sent.at[to],
            dst_ref=grads.at[me],
            send_sem=go_send.at[step],
            recv_sem=go_recv.at[step],
            device_id=device,
            device_id_type=MESH_ID,
        )

    def back_copy(to):
        step = lax.rem(to - me + 32, 32)
        return pltpu.make_async_remote_copy(
            src_ref=packed.at[to],
            dst_ref=result.at[me],
            send_sem=back_send.at[step],
            recv_sem=back_recv.at[step],
            device_id=(to // 4, lax.rem(to, 4)),
            device_id_type=MESH_ID,
        )

    @pl.loop(1, 32)
    def _(step):
        go_copy(step).start()

    mine = pltpu.make_async_copy(sent.at[me], grads.at[me], mine_sem.at[0])
    mine.start()
    start, turn, end = plane_moves(kinds, cuts, parts, outs, *refs[19 + 2 * count :])
    start()
    keys[0:1024] = got[:, 0:32, :].reshape(1024, 128)
    keys[1024:2048] = got[:, 32:64, :].reshape(1024, 128)
    values[...] = got[:, 64:96, :].reshape(1024, 128)
    dk[...] = jnp.zeros_like(dk)
    dv[...] = jnp.zeros_like(dv)
    mine.wait()

    @pl.loop(1, 32)
    def _(step):
        go_copy(step).wait()

    def rows_of(block):
        return (
            pl.ds(pl.multiple_of(block * 128, 128), 128),
            pl.ds(pl.multiple_of(1024 + block * 128, 128), 128),
        )

    def grad_block(block):
        low_rows, high_rows = rows_of(block)
        queries = swap_lanes(jnp.concatenate([keys[low_rows], keys[high_rows]], axis=0))
        queries = jnp.where(low_lanes(queries), 0.0, queries).astype(jnp.bfloat16)
        pair = grads[pl.ds(4 * block, 4)].reshape(128, 128).astype(jnp.float32)
        side = pltpu.roll(pair, 64, 1)
        first = low_lanes(pair)
        grad = jnp.concatenate([jnp.where(first, pair, 0.0), jnp.where(first, side, 0.0)], axis=0)
        above = jnp.concatenate([jnp.where(first, 0.0, side), jnp.where(first, 0.0, pair)], axis=0)
        grad, above = grad.astype(jnp.bfloat16), above.astype(jnp.bfloat16)
        product = pair * context[low_rows]
        inner = jnp.concatenate(
            [
                jnp.sum(jnp.where(first, product, 0.0), axis=-1, keepdims=True),
                jnp.sum(jnp.where(first, 0.0, product), axis=-1, keepdims=True),
            ],
            axis=0,
        )
        log_total = jnp.concatenate([log_ref[0, low_rows], log_ref[1, low_rows]], axis=0)
        scores = lax.dot_general(
            queries, keys[...], CONTRACT_LAST, preferred_element_type=jnp.float32
        )
        probs = jnp.exp(scores - log_total)
        prob_grad = jnp.concatenate(
            [
                lax.dot_general(
                    side_grad, values[...], CONTRACT_LAST, preferred_element_type=jnp.float32
                )
                for side_grad in (grad, above)
            ],
            axis=1,
        )
        score_grad = (probs * (prob_grad - inner)).astype(jnp.bfloat16)
        dv[...] += lax.dot_general(
            probs.astype(jnp.bfloat16), grad, CONTRACT_FIRST, preferred_element_type=jnp.float32
        )
        dk[...] += lax.dot_general(
            score_grad, queries, CONTRACT_FIRST, preferred_element_type=jnp.float32
        )
        query_grad = jnp.dot(score_grad, keys[...], preferred_element_type=jnp.float32)
        dq[low_rows] = query_grad[:128]
        dq[high_rows] = query_grad[128:]

    @pl.loop(0, 4)
    def _(block):
        grad_block(block)

    turn(4)

    @pl.loop(4, 8)
    def _(block):
        grad_block(block)

    turn(3)

    def unrotated(rows):
        both = jnp.where(
            low_lanes(dk[rows]), pltpu.roll(dq[rows] * scaling, 64, 1), dk[rows]
        )
        sined = both * sin_ref[rows]
        lane = lax.rem(lax.broadcasted_iota(jnp.int32, both.shape, 1), 64)
        turned = jnp.where(lane < 32, pltpu.roll(sined, 96, 1), -pltpu.roll(sined, 32, 1))
        return (both * cos_ref[rows] + turned).astype(jnp.bfloat16).reshape(4, 32, 128)

    @pl.loop(0, 8)
    def _(b):
        block = lax.rem(b + me // 4, 8)
        low_rows, high_rows = rows_of(block)
        places = pl.ds(4 * block, 4)
        packed[places, 0:32, :] = unrotated(low_rows)
        packed[places, 32:64, :] = unrotated(high_rows)
        side = pltpu.roll(dv[high_rows], 64, 1)
        value_pair = jnp.where(low_lanes(side), dv[low_rows], side)
        packed[places, 64:96, :] = value_pair.astype(jnp.bfloat16).reshape(4, 32, 128)

        @pl.loop(4 * block, 4 * block + 4)
        def _(to):
            @pl.when(to != me)
            def _():
                back_copy(to).start()

    own = pltpu.make_async_copy(packed.at[me], result.at[me], mine_sem.at[1])
    own.start()
    turn(64)

    @pl.loop(1, 32)
    def _(step):
        back_copy(lax.rem(me + step, 32)).wait()

    own.wait()
    end()


def back_heads(sent, saved, tables, parts, kinds, widths, cuts, scaling, collective_id):
    in_vmem, anywhere = pl.BlockSpec(memory_space=pltpu.VMEM), pl.BlockSpec(memory_space=pl.ANY)
    low, full, rows = jnp.bfloat16, jnp.float32, parts[0].shape[-2]
    result, *outs = pl.pallas_call(
        functools.partial(back_kernel, kinds, cuts, scaling),
        out_shape=[jax.ShapeDtypeStruct((32, 96, 128), low)]
        + [jax.ShapeDtypeStruct((4, rows, width), low) for width in widths],
        in_specs=[in_vmem] * (6 + len(parts)),
        out_specs=[in_vmem] + [anywhere] * len(parts),
        scratch_shapes=[
            pltpu.VMEM((32, 32, 128), low),
            pltpu.VMEM((2048, 128), low),
            pltpu.VMEM((1024, 128), low),
            pltpu.VMEM((2048, 128), full),
            pltpu.VMEM((2048, 128), full),
            pltpu.VMEM((2048, 128), full),
            pltpu.VMEM((32, 96, 128), low),
            *[pltpu.SemaphoreType.DMA((32,))] * 4,
            pltpu.SemaphoreType.DMA((2,)),
            pltpu.SemaphoreType.DMA((3 * sum(cuts),)),
            pltpu.SemaphoreType.DMA((3 * sum(cuts),)),
            pltpu.SemaphoreType.DMA((len(parts),)),
        ],
        compiler_params=pltpu.CompilerParams(
            collective_id=collective_id,
            has_side_effects=True,
            vmem_limit_bytes=56 * 1024 * 1024,
        ),
    )(sent, *saved, *tables, *parts)
    return result, [out.reshape(4 * rows, width) for out, width in zip(outs, widths)]


def by_head_forward(mixed_rows, cos_table, sin_table, scaling):
    seq_count, row_count, _, head_count, head_size = mixed_rows.shape
    ctx_count, fsdp_count = lax.axis_size("ctx"), lax.axis_size("fsdp")
    count = ctx_count * fsdp_count
    queries = rotate(mixed_rows[:, :, 0], cos_table, sin_table).astype(jnp.bfloat16) * scaling
    key_rows = rotate(mixed_rows[:, :, 1], cos_table, sin_table).astype(jnp.bfloat16)
    value_rows = mixed_rows[:, :, 2].astype(jnp.bfloat16)
    to_head = lambda rows: rows.transpose(0, 2, 1, 3).reshape(count, row_count, head_size)
    sent = jnp.concatenate(
        [
            jnp.concatenate([to_head(queries), to_head(key_rows)], axis=-1),
            pack(to_head(value_rows)),
        ],
        axis=1,
    )
    got = exchange(sent, ctx_count, fsdp_count, 1)
    flat = lambda rows: rows.reshape(count * row_count, head_size)
    queries = flat(got[:, :row_count, :head_size])
    key_rows = flat(got[:, :row_count, head_size:])
    value_rows = flat(unpack(got[:, row_count:]))
    context, log_total = attend(queries, key_rows, value_rows, 256)
    back = exchange(
        pack(context.astype(jnp.bfloat16).reshape(count, row_count, head_size)),
        ctx_count,
        fsdp_count,
        2,
    )
    context_low = (
        unpack(back)
        .reshape(seq_count, head_count, row_count, head_size)
        .transpose(0, 2, 1, 3)
        .reshape(seq_count * row_count, head_count * head_size)
    )
    return context_low, (queries, key_rows, value_rows, context, log_total)


def by_head_back(context_grad, saved, scaling, after, planes=()):
    seq_count, row_count, head_count, head_size = context_grad.shape
    ctx_count, fsdp_count = lax.axis_size("ctx"), lax.axis_size("fsdp")
    count = ctx_count * fsdp_count
    if planes:
        sent = pack(context_grad.transpose(0, 2, 1, 3).reshape(count, row_count, head_size))
        order = jnp.arange(count * row_count, dtype=jnp.int32)
        order = order.reshape(count, 2, row_count // 2).transpose(1, 0, 2).reshape(-1)
        tables = [jnp.tile(table[:, 0], (1, 2)) for table in angles(order, head_size)]
        got, lefts = back_heads(sent, saved, tables, *planes, scaling, 2)
        parts = jnp.stack(
            [
                got[:, :row_count, :head_size],
                got[:, :row_count, head_size:],
                unpack(got[:, row_count:]),
            ]
        )
        return (
            parts.reshape(3, seq_count, head_count, row_count, head_size)
            .transpose(1, 3, 0, 2, 4)
            .reshape(seq_count * row_count, 3 * head_count * head_size)
        ), lefts
    queries, key_rows, value_rows, context, log_total = saved
    sent = pack(context_grad.transpose(0, 2, 1, 3).reshape(count, row_count, head_size))
    grad = unpack(exchange(sent, ctx_count, fsdp_count, 3)).reshape(count * row_count, head_size)
    query_grad, key_grad, value_grad = attend_back(
        queries, key_rows, value_rows, context, log_total, grad, 256
    )
    cos_all, sin_all = angles(jnp.arange(count * row_count, dtype=jnp.int32), head_size)
    cos_all, sin_all = cos_all[:, 0], sin_all[:, 0]
    query_pre = unrotate(query_grad * scaling, cos_all, sin_all).astype(jnp.bfloat16)
    key_pre = unrotate(key_grad, cos_all, sin_all).astype(jnp.bfloat16)
    split = lambda rows: rows.reshape(count, row_count, head_size)
    sent = jnp.concatenate(
        [
            jnp.concatenate([split(query_pre), split(key_pre)], axis=-1),
            pack(split(value_grad.astype(jnp.bfloat16))),
        ],
        axis=1,
    )
    if after:
        sent, after = lax.optimization_barrier((sent, after))
    got = exchange(sent, ctx_count, fsdp_count, 4)
    parts = jnp.stack(
        [got[:, :row_count, :head_size], got[:, :row_count, head_size:], unpack(got[:, row_count:])]
    )
    return (
        parts.reshape(3, seq_count, head_count, row_count, head_size)
        .transpose(1, 3, 0, 2, 4)
        .reshape(seq_count * row_count, 3 * head_count * head_size)
    ), after


def by_block_forward(mixed_rows, cos_table, sin_table, scaling):
    seq_count, row_count, _, head_count, head_size = mixed_rows.shape
    width = head_count * head_size
    queries = rotate(mixed_rows[:, :, 0], cos_table, sin_table).astype(jnp.bfloat16)
    key_flat = (
        rotate(mixed_rows[:, :, 1], cos_table, sin_table)
        .astype(jnp.bfloat16)
        .reshape(seq_count, row_count, width)
    )
    value_flat = mixed_rows[:, :, 2].astype(jnp.bfloat16).reshape(seq_count, row_count, width)
    key_block, value_block = (
        lax.all_gather(key_flat, "fsdp", axis=1, tiled=True),
        lax.all_gather(value_flat, "fsdp", axis=1, tiled=True),
    )
    start_state = empty_state(seq_count, head_count, row_count, head_size)
    running_max, denominator, weighted = forward_step(
        queries,
        scaling,
        start_state,
        (
            lax.all_gather(key_block, "ctx", axis=1, tiled=True),
            lax.all_gather(value_block, "ctx", axis=1, tiled=True),
        ),
    )
    context = (weighted / denominator[..., None]).transpose(0, 2, 1, 3)
    log_total = running_max + jnp.log(denominator)
    context_low = context.reshape(seq_count * row_count, width).astype(jnp.bfloat16)
    saved = queries, key_block, value_block, context, log_total, cos_table, sin_table
    return context_low, saved


def by_block_back(context_grad, saved, scaling, after, planes=()):
    seq_count, row_count, head_count, head_size = context_grad.shape
    width = head_count * head_size
    queries, key_block, value_block, context, log_total, cos_table, sin_table = saved
    inner = jnp.sum(context_grad.astype(jnp.float32) * context, axis=-1)
    inner_heads = inner.transpose(0, 2, 1)
    log_rows = log_total.transpose(0, 2, 1)
    query_grad = query_step(
        queries,
        context_grad,
        log_total,
        inner_heads,
        scaling,
        (
            lax.all_gather(key_block, "ctx", axis=1, tiled=True),
            lax.all_gather(value_block, "ctx", axis=1, tiled=True),
        ),
    )
    block_len = key_block.shape[1]
    query_wide = queries.reshape(seq_count, row_count, width).astype(jnp.float32)
    grad_wide = context_grad.reshape(seq_count, row_count, width).astype(jnp.float32)
    key_grad, value_grad = key_step(
        as_heads(key_block, head_size),
        as_heads(value_block, head_size),
        scaling,
        (
            lax.all_gather(query_wide, "ctx", axis=1, tiled=True),
            lax.all_gather(grad_wide, "ctx", axis=1, tiled=True),
            lax.all_gather(log_rows, "ctx", axis=1, tiled=True),
            lax.all_gather(inner, "ctx", axis=1, tiled=True),
        ),
    )
    own = lambda grad: lax.psum_scatter(
        grad.reshape(seq_count, block_len, width), "fsdp", scatter_dimension=1, tiled=True
    ).reshape(seq_count, row_count, head_count, head_size)
    query_pre = unrotate(query_grad * scaling, cos_table, sin_table)
    key_pre = unrotate(own(key_grad) * scaling, cos_table, sin_table)
    return (
        jnp.stack([query_pre, key_pre, own(value_grad)], axis=2)
        .reshape(seq_count * row_count, 3 * width)
        .astype(jnp.bfloat16)
    ), after


def group_rows(rows):
    return lax.all_gather(rows, "fsdp", axis=0, tiled=True)


def group_columns(arrays):
    count = lax.axis_size("fsdp")
    widths = [rows.shape[1] // count for rows in arrays]
    sent = jnp.stack(
        [
            jnp.concatenate(
                [rows[:, f * width : (f + 1) * width] for rows, width in zip(arrays, widths)],
                axis=1,
            )
            for f in range(count)
        ]
    )
    got = lax.all_to_all(sent, "fsdp", split_axis=0, concat_axis=0, tiled=True)
    got = got.reshape(-1, sum(widths))
    edges = [sum(widths[:i]) for i in range(len(widths) + 1)]
    return [got[:, edges[i] : edges[i + 1]] for i in range(len(widths))]


def weight_grad(left, right):
    return jnp.einsum("tw,tf->wf", left, right, preferred_element_type=jnp.float32)


def mesh_place():
    ctx, place = lax.axis_index("ctx"), lax.axis_index("fsdp")
    return ctx // 2, lax.rem(ctx, 2), place // 2, lax.rem(place, 2)


def device_at(z, y, x, core):
    return (2 * z + y, 2 * x + core)


def greet(barrier, devices):
    for device in devices:
        pl.semaphore_signal(barrier, inc=1, device_id=device, device_id_type=MESH_ID)
    pl.semaphore_wait(barrier, len(devices))


def spans(total, count):
    edges = [total * i // (count * 16) * 16 for i in range(count)] + [total]
    return list(zip(edges[:-1], edges[1:]))


def sender(send_sem, recv_sem):
    serial = iter(range(send_sem.shape[0]))

    def send(src, dst, device):
        sem = next(serial)
        copy = pltpu.make_async_remote_copy(
            src_ref=src,
            dst_ref=dst,
            send_sem=send_sem.at[sem],
            recv_sem=recv_sem.at[sem],
            device_id=device,
            device_id_type=MESH_ID,
        )
        copy.start()
        return copy

    return send


def plane_moves(kinds, cuts, ins, outs, send_sem, recv_sem, own_sem):
    z, y, x, core = mesh_place()
    to_x, to_y = device_at(z, y, 1 - x, core), device_at(z, 1 - y, x, core)
    send = sender(send_sem, recv_sem)
    firsts, seconds, owns = [], [], []

    def block(i, index):
        ref, width = ins[i], outs[i].shape[2]
        if len(ref.shape) == 3:
            return ref.at[index]
        step = ref.shape[1] - width
        return ref.at[:, pl.ds(pl.multiple_of(index * step, 128), width)]

    def start():
        for i, kind in enumerate(kinds):
            own = block(i, y if kind else x)
            away = block(i, 1 - y if kind else 1 - x)
            for low, high in spans(outs[i].shape[1], cuts[i]):
                rows = pl.ds(low, high - low)
                by_x = send((own if kind else away).at[rows], outs[i].at[1, rows], to_x)
                by_y = send((away if kind else own).at[rows], outs[i].at[2, rows], to_y)
                firsts.append((i, rows, by_x, by_y))
        for i, kind in enumerate(kinds):
            own = block(i, y if kind else x)
            copy = pltpu.make_async_copy(own, outs[i].at[0], own_sem.at[i])
            copy.start()
            owns.append(copy)

    def turn(count):
        for i, rows, by_x, by_y in firsts[len(seconds) :][:count]:
            if kinds[i]:
                by_y.wait_recv()
                seconds.append(send(outs[i].at[2, rows], outs[i].at[3, rows], to_x))
            else:
                by_x.wait_recv()
                seconds.append(send(outs[i].at[1, rows], outs[i].at[3, rows], to_y))

    def end():
        turn(len(firsts))
        for i, rows, by_x, by_y in firsts:
            (by_x if kinds[i] else by_y).wait_recv()
            by_x.wait_send()
            by_y.wait_send()
        for copy in seconds:
            copy.wait()
        for copy in owns:
            copy.wait()

    return start, turn, end


def plane_kernel(kinds, cuts, *refs):
    count = len(kinds)
    z, y, x, core = mesh_place()
    greet(
        pltpu.get_barrier_semaphore(),
        (device_at(z, y, 1 - x, core), device_at(z, 1 - y, x, core)),
    )
    start, turn, end = plane_moves(
        kinds, cuts, refs[:count], refs[count : 2 * count], *refs[2 * count :]
    )
    start()
    end()


def plane(parts, kinds, widths, cuts, collective_id):
    rows = parts[0].shape[-2]
    sems = 3 * sum(cuts)
    outs = pl.pallas_call(
        functools.partial(plane_kernel, kinds, cuts),
        out_shape=[jax.ShapeDtypeStruct((4, rows, width), jnp.bfloat16) for width in widths],
        in_specs=[pl.BlockSpec(memory_space=pltpu.VMEM)] * len(parts),
        out_specs=[pl.BlockSpec(memory_space=pl.ANY)] * len(parts),
        scratch_shapes=[
            pltpu.SemaphoreType.DMA((sems,)),
            pltpu.SemaphoreType.DMA((sems,)),
            pltpu.SemaphoreType.DMA((len(parts),)),
        ],
        compiler_params=pltpu.CompilerParams(collective_id=collective_id, has_side_effects=True),
    )(*parts)
    return [out.reshape(4 * rows, width) for out, width in zip(outs, widths)]


def finish_kernel(chunks, count, *refs):
    parts, gains = refs[:count], refs[count]
    outs, gain_got = refs[count + 1 : 2 * count + 1], refs[2 * count + 1]
    scratch = refs[2 * count + 2 :]
    core_got, z_got, mid_got, z_sent = (scratch[i * count : (i + 1) * count] for i in range(4))
    send_sem, recv_sem, gain_send, gain_recv, own_sem = scratch[4 * count :]
    z, y, x, core = mesh_place()
    me = lax.axis_index("ctx") * 4 + lax.axis_index("fsdp")
    total = len(chunks)
    barrier = pltpu.get_barrier_semaphore()

    def other(step):
        place = lax.rem(me + step, 32)
        return place, (place // 4, lax.rem(place, 4))

    @pl.loop(1, 32)
    def _(step):
        pl.semaphore_signal(barrier, inc=1, device_id=other(step)[1], device_id_type=MESH_ID)

    pl.semaphore_wait(barrier, 31)

    def send(stage, k, src, dst, device):
        return pltpu.make_async_remote_copy(
            src_ref=src,
            dst_ref=dst,
            send_sem=send_sem.at[stage * total + k],
            recv_sem=recv_sem.at[stage * total + k],
            device_id=device,
            device_id_type=MESH_ID,
        )

    def at(k):
        i, low, high = chunks[k]
        return i, pl.ds(low, high - low)

    def core_copy(k):
        i, rows = at(k)
        return send(
            0, k, parts[i].at[1 - core, rows], core_got[i].at[rows], device_at(z, y, x, 1 - core)
        )

    def inward(k):
        i, rows = at(k)
        return send(
            1, k, z_sent[i].at[rows], z_got[i].at[rows], device_at(1 + z // 2, y, x, core)
        )

    def middle(k):
        i, rows = at(k)
        return send(2, k, z_sent[i].at[rows], mid_got[i].at[rows], device_at(3 - z, y, x, core))

    def outward(k):
        i, rows = at(k)
        here = outs[i].at[y, rows]
        return send(3, k, here, here, device_at(3 * (z // 2), y, x, core))

    def across(k):
        i, rows = at(k)
        here = outs[i].at[y, rows]
        return send(4, k, here, here, device_at(z, 1 - y, x, core))

    def gain_copy(step):
        place, device = other(step)
        return pltpu.make_async_remote_copy(
            src_ref=gains.at[lax.rem(place, 4)],
            dst_ref=gain_got.at[me],
            send_sem=gain_send.at[step],
            recv_sem=gain_recv.at[step],
            device_id=device,
            device_id_type=MESH_ID,
        )

    def wide(value):
        return value.astype(jnp.float32)

    for k in range(total):
        core_copy(k).start()
    own = pltpu.make_async_copy(gains.at[lax.rem(me, 4)], gain_got.at[me], own_sem)
    own.start()

    @pl.loop(1, 32)
    def _(step):
        gain_copy(step).start()

    @pl.when((z == 0) | (z == 3))
    def _():
        for k in range(total):
            i, rows = at(k)
            core_copy(k).wait_recv()
            value = wide(parts[i][core, rows]) + wide(core_got[i][rows])
            z_sent[i][rows] = value.astype(jnp.bfloat16)
            inward(k).start()
        for k in range(total):
            outward(k).wait_recv()
            across(k).start()
        for k in range(total):
            inward(k).wait_send()

    @pl.when((z == 1) | (z == 2))
    def _():
        def meet(k):
            i, rows = at(k)
            middle(k).wait_recv()
            value = wide(z_sent[i][rows]) + wide(mid_got[i][rows])
            outs[i][y, rows] = value.astype(jnp.bfloat16)
            outward(k).start()
            across(k).start()

        for k in range(total):
            i, rows = at(k)
            core_copy(k).wait_recv()
            inward(k).wait_recv()
            value = wide(parts[i][core, rows]) + wide(core_got[i][rows]) + wide(z_got[i][rows])
            z_sent[i][rows] = value.astype(jnp.bfloat16)
            middle(k).start()
            if k > 0:
                meet(k - 1)
        meet(total - 1)
        for k in range(total):
            middle(k).wait_send()
            outward(k).wait_send()

    for k in range(total):
        i, rows = at(k)
        there = outs[i].at[1 - y, rows]
        send(4, k, there, there, device_at(z, 1 - y, x, core)).wait_recv()
        across(k).wait_send()
        core_copy(k).wait_send()
    own.wait()

    @pl.loop(1, 32)
    def _(step):
        gain_copy(step).wait()


def finish(parts, gains, cuts, collective_id):
    chunks = [
        (i, low, high) for i, cut in enumerate(cuts) for low, high in spans(parts[i].shape[1], cut)
    ]
    shapes = [part.shape for part in parts]
    buffers = [pltpu.VMEM(shape[1:], jnp.bfloat16) for shape in shapes]
    in_vmem = pl.BlockSpec(memory_space=pltpu.VMEM)
    return pl.pallas_call(
        functools.partial(finish_kernel, chunks, len(parts)),
        out_shape=[jax.ShapeDtypeStruct(shape, jnp.bfloat16) for shape in shapes]
        + [jax.ShapeDtypeStruct((32, 8, gains.shape[2]), jnp.float32)],
        in_specs=[in_vmem] * (len(parts) + 1),
        out_specs=[in_vmem] * (len(parts) + 1),
        scratch_shapes=buffers * 4
        + [
            pltpu.SemaphoreType.DMA((5 * len(chunks),)),
            pltpu.SemaphoreType.DMA((5 * len(chunks),)),
            pltpu.SemaphoreType.DMA((32,)),
            pltpu.SemaphoreType.DMA((32,)),
            pltpu.SemaphoreType.DMA,
        ],
        compiler_params=pltpu.CompilerParams(
            collective_id=collective_id,
            has_side_effects=True,
            vmem_limit_bytes=48 * 1024 * 1024,
        ),
    )(*parts, gains)


def core_blocks(left, right):
    both = weight_grad(left, right).astype(jnp.bfloat16)
    return both.reshape(2, both.shape[0] // 2, both.shape[1])


def joined_halves(out, full):
    skip = 2 * out.shape[2] - full
    return jnp.concatenate([out[0], out[1][:, skip:]], axis=1).astype(jnp.float32)


def on_device(inputs, attn_gain, attn_proj, attn_out, mlp_gain, mlp_in, mlp_out, cotangent):
    seq_count, row_count, model_width = inputs.shape
    head_size = HEAD_DIM
    head_count = HEADS
    scaling = head_size ** (-0.5)
    fsdp_count = lax.axis_size("fsdp")
    fsdp_place = lax.axis_index("fsdp")
    device_count = lax.axis_size("ctx") * fsdp_count
    one_head_each = device_count == seq_count * head_count
    start_row = (lax.axis_index("ctx") * fsdp_count + fsdp_place) * row_count
    cos_table, sin_table = angles(start_row + jnp.arange(row_count, dtype=jnp.int32), head_size)
    tokens = seq_count * row_count
    gain_width = own_rows = attn_gain.shape[0]
    ctx_count = lax.axis_size("ctx")
    small = one_head_each and fsdp_count == 4 and ctx_count == 8
    states = inputs.astype(jnp.float32)
    attention, attention_back = (
        (by_head_forward, by_head_back) if one_head_each else (by_block_forward, by_block_back)
    )
    if small:
        gain_rows = jnp.concatenate(
            [attn_gain[None], mlp_gain[None], jnp.zeros((14, gain_width), attn_gain.dtype)], axis=0
        )
        normed_low, gains, got, context, log_total, back, *fulls = forward_heads(
            inputs.reshape(tokens, model_width),
            *(
                jnp.tile(table.reshape(row_count, head_size), (seq_count, 2))
                for table in (cos_table, sin_table)
            ),
            gain_rows,
            (attn_proj, attn_out, mlp_in, mlp_out),
            CUTS,
            scaling,
            1,
        )
        saved = got, context, log_total
        context_low = (
            unpack(back)
            .reshape(seq_count, head_count, row_count, head_size)
            .transpose(0, 2, 1, 3)
            .reshape(tokens, head_count * head_size)
        )
        proj_full, out_full, lift_full, down_full = (
            full.reshape(4 * full.shape[1], full.shape[2]) for full in fulls
        )
        gain_one = gains[:, 0, :].reshape(model_width).astype(jnp.float32)
        gain_two = gains[:, 1, :].reshape(model_width).astype(jnp.float32)
        _, norm_back_one = jax.vjp(layer_norm, states, gain_one)
    else:
        gains = lax.all_gather(jnp.stack([attn_gain, mlp_gain]), "fsdp", axis=1, tiled=True)
        gain_one, gain_two = gains.astype(jnp.float32)
        proj_full, out_full, lift_full, down_full = (
            lax.all_gather(rows, "fsdp", axis=0, tiled=True)
            for rows in (attn_proj, attn_out, mlp_in, mlp_out)
        )
        normed, norm_back_one = jax.vjp(layer_norm, states, gain_one)
        normed_low = normed.astype(jnp.bfloat16).reshape(tokens, model_width)
        mixed_rows = jnp.dot(normed_low, proj_full, preferred_element_type=jnp.float32).reshape(
            seq_count, row_count, 3, head_count, head_size
        )
        context_low, saved = attention(mixed_rows, cos_table, sin_table, scaling)
    branch = jnp.dot(context_low, out_full, preferred_element_type=jnp.float32).reshape(
        seq_count, row_count, model_width
    )
    middle = states + branch
    normed_two, norm_back_two = jax.vjp(layer_norm, middle, gain_two)
    normed_two_low = normed_two.astype(jnp.bfloat16).reshape(tokens, model_width)
    lifted = jnp.dot(normed_two_low, lift_full, preferred_element_type=jnp.float32)
    gate_out, gated_back = jax.vjp(gated_unit, lifted)
    gate_low = gate_out.astype(jnp.bfloat16)
    outputs = (
        middle
        + jnp.dot(gate_low, down_full, preferred_element_type=jnp.float32).reshape(
            seq_count, row_count, model_width
        )
    ).astype(jnp.bfloat16)
    seed_rows = cotangent.reshape(tokens, model_width)
    gate_grad = jnp.einsum("td,fd->tf", seed_rows, down_full, preferred_element_type=jnp.float32)
    lifted_grad = gated_back(gate_grad)[0].astype(jnp.bfloat16)
    normed_two_grad = jnp.einsum(
        "tf,wf->tw", lifted_grad, lift_full, preferred_element_type=jnp.float32
    ).reshape(seq_count, row_count, model_width)
    middle_part, gain_two_grad = norm_back_two(normed_two_grad)
    middle_grad = cotangent.astype(jnp.float32) + middle_part
    middle_low = middle_grad.reshape(tokens, model_width).astype(jnp.bfloat16)
    context_grad = (
        jnp.einsum("tv,wv->tw", middle_low, out_full, preferred_element_type=jnp.float32)
        .astype(jnp.bfloat16)
        .reshape(seq_count, row_count, head_count, head_size)
    )
    if small:
        width, lifted_width = model_width // 2, lifted_grad.shape[1]
        hidden = gate_low.shape[1] // 2
        lift_half = -(-lifted_width // 256) * 128
        gate_halves = jnp.stack([gate_low[:, :hidden], gate_low[:, hidden:]])
        planes = (
            (lifted_grad, normed_two_low, gate_halves, context_low, normed_low, seed_rows, middle_low),
            (1, 0, 0, 0, 0, 1, 1),
            (lift_half, width, hidden, width, width, width, width),
            (4, 1, 2, 1, 1, 1, 1),
        )
        mixed_grad, sides = attention_back(context_grad, saved, scaling, (), planes)
        lift_right, normed_two_left, gate_left, context_left, normed_left, seed_right, middle_right = (
            sides
        )
        (mixed_right,) = plane((mixed_grad,), (1,), (mixed_grad.shape[1] // 2,), (4,), 7)
        lift_part = core_blocks(normed_two_left, lift_right)
        down_part = core_blocks(gate_left, seed_right)
        out_part = core_blocks(context_left, middle_right)
        proj_part = core_blocks(normed_left, mixed_right)
    else:
        normed_two_part, gate_part, context_part, normed_part = group_columns(
            (normed_two_low, gate_low, context_low, normed_low)
        )
        seed_group = group_rows(seed_rows)
        joined = group_rows(jnp.concatenate([lifted_grad, middle_low], axis=1))
        lift_grad = weight_grad(normed_two_part, joined[:, : lifted_grad.shape[1]])
        out_grad = weight_grad(context_part, joined[:, lifted_grad.shape[1] :])
        down_grad = weight_grad(gate_part, seed_group)
        first_grads = tuple(grad.astype(jnp.bfloat16) for grad in (lift_grad, down_grad, out_grad))
        mixed_grad, first_grads = attention_back(context_grad, saved, scaling, first_grads)
        mixed_group = group_rows(mixed_grad)
        proj_grad = weight_grad(normed_part, mixed_group).astype(jnp.bfloat16)
        lift_sum, down_sum, out_sum, proj_sum = (
            total.astype(jnp.float32) for total in lax.psum((*first_grads, proj_grad), "ctx")
        )
    normed_grad = jnp.einsum(
        "tm,wm->tw", mixed_grad, proj_full, preferred_element_type=jnp.float32
    ).reshape(seq_count, row_count, model_width)
    state_part, gain_one_grad = norm_back_one(normed_grad)
    input_grad = middle_grad + state_part
    gain_grads = jnp.stack([gain_one_grad, gain_two_grad])
    if small:
        shares = gain_grads.reshape(2, fsdp_count, gain_width).transpose(1, 0, 2)
        shares = jnp.concatenate([shares, jnp.zeros((fsdp_count, 6, gain_width))], axis=1)
        lift_sum, down_sum, out_sum, proj_sum, gain_got = finish(
            (lift_part, down_part, out_part, proj_part), shares, (8, 4, 2, 4), 8
        )
        lift_sum = joined_halves(lift_sum, lifted_width)
        down_sum = joined_halves(down_sum, model_width)
        out_sum = joined_halves(out_sum, model_width)
        proj_sum = joined_halves(proj_sum, mixed_grad.shape[1])
        gain_own = jnp.sum(gain_got, axis=0)
    else:
        gain_sums = lax.psum(gain_grads, ("ctx", "fsdp"))
        gain_own = lax.dynamic_slice_in_dim(gain_sums, fsdp_place * gain_width, gain_width, axis=1)
    return (
        outputs,
        input_grad,
        gain_own[0],
        proj_sum,
        out_sum,
        gain_own[1],
        lift_sum,
        down_sum,
    )


def solution(mesh):
    in_specs = (
        P(None, ("ctx", "fsdp"), None),
        P("fsdp"),
        P("fsdp", None),
        P("fsdp", None),
        P("fsdp"),
        P("fsdp", None),
        P("fsdp", None),
        P(None, ("ctx", "fsdp"), None),
    )
    out_specs = (
        P(None, ("ctx", "fsdp"), None),
        P(None, ("ctx", "fsdp"), None),
        P("fsdp"),
        P("fsdp", None),
        P("fsdp", None),
        P("fsdp"),
        P("fsdp", None),
        P("fsdp", None),
    )
    return jax.shard_map(
        on_device, mesh=mesh, in_specs=in_specs, out_specs=out_specs, check_vma=False
    )
```

```python
import functools

import jax
import jax.numpy as jnp
from jax import lax
from jax.experimental import pallas as pl
from jax.experimental.pallas import tpu as pltpu
from jax.sharding import PartitionSpec as P

HEADS = 16
HEAD_DIM = 64


eps = 1e-05
rope_base = 160000.0


def layer_norm(values, norm_gain):
    center = jnp.mean(values, axis=-1, keepdims=True)
    centred = values - center
    spread = jnp.mean(centred * centred, axis=-1, keepdims=True)
    return centred * lax.rsqrt(spread + eps) * norm_gain


def rotate(values, cos_table, sin_table):
    halfway = values.shape[-1] // 2
    turned = jnp.concatenate([-values[..., halfway:], values[..., :halfway]], axis=-1)
    return values * cos_table + turned * sin_table


def unrotate(gradient, cos_table, sin_table):
    halfway = gradient.shape[-1] // 2
    sined = gradient * sin_table
    return gradient * cos_table + jnp.concatenate(
        [sined[..., halfway:], -sined[..., :halfway]], axis=-1
    )


def angles(positions, head_size):
    exponent = jnp.arange(0, head_size, 2, dtype=jnp.float32) / head_size
    inverse = rope_base ** (-exponent)
    phases = positions.astype(jnp.float32)[:, None] * inverse[None, :]
    phases = jnp.concatenate([phases, phases], axis=-1)
    return (jnp.cos(phases)[:, None, :], jnp.sin(phases)[:, None, :])


def gated_unit(lifted):
    hidden_units = lifted.shape[-1] // 2
    return jax.nn.gelu(lifted[..., :hidden_units], approximate=False) * lifted[..., hidden_units:]


def as_heads(flat_rows, head_size):
    return flat_rows.reshape(flat_rows.shape[0], flat_rows.shape[1], -1, head_size)


def empty_state(seq_count, head_count, query_rows, head_size):
    return (
        jnp.full((seq_count, head_count, query_rows), -jnp.inf, jnp.float32),
        jnp.zeros((seq_count, head_count, query_rows), jnp.float32),
        jnp.zeros((seq_count, head_count, query_rows, head_size), jnp.float32),
    )


def forward_step(queries, scaling, state_now, shard_part):
    running_max, denominator, weighted = state_now
    key_part = as_heads(shard_part[0], queries.shape[3])
    value_part = as_heads(shard_part[1], queries.shape[3])
    scores = (
        jnp.einsum("sqhd,skhd->shqk", queries, key_part, preferred_element_type=jnp.float32)
        * scaling
    )
    new_max = jnp.max(scores, axis=-1)
    fading = jnp.exp(running_max - new_max)
    weights = jnp.exp(scores - new_max[..., None])
    denominator = denominator * fading + jnp.sum(weights, axis=-1)
    weighted = weighted * fading[..., None] + jnp.einsum(
        "shqk,skhd->shqd",
        weights.astype(jnp.bfloat16),
        value_part,
        preferred_element_type=jnp.float32,
    )
    return (new_max, denominator, weighted)


def query_step(queries, grad_out, log_total, inner_heads, scaling, shard_part):
    key_part = as_heads(shard_part[0], queries.shape[3])
    value_part = as_heads(shard_part[1], queries.shape[3])
    scores = (
        jnp.einsum("sqhd,skhd->shqk", queries, key_part, preferred_element_type=jnp.float32)
        * scaling
    )
    weights = jnp.exp(scores - log_total[..., None])
    weight_grad = jnp.einsum(
        "sqhd,skhd->shqk", grad_out, value_part, preferred_element_type=jnp.float32
    )
    score_grad = (weights * (weight_grad - inner_heads[..., None])).astype(jnp.bfloat16)
    return jnp.einsum("shqk,skhd->sqhd", score_grad, key_part, preferred_element_type=jnp.float32)


def key_step(key_heads, value_heads, scaling, shard_part):
    head_size = key_heads.shape[3]
    query_part = as_heads(shard_part[0].astype(jnp.bfloat16), head_size)
    grad_part = as_heads(shard_part[1].astype(jnp.bfloat16), head_size)
    log_part = shard_part[2].transpose(0, 2, 1)
    inner_part = shard_part[3].transpose(0, 2, 1)
    scores = (
        jnp.einsum("sqhd,skhd->shqk", query_part, key_heads, preferred_element_type=jnp.float32)
        * scaling
    )
    weights = jnp.exp(scores - log_part[..., None])
    value_grad = jnp.einsum(
        "shqk,sqhd->skhd",
        weights.astype(jnp.bfloat16),
        grad_part,
        preferred_element_type=jnp.float32,
    )
    weight_grad = jnp.einsum(
        "sqhd,skhd->shqk", grad_part, value_heads, preferred_element_type=jnp.float32
    )
    score_grad = (weights * (weight_grad - inner_part[..., None])).astype(jnp.bfloat16)
    key_grad = jnp.einsum(
        "shqk,sqhd->skhd", score_grad, query_part, preferred_element_type=jnp.float32
    )
    return (key_grad, value_grad)


MESH_ID = pl.DeviceIdType.MESH


def exchange_kernel(ctx_count, fsdp_count, x_ref, o_ref, send_sem, recv_sem, own_sem):
    count = ctx_count * fsdp_count
    me = lax.axis_index("ctx") * fsdp_count + lax.axis_index("fsdp")
    barrier = pltpu.get_barrier_semaphore()

    def target(step):
        place = lax.rem(me + step, count)
        return place, (place // fsdp_count, lax.rem(place, fsdp_count))

    def copy_to(step):
        place, device = target(step)
        return pltpu.make_async_remote_copy(
            src_ref=x_ref.at[place],
            dst_ref=o_ref.at[me],
            send_sem=send_sem.at[step],
            recv_sem=recv_sem.at[step],
            device_id=device,
            device_id_type=MESH_ID,
        )

    @pl.loop(1, count)
    def _(step):
        pl.semaphore_signal(barrier, inc=1, device_id=target(step)[1], device_id_type=MESH_ID)

    pl.semaphore_wait(barrier, count - 1)
    own = pltpu.make_async_copy(x_ref.at[me], o_ref.at[me], own_sem)
    own.start()

    @pl.loop(1, count)
    def _(step):
        copy_to(step).start()

    own.wait()

    @pl.loop(1, count)
    def _(step):
        copy_to(step).wait()


def exchange(blocks, ctx_count, fsdp_count, collective_id):
    count = ctx_count * fsdp_count
    return pl.pallas_call(
        functools.partial(exchange_kernel, ctx_count, fsdp_count),
        out_shape=jax.ShapeDtypeStruct(blocks.shape, blocks.dtype),
        in_specs=[pl.BlockSpec(memory_space=pl.ANY)],
        out_specs=pl.BlockSpec(memory_space=pl.ANY),
        scratch_shapes=[
            pltpu.SemaphoreType.DMA((count,)),
            pltpu.SemaphoreType.DMA((count,)),
            pltpu.SemaphoreType.DMA,
        ],
        compiler_params=pltpu.CompilerParams(collective_id=collective_id, has_side_effects=True),
    )(blocks)


def pack(blocks):
    half = blocks.shape[-2] // 2
    return jnp.concatenate([blocks[..., :half, :], blocks[..., half:, :]], axis=-1)


def unpack(blocks):
    half = blocks.shape[-1] // 2
    return jnp.concatenate([blocks[..., :half], blocks[..., half:]], axis=-2)


AHEAD = 3
LAG = 6
CUTS = ((False, 6), (False, 1), (True, 4), (False, 4))
CONTRACT_LAST = (((1,), (1,)), ((), ()))
CONTRACT_FIRST = (((0,), (0,)), ((), ()))


def attend_kernel(q_ref, k_ref, v_ref, context_ref, log_ref):
    scores = lax.dot_general(
        q_ref[...], k_ref[...], CONTRACT_LAST, preferred_element_type=jnp.float32
    )
    top = jnp.max(scores, axis=-1, keepdims=True)
    weights = jnp.exp(scores - top)
    total = jnp.sum(weights, axis=-1, keepdims=True)
    weighted = jnp.dot(
        weights.astype(jnp.bfloat16), v_ref[...], preferred_element_type=jnp.float32
    )
    context_ref[...] = weighted / total
    log_ref[...] = top + jnp.log(total)


def attend(queries, key_rows, value_rows, block):
    rows, size = queries.shape
    return pl.pallas_call(
        attend_kernel,
        grid=(rows // block,),
        out_shape=(
            jax.ShapeDtypeStruct((rows, size), jnp.float32),
            jax.ShapeDtypeStruct((rows, 1), jnp.float32),
        ),
        in_specs=[
            pl.BlockSpec((block, size), lambda i: (i, 0)),
            pl.BlockSpec((rows, size), lambda i: (0, 0)),
            pl.BlockSpec((rows, size), lambda i: (0, 0)),
        ],
        out_specs=(
            pl.BlockSpec((block, size), lambda i: (i, 0)),
            pl.BlockSpec((block, 1), lambda i: (i, 0)),
        ),
        compiler_params=pltpu.CompilerParams(vmem_limit_bytes=48 * 1024 * 1024),
    )(queries, key_rows, value_rows)


def attend_back_kernel(
    q_ref, k_ref, v_ref, context_ref, log_ref, grad_ref, dq_ref, dk_ref, dv_ref
):
    @pl.when(pl.program_id(0) == 0)
    def _():
        dk_ref[...] = jnp.zeros_like(dk_ref)
        dv_ref[...] = jnp.zeros_like(dv_ref)

    grad = grad_ref[...]
    inner = jnp.sum(grad.astype(jnp.float32) * context_ref[...], axis=-1, keepdims=True)
    scores = lax.dot_general(
        q_ref[...], k_ref[...], CONTRACT_LAST, preferred_element_type=jnp.float32
    )
    probs = jnp.exp(scores - log_ref[...])
    prob_grad = lax.dot_general(
        grad, v_ref[...], CONTRACT_LAST, preferred_element_type=jnp.float32
    )
    score_grad = (probs * (prob_grad - inner)).astype(jnp.bfloat16)
    dv_ref[...] += lax.dot_general(
        probs.astype(jnp.bfloat16), grad, CONTRACT_FIRST, preferred_element_type=jnp.float32
    )
    dk_ref[...] += lax.dot_general(
        score_grad, q_ref[...], CONTRACT_FIRST, preferred_element_type=jnp.float32
    )
    dq_ref[...] = jnp.dot(score_grad, k_ref[...], preferred_element_type=jnp.float32)


def attend_back(queries, key_rows, value_rows, context, log_total, grad, block):
    rows, size = queries.shape
    part = pl.BlockSpec((block, size), lambda i: (i, 0))
    whole = pl.BlockSpec((rows, size), lambda i: (0, 0))
    return pl.pallas_call(
        attend_back_kernel,
        grid=(rows // block,),
        out_shape=(jax.ShapeDtypeStruct((rows, size), jnp.float32),) * 3,
        in_specs=[
            part,
            whole,
            whole,
            part,
            pl.BlockSpec((block, 1), lambda i: (i, 0)),
            part,
        ],
        out_specs=(part, whole, whole),
        compiler_params=pltpu.CompilerParams(vmem_limit_bytes=48 * 1024 * 1024),
    )(queries, key_rows, value_rows, context, log_total, grad)


def whole_mesh(me):
    def other(step):
        place = lax.rem(me + step, 32)
        return place, (place // 4, lax.rem(place, 4))

    return other


def greet_all(other):
    barrier = pltpu.get_barrier_semaphore()

    @pl.loop(1, 32)
    def _(step):
        pl.semaphore_signal(barrier, inc=1, device_id=other(step)[1], device_id_type=MESH_ID)

    pl.semaphore_wait(barrier, 31)


def swap_lanes(value):
    return pltpu.roll(value.astype(jnp.float32), 64, 1)


def low_lanes(value):
    return lax.broadcasted_iota(jnp.int32, value.shape, 1) < 64


def weight_piece(ref, by_rows, half, index, count):
    if by_rows:
        size = ref.shape[0] // (2 * count)
        start = pl.multiple_of((half * count + index) * size, 16)
        return ref.at[pl.ds(start, size), :]
    size = ref.shape[1] // (2 * count)
    start = pl.multiple_of((half * count + index) * size, 128)
    return ref.at[:, pl.ds(start, size)]


def forward_kernel(cuts, scaling, *refs):
    count = len(cuts)
    x_ref, cos_ref, sin_ref, gain_ref = refs[:4]
    shards = refs[4 : 4 + count]
    normed_ref, gains, got, context, log_ref, back = refs[4 + count : 10 + count]
    fulls = refs[10 + count : 10 + 2 * count]
    (sent, keys, values, packed, head_send, head_recv, back_send, back_recv, own_sem) = refs[
        10 + 2 * count : 19 + 2 * count
    ]
    w_send, w_recv = refs[19 + 2 * count :]
    targets, proj = fulls, fulls[0]
    z, y, x, core = mesh_place()
    place = 2 * x + core
    me = 4 * (2 * z + y) + place
    across = lax.rem(place + 2, 4)
    other = whole_mesh(me)
    sibling, partner = device_at(z, y, x, 1 - core), device_at(z, y, 1 - x, core)
    corner = device_at(z, y, 1 - x, 1 - core)
    neighbour = device_at(z, 1 - y, x, core)
    greet_all(other)

    def head_copy(step):
        to, device = other(step)
        return pltpu.make_async_remote_copy(
            src_ref=sent.at[to],
            dst_ref=got.at[me],
            send_sem=head_send.at[step],
            recv_sem=head_recv.at[step],
            device_id=device,
            device_id_type=MESH_ID,
        )

    def back_copy(to):
        step = lax.rem(to - me + 32, 32)
        return pltpu.make_async_remote_copy(
            src_ref=packed.at[to],
            dst_ref=back.at[me],
            send_sem=back_send.at[step],
            recv_sem=back_recv.at[step],
            device_id=(to // 4, lax.rem(to, 4)),
            device_id_type=MESH_ID,
        )

    send = sender(w_send, w_recv)
    crossing, handed, turned = [], [], []

    todo = [(i, c) for i in range(count) for c in range(cuts[i][1])]
    first = cuts[0][1]

    def cross(pieces=1):
        for i, c in todo[len(crossing) :][:pieces]:
            src = weight_piece(shards[i], cuts[i][0], y, c, cuts[i][1])
            dst = weight_piece(targets[i].at[place], cuts[i][0], y, c, cuts[i][1])
            crossing.append((i, c, send(src, dst, partner)))

    def keep(i):
        copy = pltpu.make_async_copy(shards[i], targets[i].at[place], own_sem.at[i])
        copy.start()
        return copy

    def turn(entry):
        i, c, copy = entry
        copy.wait_recv()
        here = weight_piece(targets[i].at[across], cuts[i][0], y, c, cuts[i][1])
        turned.append((i, c, send(here, here, neighbour)))
        cross()
        handed.append(send(here, here, sibling))

    def hand(entry):
        i, c, copy = entry
        copy.wait_recv()
        here = weight_piece(targets[i].at[across], cuts[i][0], 1 - y, c, cuts[i][1])
        handed.append(send(here, here, sibling))

    gain_moves = [
        send(gain_ref, gains.at[place], device) for device in (sibling, partner, corner)
    ]
    cross(AHEAD)
    handed.append(send(shards[0], proj.at[place], sibling))
    kept = pltpu.make_async_copy(gain_ref, gains.at[place], own_sem.at[count])
    kept.start()
    owns = [keep(0)]
    states = x_ref[...].astype(jnp.float32)
    centred = states - jnp.mean(states, axis=-1, keepdims=True)
    spread = jnp.mean(centred * centred, axis=-1, keepdims=True)
    centred = centred * lax.rsqrt(spread + eps)
    kept.wait()
    for copy in gain_moves:
        copy.wait()
    for f in range(4):
        part = centred[:, f * 256 : (f + 1) * 256] * gains[f, 0:1, :].astype(jnp.float32)
        normed_ref[:, f * 256 : (f + 1) * 256] = part.astype(jnp.bfloat16)
    for c in range(first):
        turn(crossing[c])
    for c in range(first):
        hand(turned[c])
    owns[0].wait()
    for copy in handed[: 1 + 2 * first]:
        copy.wait_recv()
    cos = jnp.concatenate([cos_ref[...]] * 2, axis=1)
    sin = jnp.concatenate([sin_ref[...]] * 2, axis=1)

    def turn_heads(value):
        lane = lax.rem(lax.broadcasted_iota(jnp.int32, value.shape, 1), 64)
        turned_lanes = jnp.where(lane < 32, -pltpu.roll(value, 224, 1), pltpu.roll(value, 32, 1))
        return value * cos + turned_lanes * sin

    @pl.loop(0, 4)
    def _(quad):
        def product(start):
            columns = pl.ds(pl.multiple_of(start + quad * 256, 128), 256)
            total = jnp.dot(
                normed_ref[:, :256], proj[0, :, columns], preferred_element_type=jnp.float32
            )
            for f in range(1, 4):
                total += jnp.dot(
                    normed_ref[:, f * 256 : (f + 1) * 256],
                    proj[f, :, columns],
                    preferred_element_type=jnp.float32,
                )
            return total

        queries = turn_heads(product(0)).astype(jnp.bfloat16).astype(jnp.float32) * scaling
        key_rows = turn_heads(product(1024))
        value_rows = product(2048)
        for pair in range(2):
            lanes = slice(pair * 128, (pair + 1) * 128)
            q, k, v = queries[:, lanes], key_rows[:, lanes], value_rows[:, lanes]
            swapped_q, swapped_k = pltpu.roll(q, 64, 1), pltpu.roll(k, 64, 1)
            even = jnp.where(low_lanes(q), q, swapped_k).astype(jnp.bfloat16)
            odd = jnp.where(low_lanes(q), swapped_q, k).astype(jnp.bfloat16)
            swapped_v = pltpu.roll(v, 64, 1)
            for seq in range(2):
                head = seq * 16 + quad * 4 + pair * 2
                low, mid, high = seq * 64, seq * 64 + 32, seq * 64 + 64
                sent[head, 0:64] = even[low:high]
                sent[head + 1, 0:64] = odd[low:high]
                mask = low_lanes(v[low:mid])
                sent[head, 64:96] = jnp.where(mask, v[low:mid], swapped_v[mid:high]).astype(
                    jnp.bfloat16
                )
                sent[head + 1, 64:96] = jnp.where(mask, swapped_v[low:mid], v[mid:high]).astype(
                    jnp.bfloat16
                )

    @pl.loop(1, 32)
    def _(step):
        head_copy(step).start()

    own_head = pltpu.make_async_copy(sent.at[me], got.at[me], own_sem.at[count + 1])
    own_head.start()
    for i in range(1, count):
        owns.append(keep(i))
        handed.append(send(shards[i], targets[i].at[place], sibling))
    for c in range(first, first + 3):
        turn(crossing[c])
    hand(turned[first])
    own_head.wait()

    @pl.loop(1, 32)
    def _(step):
        head_copy(step).wait()

    keys[0:1024] = got[:, 0:32, :].reshape(1024, 128)
    keys[1024:2048] = got[:, 32:64, :].reshape(1024, 128)
    values[...] = got[:, 64:96, :].reshape(1024, 128)

    def attend_block(b):
        block = lax.rem(b + me // 4, 8)
        low_rows = pl.ds(pl.multiple_of(block * 128, 128), 128)
        high_rows = pl.ds(pl.multiple_of(1024 + block * 128, 128), 128)
        queries = swap_lanes(jnp.concatenate([keys[low_rows], keys[high_rows]], axis=0))
        queries = jnp.where(low_lanes(queries), 0.0, queries).astype(jnp.bfloat16)
        scores = lax.dot_general(
            queries, keys[...], CONTRACT_LAST, preferred_element_type=jnp.float32
        )
        top = jnp.max(scores, axis=-1, keepdims=True)
        weights = jnp.exp(scores - top)
        total = jnp.sum(weights, axis=-1, keepdims=True)
        weights = weights.astype(jnp.bfloat16)
        first = jnp.dot(weights[:, :1024], values[...], preferred_element_type=jnp.float32)
        second = jnp.dot(weights[:, 1024:], values[...], preferred_element_type=jnp.float32)
        outcome = (first + pltpu.roll(second, 64, 1)) / total
        side = pltpu.roll(outcome[128:], 64, 1)
        outcome = jnp.where(low_lanes(side), outcome[:128], side)
        context[low_rows] = outcome
        log_total = top + jnp.log(total)
        log_ref[0, low_rows] = log_total[:128]
        log_ref[1, low_rows] = log_total[128:]
        packed[pl.ds(4 * block, 4)] = outcome.astype(jnp.bfloat16).reshape(4, 32, 128)

        @pl.loop(4 * block, 4 * block + 4)
        def _(to):
            @pl.when(to != me)
            def _():
                back_copy(to).start()

    turn(crossing[first + 3])
    hand(turned[first + 1])

    @pl.loop(0, 4)
    def _(b):
        attend_block(b)

    turn(crossing[first + 4])
    hand(turned[first + 2])

    @pl.loop(4, 8)
    def _(b):
        attend_block(b)

    mine = pltpu.make_async_copy(packed.at[me], back.at[me], own_sem.at[count + 2])
    mine.start()
    owns.append(mine)
    for index in range(first + 5, len(todo)):
        turn(crossing[index])
        hand(turned[index - 2])
    hand(turned[-2])
    hand(turned[-1])

    @pl.loop(1, 32)
    def _(step):
        back_copy(lax.rem(me + step, 32)).wait()

    for copy in handed[1 + 2 * first :]:
        copy.wait_recv()
    for copy in handed:
        copy.wait_send()
    for _, _, copy in crossing + turned:
        copy.wait_send()
    for copy in owns[1:]:
        copy.wait()


def forward_heads(rows, cos_table, sin_table, gain, shards, cuts, scaling, collective_id):
    in_vmem, anywhere = pl.BlockSpec(memory_space=pltpu.VMEM), pl.BlockSpec(memory_space=pl.ANY)
    copies = 3 + len(shards) + sum(4 * pieces for _, pieces in cuts)
    low, full = jnp.bfloat16, jnp.float32
    sems = [pltpu.SemaphoreType.DMA((32,))] * 4
    proj, *rest = shards
    return pl.pallas_call(
        functools.partial(forward_kernel, cuts, scaling),
        out_shape=[
            jax.ShapeDtypeStruct(rows.shape, low),
            jax.ShapeDtypeStruct((4, *gain.shape), low),
            jax.ShapeDtypeStruct((32, 96, 128), low),
            jax.ShapeDtypeStruct((1024, 128), full),
            jax.ShapeDtypeStruct((2, 1024, 1), full),
            jax.ShapeDtypeStruct((32, 32, 128), low),
        ]
        + [jax.ShapeDtypeStruct((4, *shard.shape), low) for shard in shards],
        in_specs=[in_vmem] * (4 + len(shards)),
        out_specs=[in_vmem] * 7 + [anywhere] * len(rest),
        scratch_shapes=[
            pltpu.VMEM((32, 96, 128), low),
            pltpu.VMEM((2048, 128), low),
            pltpu.VMEM((1024, 128), low),
            pltpu.VMEM((32, 32, 128), low),
            *sems,
            pltpu.SemaphoreType.DMA((len(shards) + 3,)),
            pltpu.SemaphoreType.DMA((copies,)),
            pltpu.SemaphoreType.DMA((copies,)),
        ],
        compiler_params=pltpu.CompilerParams(
            collective_id=collective_id,
            has_side_effects=True,
            vmem_limit_bytes=56 * 1024 * 1024,
        ),
    )(rows, cos_table, sin_table, gain, *shards)


def back_kernel(kinds, cuts, scaling, *refs):
    count = len(kinds)
    sent, got, context, log_ref, cos_ref, sin_ref = refs[:6]
    parts, result = refs[6 : 6 + count], refs[6 + count]
    outs = refs[7 + count : 7 + 2 * count]
    (grads, keys, values, dq, dk, dv, packed, go_send, go_recv, back_send, back_recv, mine_sem) = refs[
        7 + 2 * count : 19 + 2 * count
    ]
    me = lax.axis_index("ctx") * 4 + lax.axis_index("fsdp")
    other = whole_mesh(me)
    greet_all(other)

    def go_copy(step):
        to, device = other(step)
        return pltpu.make_async_remote_copy(
            src_ref=sent.at[to],
            dst_ref=grads.at[me],
            send_sem=go_send.at[step],
            recv_sem=go_recv.at[step],
            device_id=device,
            device_id_type=MESH_ID,
        )

    def back_copy(to):
        step = lax.rem(to - me + 32, 32)
        return pltpu.make_async_remote_copy(
            src_ref=packed.at[to],
            dst_ref=result.at[me],
            send_sem=back_send.at[step],
            recv_sem=back_recv.at[step],
            device_id=(to // 4, lax.rem(to, 4)),
            device_id_type=MESH_ID,
        )

    @pl.loop(1, 32)
    def _(step):
        go_copy(step).start()

    mine = pltpu.make_async_copy(sent.at[me], grads.at[me], mine_sem.at[0])
    mine.start()
    start, turn, end = plane_moves(kinds, cuts, parts, outs, *refs[19 + 2 * count :])
    start()
    keys[0:1024] = got[:, 0:32, :].reshape(1024, 128)
    keys[1024:2048] = got[:, 32:64, :].reshape(1024, 128)
    values[...] = got[:, 64:96, :].reshape(1024, 128)
    dk[...] = jnp.zeros_like(dk)
    dv[...] = jnp.zeros_like(dv)
    mine.wait()

    @pl.loop(1, 32)
    def _(step):
        go_copy(step).wait()

    def rows_of(block):
        return (
            pl.ds(pl.multiple_of(block * 128, 128), 128),
            pl.ds(pl.multiple_of(1024 + block * 128, 128), 128),
        )

    def grad_block(block):
        low_rows, high_rows = rows_of(block)
        queries = swap_lanes(jnp.concatenate([keys[low_rows], keys[high_rows]], axis=0))
        queries = jnp.where(low_lanes(queries), 0.0, queries).astype(jnp.bfloat16)
        pair = grads[pl.ds(4 * block, 4)].reshape(128, 128).astype(jnp.float32)
        side = pltpu.roll(pair, 64, 1)
        first = low_lanes(pair)
        grad = jnp.concatenate([jnp.where(first, pair, 0.0), jnp.where(first, side, 0.0)], axis=0)
        above = jnp.concatenate([jnp.where(first, 0.0, side), jnp.where(first, 0.0, pair)], axis=0)
        grad, above = grad.astype(jnp.bfloat16), above.astype(jnp.bfloat16)
        product = pair * context[low_rows]
        inner = jnp.concatenate(
            [
                jnp.sum(jnp.where(first, product, 0.0), axis=-1, keepdims=True),
                jnp.sum(jnp.where(first, 0.0, product), axis=-1, keepdims=True),
            ],
            axis=0,
        )
        log_total = jnp.concatenate([log_ref[0, low_rows], log_ref[1, low_rows]], axis=0)
        scores = lax.dot_general(
            queries, keys[...], CONTRACT_LAST, preferred_element_type=jnp.float32
        )
        probs = jnp.exp(scores - log_total)
        prob_grad = jnp.concatenate(
            [
                lax.dot_general(
                    side_grad, values[...], CONTRACT_LAST, preferred_element_type=jnp.float32
                )
                for side_grad in (grad, above)
            ],
            axis=1,
        )
        score_grad = (probs * (prob_grad - inner)).astype(jnp.bfloat16)
        dv[...] += lax.dot_general(
            probs.astype(jnp.bfloat16), grad, CONTRACT_FIRST, preferred_element_type=jnp.float32
        )
        dk[...] += lax.dot_general(
            score_grad, queries, CONTRACT_FIRST, preferred_element_type=jnp.float32
        )
        query_grad = jnp.dot(score_grad, keys[...], preferred_element_type=jnp.float32)
        dq[low_rows] = query_grad[:128]
        dq[high_rows] = query_grad[128:]

    @pl.loop(0, 4)
    def _(block):
        grad_block(block)

    turn(4)

    @pl.loop(4, 8)
    def _(block):
        grad_block(block)

    turn(3)

    def unrotated(rows):
        both = jnp.where(
            low_lanes(dk[rows]), pltpu.roll(dq[rows] * scaling, 64, 1), dk[rows]
        )
        sined = both * sin_ref[rows]
        lane = lax.rem(lax.broadcasted_iota(jnp.int32, both.shape, 1), 64)
        turned = jnp.where(lane < 32, pltpu.roll(sined, 96, 1), -pltpu.roll(sined, 32, 1))
        return (both * cos_ref[rows] + turned).astype(jnp.bfloat16).reshape(4, 32, 128)

    @pl.loop(0, 8)
    def _(b):
        block = lax.rem(b + me // 4, 8)
        low_rows, high_rows = rows_of(block)
        places = pl.ds(4 * block, 4)
        packed[places, 0:32, :] = unrotated(low_rows)
        packed[places, 32:64, :] = unrotated(high_rows)
        side = pltpu.roll(dv[high_rows], 64, 1)
        value_pair = jnp.where(low_lanes(side), dv[low_rows], side)
        packed[places, 64:96, :] = value_pair.astype(jnp.bfloat16).reshape(4, 32, 128)

        @pl.loop(4 * block, 4 * block + 4)
        def _(to):
            @pl.when(to != me)
            def _():
                back_copy(to).start()

    own = pltpu.make_async_copy(packed.at[me], result.at[me], mine_sem.at[1])
    own.start()
    turn(64)

    @pl.loop(1, 32)
    def _(step):
        back_copy(lax.rem(me + step, 32)).wait()

    own.wait()
    end()


def back_heads(sent, saved, tables, parts, kinds, widths, cuts, scaling, collective_id):
    in_vmem, anywhere = pl.BlockSpec(memory_space=pltpu.VMEM), pl.BlockSpec(memory_space=pl.ANY)
    low, full, rows = jnp.bfloat16, jnp.float32, parts[0].shape[-2]
    result, *outs = pl.pallas_call(
        functools.partial(back_kernel, kinds, cuts, scaling),
        out_shape=[jax.ShapeDtypeStruct((32, 96, 128), low)]
        + [jax.ShapeDtypeStruct((4, rows, width), low) for width in widths],
        in_specs=[in_vmem] * (6 + len(parts)),
        out_specs=[in_vmem] + [anywhere] * len(parts),
        scratch_shapes=[
            pltpu.VMEM((32, 32, 128), low),
            pltpu.VMEM((2048, 128), low),
            pltpu.VMEM((1024, 128), low),
            pltpu.VMEM((2048, 128), full),
            pltpu.VMEM((2048, 128), full),
            pltpu.VMEM((2048, 128), full),
            pltpu.VMEM((32, 96, 128), low),
            *[pltpu.SemaphoreType.DMA((32,))] * 4,
            pltpu.SemaphoreType.DMA((2,)),
            pltpu.SemaphoreType.DMA((3 * sum(cuts),)),
            pltpu.SemaphoreType.DMA((3 * sum(cuts),)),
            pltpu.SemaphoreType.DMA((len(parts),)),
        ],
        compiler_params=pltpu.CompilerParams(
            collective_id=collective_id,
            has_side_effects=True,
            vmem_limit_bytes=56 * 1024 * 1024,
        ),
    )(sent, *saved, *tables, *parts)
    return result, [out.reshape(4 * rows, width) for out, width in zip(outs, widths)]


def by_head_forward(mixed_rows, cos_table, sin_table, scaling):
    seq_count, row_count, _, head_count, head_size = mixed_rows.shape
    ctx_count, fsdp_count = lax.axis_size("ctx"), lax.axis_size("fsdp")
    count = ctx_count * fsdp_count
    queries = rotate(mixed_rows[:, :, 0], cos_table, sin_table).astype(jnp.bfloat16) * scaling
    key_rows = rotate(mixed_rows[:, :, 1], cos_table, sin_table).astype(jnp.bfloat16)
    value_rows = mixed_rows[:, :, 2].astype(jnp.bfloat16)
    to_head = lambda rows: rows.transpose(0, 2, 1, 3).reshape(count, row_count, head_size)
    sent = jnp.concatenate(
        [
            jnp.concatenate([to_head(queries), to_head(key_rows)], axis=-1),
            pack(to_head(value_rows)),
        ],
        axis=1,
    )
    got = exchange(sent, ctx_count, fsdp_count, 1)
    flat = lambda rows: rows.reshape(count * row_count, head_size)
    queries = flat(got[:, :row_count, :head_size])
    key_rows = flat(got[:, :row_count, head_size:])
    value_rows = flat(unpack(got[:, row_count:]))
    context, log_total = attend(queries, key_rows, value_rows, 256)
    back = exchange(
        pack(context.astype(jnp.bfloat16).reshape(count, row_count, head_size)),
        ctx_count,
        fsdp_count,
        2,
    )
    context_low = (
        unpack(back)
        .reshape(seq_count, head_count, row_count, head_size)
        .transpose(0, 2, 1, 3)
        .reshape(seq_count * row_count, head_count * head_size)
    )
    return context_low, (queries, key_rows, value_rows, context, log_total)


def by_head_back(context_grad, saved, scaling, after, planes=()):
    seq_count, row_count, head_count, head_size = context_grad.shape
    ctx_count, fsdp_count = lax.axis_size("ctx"), lax.axis_size("fsdp")
    count = ctx_count * fsdp_count
    if planes:
        sent = pack(context_grad.transpose(0, 2, 1, 3).reshape(count, row_count, head_size))
        order = jnp.arange(count * row_count, dtype=jnp.int32)
        order = order.reshape(count, 2, row_count // 2).transpose(1, 0, 2).reshape(-1)
        tables = [jnp.tile(table[:, 0], (1, 2)) for table in angles(order, head_size)]
        got, lefts = back_heads(sent, saved, tables, *planes, scaling, 2)
        parts = jnp.stack(
            [
                got[:, :row_count, :head_size],
                got[:, :row_count, head_size:],
                unpack(got[:, row_count:]),
            ]
        )
        return (
            parts.reshape(3, seq_count, head_count, row_count, head_size)
            .transpose(1, 3, 0, 2, 4)
            .reshape(seq_count * row_count, 3 * head_count * head_size)
        ), lefts
    queries, key_rows, value_rows, context, log_total = saved
    sent = pack(context_grad.transpose(0, 2, 1, 3).reshape(count, row_count, head_size))
    grad = unpack(exchange(sent, ctx_count, fsdp_count, 3)).reshape(count * row_count, head_size)
    query_grad, key_grad, value_grad = attend_back(
        queries, key_rows, value_rows, context, log_total, grad, 256
    )
    cos_all, sin_all = angles(jnp.arange(count * row_count, dtype=jnp.int32), head_size)
    cos_all, sin_all = cos_all[:, 0], sin_all[:, 0]
    query_pre = unrotate(query_grad * scaling, cos_all, sin_all).astype(jnp.bfloat16)
    key_pre = unrotate(key_grad, cos_all, sin_all).astype(jnp.bfloat16)
    split = lambda rows: rows.reshape(count, row_count, head_size)
    sent = jnp.concatenate(
        [
            jnp.concatenate([split(query_pre), split(key_pre)], axis=-1),
            pack(split(value_grad.astype(jnp.bfloat16))),
        ],
        axis=1,
    )
    if after:
        sent, after = lax.optimization_barrier((sent, after))
    got = exchange(sent, ctx_count, fsdp_count, 4)
    parts = jnp.stack(
        [got[:, :row_count, :head_size], got[:, :row_count, head_size:], unpack(got[:, row_count:])]
    )
    return (
        parts.reshape(3, seq_count, head_count, row_count, head_size)
        .transpose(1, 3, 0, 2, 4)
        .reshape(seq_count * row_count, 3 * head_count * head_size)
    ), after


def by_block_forward(mixed_rows, cos_table, sin_table, scaling):
    seq_count, row_count, _, head_count, head_size = mixed_rows.shape
    width = head_count * head_size
    queries = rotate(mixed_rows[:, :, 0], cos_table, sin_table).astype(jnp.bfloat16)
    key_flat = (
        rotate(mixed_rows[:, :, 1], cos_table, sin_table)
        .astype(jnp.bfloat16)
        .reshape(seq_count, row_count, width)
    )
    value_flat = mixed_rows[:, :, 2].astype(jnp.bfloat16).reshape(seq_count, row_count, width)
    key_block, value_block = (
        lax.all_gather(key_flat, "fsdp", axis=1, tiled=True),
        lax.all_gather(value_flat, "fsdp", axis=1, tiled=True),
    )
    start_state = empty_state(seq_count, head_count, row_count, head_size)
    running_max, denominator, weighted = forward_step(
        queries,
        scaling,
        start_state,
        (
            lax.all_gather(key_block, "ctx", axis=1, tiled=True),
            lax.all_gather(value_block, "ctx", axis=1, tiled=True),
        ),
    )
    context = (weighted / denominator[..., None]).transpose(0, 2, 1, 3)
    log_total = running_max + jnp.log(denominator)
    context_low = context.reshape(seq_count * row_count, width).astype(jnp.bfloat16)
    saved = queries, key_block, value_block, context, log_total, cos_table, sin_table
    return context_low, saved


def by_block_back(context_grad, saved, scaling, after, planes=()):
    seq_count, row_count, head_count, head_size = context_grad.shape
    width = head_count * head_size
    queries, key_block, value_block, context, log_total, cos_table, sin_table = saved
    inner = jnp.sum(context_grad.astype(jnp.float32) * context, axis=-1)
    inner_heads = inner.transpose(0, 2, 1)
    log_rows = log_total.transpose(0, 2, 1)
    query_grad = query_step(
        queries,
        context_grad,
        log_total,
        inner_heads,
        scaling,
        (
            lax.all_gather(key_block, "ctx", axis=1, tiled=True),
            lax.all_gather(value_block, "ctx", axis=1, tiled=True),
        ),
    )
    block_len = key_block.shape[1]
    query_wide = queries.reshape(seq_count, row_count, width).astype(jnp.float32)
    grad_wide = context_grad.reshape(seq_count, row_count, width).astype(jnp.float32)
    key_grad, value_grad = key_step(
        as_heads(key_block, head_size),
        as_heads(value_block, head_size),
        scaling,
        (
            lax.all_gather(query_wide, "ctx", axis=1, tiled=True),
            lax.all_gather(grad_wide, "ctx", axis=1, tiled=True),
            lax.all_gather(log_rows, "ctx", axis=1, tiled=True),
            lax.all_gather(inner, "ctx", axis=1, tiled=True),
        ),
    )
    own = lambda grad: lax.psum_scatter(
        grad.reshape(seq_count, block_len, width), "fsdp", scatter_dimension=1, tiled=True
    ).reshape(seq_count, row_count, head_count, head_size)
    query_pre = unrotate(query_grad * scaling, cos_table, sin_table)
    key_pre = unrotate(own(key_grad) * scaling, cos_table, sin_table)
    return (
        jnp.stack([query_pre, key_pre, own(value_grad)], axis=2)
        .reshape(seq_count * row_count, 3 * width)
        .astype(jnp.bfloat16)
    ), after


def group_rows(rows):
    return lax.all_gather(rows, "fsdp", axis=0, tiled=True)


def group_columns(arrays):
    count = lax.axis_size("fsdp")
    widths = [rows.shape[1] // count for rows in arrays]
    sent = jnp.stack(
        [
            jnp.concatenate(
                [rows[:, f * width : (f + 1) * width] for rows, width in zip(arrays, widths)],
                axis=1,
            )
            for f in range(count)
        ]
    )
    got = lax.all_to_all(sent, "fsdp", split_axis=0, concat_axis=0, tiled=True)
    got = got.reshape(-1, sum(widths))
    edges = [sum(widths[:i]) for i in range(len(widths) + 1)]
    return [got[:, edges[i] : edges[i + 1]] for i in range(len(widths))]


def weight_grad(left, right):
    return jnp.einsum("tw,tf->wf", left, right, preferred_element_type=jnp.float32)


def mesh_place():
    ctx, place = lax.axis_index("ctx"), lax.axis_index("fsdp")
    return ctx // 2, lax.rem(ctx, 2), place // 2, lax.rem(place, 2)


def device_at(z, y, x, core):
    return (2 * z + y, 2 * x + core)


def greet(barrier, devices):
    for device in devices:
        pl.semaphore_signal(barrier, inc=1, device_id=device, device_id_type=MESH_ID)
    pl.semaphore_wait(barrier, len(devices))


def spans(total, count):
    edges = [total * i // (count * 16) * 16 for i in range(count)] + [total]
    return list(zip(edges[:-1], edges[1:]))


def sender(send_sem, recv_sem):
    serial = iter(range(send_sem.shape[0]))

    def send(src, dst, device):
        sem = next(serial)
        copy = pltpu.make_async_remote_copy(
            src_ref=src,
            dst_ref=dst,
            send_sem=send_sem.at[sem],
            recv_sem=recv_sem.at[sem],
            device_id=device,
            device_id_type=MESH_ID,
        )
        copy.start()
        return copy

    return send


def plane_moves(kinds, cuts, ins, outs, send_sem, recv_sem, own_sem):
    z, y, x, core = mesh_place()
    to_x, to_y = device_at(z, y, 1 - x, core), device_at(z, 1 - y, x, core)
    send = sender(send_sem, recv_sem)
    firsts, seconds, owns = [], [], []

    def block(i, index):
        ref, width = ins[i], outs[i].shape[2]
        if len(ref.shape) == 3:
            return ref.at[index]
        step = ref.shape[1] - width
        return ref.at[:, pl.ds(pl.multiple_of(index * step, 128), width)]

    def start():
        for i, kind in enumerate(kinds):
            own = block(i, y if kind else x)
            away = block(i, 1 - y if kind else 1 - x)
            for low, high in spans(outs[i].shape[1], cuts[i]):
                rows = pl.ds(low, high - low)
                by_x = send((own if kind else away).at[rows], outs[i].at[1, rows], to_x)
                by_y = send((away if kind else own).at[rows], outs[i].at[2, rows], to_y)
                firsts.append((i, rows, by_x, by_y))
        for i, kind in enumerate(kinds):
            own = block(i, y if kind else x)
            copy = pltpu.make_async_copy(own, outs[i].at[0], own_sem.at[i])
            copy.start()
            owns.append(copy)

    def turn(count):
        for i, rows, by_x, by_y in firsts[len(seconds) :][:count]:
            if kinds[i]:
                by_y.wait_recv()
                seconds.append(send(outs[i].at[2, rows], outs[i].at[3, rows], to_x))
            else:
                by_x.wait_recv()
                seconds.append(send(outs[i].at[1, rows], outs[i].at[3, rows], to_y))

    def end():
        turn(len(firsts))
        for i, rows, by_x, by_y in firsts:
            (by_x if kinds[i] else by_y).wait_recv()
            by_x.wait_send()
            by_y.wait_send()
        for copy in seconds:
            copy.wait()
        for copy in owns:
            copy.wait()

    return start, turn, end


def finish_kernel(chunks, count, *refs):
    mixed, left, gains = refs[count - 1 : count + 2]
    outs, gain_got = refs[count + 2 : 2 * count + 2], refs[2 * count + 2]
    scratch = refs[2 * count + 3 :]
    core_got, z_got, mid_got, z_sent = (scratch[i * count : (i + 1) * count] for i in range(4))
    send_sem, recv_sem, gain_send, gain_recv, own_sem, last, right = scratch[
        4 * count : 4 * count + 7
    ]
    parts = (*refs[: count - 1], last)
    z, y, x, core = mesh_place()
    me = lax.axis_index("ctx") * 4 + lax.axis_index("fsdp")
    total = len(chunks)
    barrier = pltpu.get_barrier_semaphore()

    def other(step):
        place = lax.rem(me + step, 32)
        return place, (place // 4, lax.rem(place, 4))

    @pl.loop(1, 32)
    def _(step):
        pl.semaphore_signal(barrier, inc=1, device_id=other(step)[1], device_id_type=MESH_ID)

    pl.semaphore_wait(barrier, 31)

    def send(stage, k, src, dst, device):
        return pltpu.make_async_remote_copy(
            src_ref=src,
            dst_ref=dst,
            send_sem=send_sem.at[stage * total + k],
            recv_sem=recv_sem.at[stage * total + k],
            device_id=device,
            device_id_type=MESH_ID,
        )

    def at(k):
        i, low, high = chunks[k]
        return i, pl.ds(low, high - low)

    def core_copy(k):
        i, rows = at(k)
        return send(
            0, k, parts[i].at[1 - core, rows], core_got[i].at[rows], device_at(z, y, x, 1 - core)
        )

    def inward(k):
        i, rows = at(k)
        return send(
            1, k, z_sent[i].at[rows], z_got[i].at[rows], device_at(1 + z // 2, y, x, core)
        )

    def middle(k):
        i, rows = at(k)
        return send(2, k, z_sent[i].at[rows], mid_got[i].at[rows], device_at(3 - z, y, x, core))

    def outward(k):
        i, rows = at(k)
        here = outs[i].at[y, rows]
        return send(3, k, here, here, device_at(3 * (z // 2), y, x, core))

    def across(k):
        i, rows = at(k)
        here = outs[i].at[y, rows]
        return send(4, k, here, here, device_at(z, 1 - y, x, core))

    def gain_copy(step):
        place, device = other(step)
        return pltpu.make_async_remote_copy(
            src_ref=gains.at[lax.rem(place, 4)],
            dst_ref=gain_got.at[me],
            send_sem=gain_send.at[step],
            recv_sem=gain_recv.at[step],
            device_id=device,
            device_id_type=MESH_ID,
        )

    def wide(value):
        return value.astype(jnp.float32)

    outer = (z == 0) | (z == 3)
    late = [k for k in range(total) if chunks[k][0] == count - 1][0]
    start, turn, end = plane_moves((1,), (4,), (mixed,), (right,), *scratch[4 * count + 7 :])
    for k in range(AHEAD):
        core_copy(k).start()
    start()
    own = pltpu.make_async_copy(gains.at[lax.rem(me, 4)], gain_got.at[me], own_sem)
    own.start()

    @pl.loop(1, 32)
    def _(step):
        gain_copy(step).start()

    def meet(k):
        @pl.when(outer)
        def _():
            if k >= LAG:
                outward(k - LAG).wait_recv()
                across(k - LAG).start()

        if k < 1 or k > total:
            return
        i, rows = at(k - 1)

        @pl.when(jnp.logical_not(outer))
        def _():
            middle(k - 1).wait_recv()
            value = wide(z_sent[i][rows]) + wide(mid_got[i][rows])
            outs[i][y, rows] = value.astype(jnp.bfloat16)
            outward(k - 1).start()
            across(k - 1).start()

    for k in range(total):
        i, rows = at(k)
        if 2 <= k < 6:
            turn(1)
        if k == late - AHEAD:
            end()
            for half in range(2):
                block = left[0:128, half * 256 : (half + 1) * 256]
                value = lax.dot_general(
                    block, right[0], CONTRACT_FIRST, preferred_element_type=jnp.float32
                )
                for source in range(1, 4):
                    block = left[source * 128 : (source + 1) * 128, half * 256 : (half + 1) * 256]
                    value += lax.dot_general(
                        block, right[source], CONTRACT_FIRST, preferred_element_type=jnp.float32
                    )
                last[half] = value.astype(jnp.bfloat16)
        if k + AHEAD < total:
            core_copy(k + AHEAD).start()
        core_copy(k).wait_recv()
        value = wide(parts[i][core, rows]) + wide(core_got[i][rows])

        @pl.when(outer)
        def _():
            z_sent[i][rows] = value.astype(jnp.bfloat16)
            inward(k).start()

        @pl.when(jnp.logical_not(outer))
        def _():
            inward(k).wait_recv()
            z_sent[i][rows] = (value + wide(z_got[i][rows])).astype(jnp.bfloat16)
            middle(k).start()

        meet(k)

    for k in range(total, total + LAG):
        if k > total:

            @pl.when(outer)
            def _():
                outward(k - LAG).wait_recv()
                across(k - LAG).start()
        else:
            meet(k)

    @pl.when(outer)
    def _():
        for k in range(total):
            inward(k).wait_send()

    @pl.when(jnp.logical_not(outer))
    def _():
        for k in range(total):
            middle(k).wait_send()
            outward(k).wait_send()

    for k in range(total):
        i, rows = at(k)
        there = outs[i].at[1 - y, rows]
        send(4, k, there, there, device_at(z, 1 - y, x, core)).wait_recv()
        across(k).wait_send()
        core_copy(k).wait_send()
    own.wait()

    @pl.loop(1, 32)
    def _(step):
        gain_copy(step).wait()


def finish(parts, mixed, left, gains, cuts, collective_id):
    tokens, width = mixed.shape
    shapes = [part.shape for part in parts]
    shapes.append((2, left.shape[1] // 2, width // 2))
    count = len(shapes)
    chunks = [
        (i, low, high) for i, cut in enumerate(cuts) for low, high in spans(shapes[i][1], cut)
    ]
    buffers = [pltpu.VMEM(shape[1:], jnp.bfloat16) for shape in shapes]
    in_vmem = pl.BlockSpec(memory_space=pltpu.VMEM)
    return pl.pallas_call(
        functools.partial(finish_kernel, chunks, count),
        out_shape=[jax.ShapeDtypeStruct(shape, jnp.bfloat16) for shape in shapes]
        + [jax.ShapeDtypeStruct((32, 8, gains.shape[2]), jnp.float32)],
        in_specs=[in_vmem] * (count + 2),
        out_specs=[in_vmem] * (count + 1),
        scratch_shapes=buffers * 4
        + [
            pltpu.SemaphoreType.DMA((5 * len(chunks),)),
            pltpu.SemaphoreType.DMA((5 * len(chunks),)),
            pltpu.SemaphoreType.DMA((32,)),
            pltpu.SemaphoreType.DMA((32,)),
            pltpu.SemaphoreType.DMA,
            pltpu.VMEM(shapes[-1], jnp.bfloat16),
            pltpu.VMEM((4, tokens, width // 2), jnp.bfloat16),
            pltpu.SemaphoreType.DMA((12,)),
            pltpu.SemaphoreType.DMA((12,)),
            pltpu.SemaphoreType.DMA((1,)),
        ],
        compiler_params=pltpu.CompilerParams(
            collective_id=collective_id,
            has_side_effects=True,
            vmem_limit_bytes=56 * 1024 * 1024,
        ),
    )(*parts, mixed, left, gains)


def core_blocks(left, right):
    both = weight_grad(left, right).astype(jnp.bfloat16)
    return both.reshape(2, both.shape[0] // 2, both.shape[1])


def joined_halves(out, full):
    skip = 2 * out.shape[2] - full
    return jnp.concatenate([out[0], out[1][:, skip:]], axis=1).astype(jnp.float32)


def on_device(inputs, attn_gain, attn_proj, attn_out, mlp_gain, mlp_in, mlp_out, cotangent):
    seq_count, row_count, model_width = inputs.shape
    head_size = HEAD_DIM
    head_count = HEADS
    scaling = head_size ** (-0.5)
    fsdp_count = lax.axis_size("fsdp")
    fsdp_place = lax.axis_index("fsdp")
    device_count = lax.axis_size("ctx") * fsdp_count
    one_head_each = device_count == seq_count * head_count
    start_row = (lax.axis_index("ctx") * fsdp_count + fsdp_place) * row_count
    cos_table, sin_table = angles(start_row + jnp.arange(row_count, dtype=jnp.int32), head_size)
    tokens = seq_count * row_count
    gain_width = own_rows = attn_gain.shape[0]
    ctx_count = lax.axis_size("ctx")
    small = one_head_each and fsdp_count == 4 and ctx_count == 8
    states = inputs.astype(jnp.float32)
    attention, attention_back = (
        (by_head_forward, by_head_back) if one_head_each else (by_block_forward, by_block_back)
    )
    if small:
        gain_rows = jnp.concatenate(
            [attn_gain[None], mlp_gain[None], jnp.zeros((14, gain_width), attn_gain.dtype)], axis=0
        )
        normed_low, gains, got, context, log_total, back, *fulls = forward_heads(
            inputs.reshape(tokens, model_width),
            *(
                jnp.tile(table.reshape(row_count, head_size), (seq_count, 2))
                for table in (cos_table, sin_table)
            ),
            gain_rows,
            (attn_proj, attn_out, mlp_in, mlp_out),
            CUTS,
            scaling,
            1,
        )
        saved = got, context, log_total
        context_low = (
            unpack(back)
            .reshape(seq_count, head_count, row_count, head_size)
            .transpose(0, 2, 1, 3)
            .reshape(tokens, head_count * head_size)
        )
        proj_full, out_full, lift_full, down_full = (
            full.reshape(4 * full.shape[1], full.shape[2]) for full in fulls
        )
        gain_one = gains[:, 0, :].reshape(model_width).astype(jnp.float32)
        gain_two = gains[:, 1, :].reshape(model_width).astype(jnp.float32)
        _, norm_back_one = jax.vjp(layer_norm, states, gain_one)
    else:
        gains = lax.all_gather(jnp.stack([attn_gain, mlp_gain]), "fsdp", axis=1, tiled=True)
        gain_one, gain_two = gains.astype(jnp.float32)
        proj_full, out_full, lift_full, down_full = (
            lax.all_gather(rows, "fsdp", axis=0, tiled=True)
            for rows in (attn_proj, attn_out, mlp_in, mlp_out)
        )
        normed, norm_back_one = jax.vjp(layer_norm, states, gain_one)
        normed_low = normed.astype(jnp.bfloat16).reshape(tokens, model_width)
        mixed_rows = jnp.dot(normed_low, proj_full, preferred_element_type=jnp.float32).reshape(
            seq_count, row_count, 3, head_count, head_size
        )
        context_low, saved = attention(mixed_rows, cos_table, sin_table, scaling)
    branch = jnp.dot(context_low, out_full, preferred_element_type=jnp.float32).reshape(
        seq_count, row_count, model_width
    )
    middle = states + branch
    normed_two, norm_back_two = jax.vjp(layer_norm, middle, gain_two)
    normed_two_low = normed_two.astype(jnp.bfloat16).reshape(tokens, model_width)
    lifted = jnp.dot(normed_two_low, lift_full, preferred_element_type=jnp.float32)
    gate_out, gated_back = jax.vjp(gated_unit, lifted)
    gate_low = gate_out.astype(jnp.bfloat16)
    outputs = (
        middle
        + jnp.dot(gate_low, down_full, preferred_element_type=jnp.float32).reshape(
            seq_count, row_count, model_width
        )
    ).astype(jnp.bfloat16)
    seed_rows = cotangent.reshape(tokens, model_width)
    gate_grad = jnp.einsum("td,fd->tf", seed_rows, down_full, preferred_element_type=jnp.float32)
    lifted_grad = gated_back(gate_grad)[0].astype(jnp.bfloat16)
    normed_two_grad = jnp.einsum(
        "tf,wf->tw", lifted_grad, lift_full, preferred_element_type=jnp.float32
    ).reshape(seq_count, row_count, model_width)
    middle_part, gain_two_grad = norm_back_two(normed_two_grad)
    middle_grad = cotangent.astype(jnp.float32) + middle_part
    middle_low = middle_grad.reshape(tokens, model_width).astype(jnp.bfloat16)
    context_grad = (
        jnp.einsum("tv,wv->tw", middle_low, out_full, preferred_element_type=jnp.float32)
        .astype(jnp.bfloat16)
        .reshape(seq_count, row_count, head_count, head_size)
    )
    if small:
        width, lifted_width = model_width // 2, lifted_grad.shape[1]
        hidden = gate_low.shape[1] // 2
        lift_half = -(-lifted_width // 256) * 128
        gate_halves = jnp.stack([gate_low[:, :hidden], gate_low[:, hidden:]])
        planes = (
            (lifted_grad, normed_two_low, gate_halves, context_low, normed_low, seed_rows, middle_low),
            (1, 0, 0, 0, 0, 1, 1),
            (lift_half, width, hidden, width, width, width, width),
            (4, 1, 2, 1, 1, 1, 1),
        )
        mixed_grad, sides = attention_back(context_grad, saved, scaling, (), planes)
        lift_right, normed_two_left, gate_left, context_left, normed_left, seed_right, middle_right = (
            sides
        )
        lift_part = core_blocks(normed_two_left, lift_right)
        down_part = core_blocks(gate_left, seed_right)
        out_part = core_blocks(context_left, middle_right)
    else:
        normed_two_part, gate_part, context_part, normed_part = group_columns(
            (normed_two_low, gate_low, context_low, normed_low)
        )
        seed_group = group_rows(seed_rows)
        joined = group_rows(jnp.concatenate([lifted_grad, middle_low], axis=1))
        lift_grad = weight_grad(normed_two_part, joined[:, : lifted_grad.shape[1]])
        out_grad = weight_grad(context_part, joined[:, lifted_grad.shape[1] :])
        down_grad = weight_grad(gate_part, seed_group)
        first_grads = tuple(grad.astype(jnp.bfloat16) for grad in (lift_grad, down_grad, out_grad))
        mixed_grad, first_grads = attention_back(context_grad, saved, scaling, first_grads)
        mixed_group = group_rows(mixed_grad)
        proj_grad = weight_grad(normed_part, mixed_group).astype(jnp.bfloat16)
        lift_sum, down_sum, out_sum, proj_sum = (
            total.astype(jnp.float32) for total in lax.psum((*first_grads, proj_grad), "ctx")
        )
    normed_grad = jnp.einsum(
        "tm,wm->tw", mixed_grad, proj_full, preferred_element_type=jnp.float32
    ).reshape(seq_count, row_count, model_width)
    state_part, gain_one_grad = norm_back_one(normed_grad)
    input_grad = middle_grad + state_part
    gain_grads = jnp.stack([gain_one_grad, gain_two_grad])
    if small:
        shares = gain_grads.reshape(2, fsdp_count, gain_width).transpose(1, 0, 2)
        shares = jnp.concatenate([shares, jnp.zeros((fsdp_count, 6, gain_width))], axis=1)
        lift_sum, down_sum, out_sum, proj_sum, gain_got = finish(
            (lift_part, down_part, out_part), mixed_grad, normed_left, shares, (8, 4, 2, 4), 8
        )
        lift_sum = joined_halves(lift_sum, lifted_width)
        down_sum = joined_halves(down_sum, model_width)
        out_sum = joined_halves(out_sum, model_width)
        proj_sum = joined_halves(proj_sum, mixed_grad.shape[1])
        gain_own = jnp.sum(gain_got, axis=0)
    else:
        gain_sums = lax.psum(gain_grads, ("ctx", "fsdp"))
        gain_own = lax.dynamic_slice_in_dim(gain_sums, fsdp_place * gain_width, gain_width, axis=1)
    return (
        outputs,
        input_grad,
        gain_own[0],
        proj_sum,
        out_sum,
        gain_own[1],
        lift_sum,
        down_sum,
    )


def solution(mesh):
    in_specs = (
        P(None, ("ctx", "fsdp"), None),
        P("fsdp"),
        P("fsdp", None),
        P("fsdp", None),
        P("fsdp"),
        P("fsdp", None),
        P("fsdp", None),
        P(None, ("ctx", "fsdp"), None),
    )
    out_specs = (
        P(None, ("ctx", "fsdp"), None),
        P(None, ("ctx", "fsdp"), None),
        P("fsdp"),
        P("fsdp", None),
        P("fsdp", None),
        P("fsdp"),
        P("fsdp", None),
        P("fsdp", None),
    )
    return jax.shard_map(
        on_device, mesh=mesh, in_specs=in_specs, out_specs=out_specs, check_vma=False
    )
```

```python
import functools

import jax
import jax.numpy as jnp
from jax import lax
from jax.experimental import pallas as pl
from jax.experimental.pallas import tpu as pltpu
from jax.sharding import PartitionSpec as P

HEADS = 16
HEAD_DIM = 64


eps = 1e-05
rope_base = 160000.0


def layer_norm(values, norm_gain):
    center = jnp.mean(values, axis=-1, keepdims=True)
    centred = values - center
    spread = jnp.mean(centred * centred, axis=-1, keepdims=True)
    return centred * lax.rsqrt(spread + eps) * norm_gain


def rotate(values, cos_table, sin_table):
    halfway = values.shape[-1] // 2
    turned = jnp.concatenate([-values[..., halfway:], values[..., :halfway]], axis=-1)
    return values * cos_table + turned * sin_table


def unrotate(gradient, cos_table, sin_table):
    halfway = gradient.shape[-1] // 2
    sined = gradient * sin_table
    return gradient * cos_table + jnp.concatenate(
        [sined[..., halfway:], -sined[..., :halfway]], axis=-1
    )


def angles(positions, head_size):
    exponent = jnp.arange(0, head_size, 2, dtype=jnp.float32) / head_size
    inverse = rope_base ** (-exponent)
    phases = positions.astype(jnp.float32)[:, None] * inverse[None, :]
    phases = jnp.concatenate([phases, phases], axis=-1)
    return (jnp.cos(phases)[:, None, :], jnp.sin(phases)[:, None, :])


def gated_unit(lifted):
    hidden_units = lifted.shape[-1] // 2
    return jax.nn.gelu(lifted[..., :hidden_units], approximate=False) * lifted[..., hidden_units:]


def as_heads(flat_rows, head_size):
    return flat_rows.reshape(flat_rows.shape[0], flat_rows.shape[1], -1, head_size)


def empty_state(seq_count, head_count, query_rows, head_size):
    return (
        jnp.full((seq_count, head_count, query_rows), -jnp.inf, jnp.float32),
        jnp.zeros((seq_count, head_count, query_rows), jnp.float32),
        jnp.zeros((seq_count, head_count, query_rows, head_size), jnp.float32),
    )


def forward_step(queries, scaling, state_now, shard_part):
    running_max, denominator, weighted = state_now
    key_part = as_heads(shard_part[0], queries.shape[3])
    value_part = as_heads(shard_part[1], queries.shape[3])
    scores = (
        jnp.einsum("sqhd,skhd->shqk", queries, key_part, preferred_element_type=jnp.float32)
        * scaling
    )
    new_max = jnp.max(scores, axis=-1)
    fading = jnp.exp(running_max - new_max)
    weights = jnp.exp(scores - new_max[..., None])
    denominator = denominator * fading + jnp.sum(weights, axis=-1)
    weighted = weighted * fading[..., None] + jnp.einsum(
        "shqk,skhd->shqd",
        weights.astype(jnp.bfloat16),
        value_part,
        preferred_element_type=jnp.float32,
    )
    return (new_max, denominator, weighted)


def query_step(queries, grad_out, log_total, inner_heads, scaling, shard_part):
    key_part = as_heads(shard_part[0], queries.shape[3])
    value_part = as_heads(shard_part[1], queries.shape[3])
    scores = (
        jnp.einsum("sqhd,skhd->shqk", queries, key_part, preferred_element_type=jnp.float32)
        * scaling
    )
    weights = jnp.exp(scores - log_total[..., None])
    weight_grad = jnp.einsum(
        "sqhd,skhd->shqk", grad_out, value_part, preferred_element_type=jnp.float32
    )
    score_grad = (weights * (weight_grad - inner_heads[..., None])).astype(jnp.bfloat16)
    return jnp.einsum("shqk,skhd->sqhd", score_grad, key_part, preferred_element_type=jnp.float32)


def key_step(key_heads, value_heads, scaling, shard_part):
    head_size = key_heads.shape[3]
    query_part = as_heads(shard_part[0].astype(jnp.bfloat16), head_size)
    grad_part = as_heads(shard_part[1].astype(jnp.bfloat16), head_size)
    log_part = shard_part[2].transpose(0, 2, 1)
    inner_part = shard_part[3].transpose(0, 2, 1)
    scores = (
        jnp.einsum("sqhd,skhd->shqk", query_part, key_heads, preferred_element_type=jnp.float32)
        * scaling
    )
    weights = jnp.exp(scores - log_part[..., None])
    value_grad = jnp.einsum(
        "shqk,sqhd->skhd",
        weights.astype(jnp.bfloat16),
        grad_part,
        preferred_element_type=jnp.float32,
    )
    weight_grad = jnp.einsum(
        "sqhd,skhd->shqk", grad_part, value_heads, preferred_element_type=jnp.float32
    )
    score_grad = (weights * (weight_grad - inner_part[..., None])).astype(jnp.bfloat16)
    key_grad = jnp.einsum(
        "shqk,sqhd->skhd", score_grad, query_part, preferred_element_type=jnp.float32
    )
    return (key_grad, value_grad)


MESH_ID = pl.DeviceIdType.MESH


def exchange_kernel(ctx_count, fsdp_count, x_ref, o_ref, send_sem, recv_sem, own_sem):
    count = ctx_count * fsdp_count
    me = lax.axis_index("ctx") * fsdp_count + lax.axis_index("fsdp")
    barrier = pltpu.get_barrier_semaphore()

    def target(step):
        place = lax.rem(me + step, count)
        return place, (place // fsdp_count, lax.rem(place, fsdp_count))

    def copy_to(step):
        place, device = target(step)
        return pltpu.make_async_remote_copy(
            src_ref=x_ref.at[place],
            dst_ref=o_ref.at[me],
            send_sem=send_sem.at[step],
            recv_sem=recv_sem.at[step],
            device_id=device,
            device_id_type=MESH_ID,
        )

    @pl.loop(1, count)
    def _(step):
        pl.semaphore_signal(barrier, inc=1, device_id=target(step)[1], device_id_type=MESH_ID)

    pl.semaphore_wait(barrier, count - 1)
    own = pltpu.make_async_copy(x_ref.at[me], o_ref.at[me], own_sem)
    own.start()

    @pl.loop(1, count)
    def _(step):
        copy_to(step).start()

    own.wait()

    @pl.loop(1, count)
    def _(step):
        copy_to(step).wait()


def exchange(blocks, ctx_count, fsdp_count, collective_id):
    count = ctx_count * fsdp_count
    return pl.pallas_call(
        functools.partial(exchange_kernel, ctx_count, fsdp_count),
        out_shape=jax.ShapeDtypeStruct(blocks.shape, blocks.dtype),
        in_specs=[pl.BlockSpec(memory_space=pl.ANY)],
        out_specs=pl.BlockSpec(memory_space=pl.ANY),
        scratch_shapes=[
            pltpu.SemaphoreType.DMA((count,)),
            pltpu.SemaphoreType.DMA((count,)),
            pltpu.SemaphoreType.DMA,
        ],
        compiler_params=pltpu.CompilerParams(collective_id=collective_id, has_side_effects=True),
    )(blocks)


def pack(blocks):
    half = blocks.shape[-2] // 2
    return jnp.concatenate([blocks[..., :half, :], blocks[..., half:, :]], axis=-1)


def unpack(blocks):
    half = blocks.shape[-1] // 2
    return jnp.concatenate([blocks[..., :half], blocks[..., half:]], axis=-2)


AHEAD = 3
LAG = 6
CUTS = ((False, 6), (False, 1), (True, 4), (False, 4))
CONTRACT_LAST = (((1,), (1,)), ((), ()))
CONTRACT_FIRST = (((0,), (0,)), ((), ()))


def attend_kernel(q_ref, k_ref, v_ref, context_ref, log_ref):
    scores = lax.dot_general(
        q_ref[...], k_ref[...], CONTRACT_LAST, preferred_element_type=jnp.float32
    )
    top = jnp.max(scores, axis=-1, keepdims=True)
    weights = jnp.exp(scores - top)
    total = jnp.sum(weights, axis=-1, keepdims=True)
    weighted = jnp.dot(
        weights.astype(jnp.bfloat16), v_ref[...], preferred_element_type=jnp.float32
    )
    context_ref[...] = weighted / total
    log_ref[...] = top + jnp.log(total)


def attend(queries, key_rows, value_rows, block):
    rows, size = queries.shape
    return pl.pallas_call(
        attend_kernel,
        grid=(rows // block,),
        out_shape=(
            jax.ShapeDtypeStruct((rows, size), jnp.float32),
            jax.ShapeDtypeStruct((rows, 1), jnp.float32),
        ),
        in_specs=[
            pl.BlockSpec((block, size), lambda i: (i, 0)),
            pl.BlockSpec((rows, size), lambda i: (0, 0)),
            pl.BlockSpec((rows, size), lambda i: (0, 0)),
        ],
        out_specs=(
            pl.BlockSpec((block, size), lambda i: (i, 0)),
            pl.BlockSpec((block, 1), lambda i: (i, 0)),
        ),
        compiler_params=pltpu.CompilerParams(vmem_limit_bytes=48 * 1024 * 1024),
    )(queries, key_rows, value_rows)


def attend_back_kernel(
    q_ref, k_ref, v_ref, context_ref, log_ref, grad_ref, dq_ref, dk_ref, dv_ref
):
    @pl.when(pl.program_id(0) == 0)
    def _():
        dk_ref[...] = jnp.zeros_like(dk_ref)
        dv_ref[...] = jnp.zeros_like(dv_ref)

    grad = grad_ref[...]
    inner = jnp.sum(grad.astype(jnp.float32) * context_ref[...], axis=-1, keepdims=True)
    scores = lax.dot_general(
        q_ref[...], k_ref[...], CONTRACT_LAST, preferred_element_type=jnp.float32
    )
    probs = jnp.exp(scores - log_ref[...])
    prob_grad = lax.dot_general(
        grad, v_ref[...], CONTRACT_LAST, preferred_element_type=jnp.float32
    )
    score_grad = (probs * (prob_grad - inner)).astype(jnp.bfloat16)
    dv_ref[...] += lax.dot_general(
        probs.astype(jnp.bfloat16), grad, CONTRACT_FIRST, preferred_element_type=jnp.float32
    )
    dk_ref[...] += lax.dot_general(
        score_grad, q_ref[...], CONTRACT_FIRST, preferred_element_type=jnp.float32
    )
    dq_ref[...] = jnp.dot(score_grad, k_ref[...], preferred_element_type=jnp.float32)


def attend_back(queries, key_rows, value_rows, context, log_total, grad, block):
    rows, size = queries.shape
    part = pl.BlockSpec((block, size), lambda i: (i, 0))
    whole = pl.BlockSpec((rows, size), lambda i: (0, 0))
    return pl.pallas_call(
        attend_back_kernel,
        grid=(rows // block,),
        out_shape=(jax.ShapeDtypeStruct((rows, size), jnp.float32),) * 3,
        in_specs=[
            part,
            whole,
            whole,
            part,
            pl.BlockSpec((block, 1), lambda i: (i, 0)),
            part,
        ],
        out_specs=(part, whole, whole),
        compiler_params=pltpu.CompilerParams(vmem_limit_bytes=48 * 1024 * 1024),
    )(queries, key_rows, value_rows, context, log_total, grad)


def whole_mesh(me):
    def other(step):
        place = lax.rem(me + step, 32)
        return place, (place // 4, lax.rem(place, 4))

    return other


def greet_all(other):
    barrier = pltpu.get_barrier_semaphore()

    @pl.loop(1, 32)
    def _(step):
        pl.semaphore_signal(barrier, inc=1, device_id=other(step)[1], device_id_type=MESH_ID)

    pl.semaphore_wait(barrier, 31)


def swap_lanes(value):
    return pltpu.roll(value.astype(jnp.float32), 64, 1)


def low_lanes(value):
    return lax.broadcasted_iota(jnp.int32, value.shape, 1) < 64


def weight_piece(ref, by_rows, half, index, count):
    if by_rows:
        size = ref.shape[0] // (2 * count)
        start = pl.multiple_of((half * count + index) * size, 16)
        return ref.at[pl.ds(start, size), :]
    size = ref.shape[1] // (2 * count)
    start = pl.multiple_of((half * count + index) * size, 128)
    return ref.at[:, pl.ds(start, size)]


def forward_kernel(cuts, scaling, *refs):
    count = len(cuts)
    x_ref, cos_ref, sin_ref, gain_ref = refs[:4]
    shards = refs[4 : 4 + count]
    normed_ref, gains, got, context, log_ref, back = refs[4 + count : 10 + count]
    fulls = refs[10 + count : 10 + 2 * count]
    (sent, keys, values, packed, head_send, head_recv, back_send, back_recv, own_sem) = refs[
        10 + 2 * count : 19 + 2 * count
    ]
    w_send, w_recv = refs[19 + 2 * count :]
    targets, proj = fulls, fulls[0]
    z, y, x, core = mesh_place()
    place = 2 * x + core
    me = 4 * (2 * z + y) + place
    across = lax.rem(place + 2, 4)
    other = whole_mesh(me)
    sibling, partner = device_at(z, y, x, 1 - core), device_at(z, y, 1 - x, core)
    corner = device_at(z, y, 1 - x, 1 - core)
    neighbour = device_at(z, 1 - y, x, core)
    greet_all(other)

    def head_copy(step):
        to, device = other(step)
        return pltpu.make_async_remote_copy(
            src_ref=sent.at[to],
            dst_ref=got.at[me],
            send_sem=head_send.at[step],
            recv_sem=head_recv.at[step],
            device_id=device,
            device_id_type=MESH_ID,
        )

    def back_copy(to):
        step = lax.rem(to - me + 32, 32)
        return pltpu.make_async_remote_copy(
            src_ref=packed.at[to],
            dst_ref=back.at[me],
            send_sem=back_send.at[step],
            recv_sem=back_recv.at[step],
            device_id=(to // 4, lax.rem(to, 4)),
            device_id_type=MESH_ID,
        )

    send = sender(w_send, w_recv)
    crossing, handed, turned = [], [], []

    todo = [(i, c) for i in range(count) for c in range(cuts[i][1])]
    first = cuts[0][1]

    def cross(pieces=1):
        for i, c in todo[len(crossing) :][:pieces]:
            src = weight_piece(shards[i], cuts[i][0], y, c, cuts[i][1])
            dst = weight_piece(targets[i].at[place], cuts[i][0], y, c, cuts[i][1])
            crossing.append((i, c, send(src, dst, partner)))

    def keep(i):
        copy = pltpu.make_async_copy(shards[i], targets[i].at[place], own_sem.at[i])
        copy.start()
        return copy

    def turn(entry):
        i, c, copy = entry
        copy.wait_recv()
        here = weight_piece(targets[i].at[across], cuts[i][0], y, c, cuts[i][1])
        turned.append((i, c, send(here, here, neighbour)))
        cross()
        handed.append(send(here, here, sibling))

    def hand(entry):
        i, c, copy = entry
        copy.wait_recv()
        here = weight_piece(targets[i].at[across], cuts[i][0], 1 - y, c, cuts[i][1])
        handed.append(send(here, here, sibling))

    gain_moves = [
        send(gain_ref, gains.at[place], device) for device in (sibling, partner, corner)
    ]
    cross(AHEAD)
    handed.append(send(shards[0], proj.at[place], sibling))
    kept = pltpu.make_async_copy(gain_ref, gains.at[place], own_sem.at[count])
    kept.start()
    owns = [keep(0)]
    states = x_ref[...].astype(jnp.float32)
    centred = states - jnp.mean(states, axis=-1, keepdims=True)
    spread = jnp.mean(centred * centred, axis=-1, keepdims=True)
    centred = centred * lax.rsqrt(spread + eps)
    kept.wait()
    for copy in gain_moves:
        copy.wait()
    for f in range(4):
        part = centred[:, f * 256 : (f + 1) * 256] * gains[f, 0:1, :].astype(jnp.float32)
        normed_ref[:, f * 256 : (f + 1) * 256] = part.astype(jnp.bfloat16)
    for c in range(first):
        turn(crossing[c])
    for c in range(first):
        hand(turned[c])
    owns[0].wait()
    for copy in handed[: 1 + 2 * first]:
        copy.wait_recv()
    cos = jnp.concatenate([cos_ref[...]] * 2, axis=1)
    sin = jnp.concatenate([sin_ref[...]] * 2, axis=1)

    def turn_heads(value):
        lane = lax.rem(lax.broadcasted_iota(jnp.int32, value.shape, 1), 64)
        turned_lanes = jnp.where(lane < 32, -pltpu.roll(value, 224, 1), pltpu.roll(value, 32, 1))
        return value * cos + turned_lanes * sin

    @pl.loop(0, 4)
    def _(quad):
        def product(start):
            columns = pl.ds(pl.multiple_of(start + quad * 256, 128), 256)
            total = jnp.dot(
                normed_ref[:, :256], proj[0, :, columns], preferred_element_type=jnp.float32
            )
            for f in range(1, 4):
                total += jnp.dot(
                    normed_ref[:, f * 256 : (f + 1) * 256],
                    proj[f, :, columns],
                    preferred_element_type=jnp.float32,
                )
            return total

        queries = turn_heads(product(0)).astype(jnp.bfloat16).astype(jnp.float32) * scaling
        key_rows = turn_heads(product(1024))
        value_rows = product(2048)
        for pair in range(2):
            lanes = slice(pair * 128, (pair + 1) * 128)
            q, k, v = queries[:, lanes], key_rows[:, lanes], value_rows[:, lanes]
            swapped_q, swapped_k = pltpu.roll(q, 64, 1), pltpu.roll(k, 64, 1)
            even = jnp.where(low_lanes(q), q, swapped_k).astype(jnp.bfloat16)
            odd = jnp.where(low_lanes(q), swapped_q, k).astype(jnp.bfloat16)
            swapped_v = pltpu.roll(v, 64, 1)
            for seq in range(2):
                head = seq * 16 + quad * 4 + pair * 2
                low, mid, high = seq * 64, seq * 64 + 32, seq * 64 + 64
                sent[head, 0:64] = even[low:high]
                sent[head + 1, 0:64] = odd[low:high]
                mask = low_lanes(v[low:mid])
                sent[head, 64:96] = jnp.where(mask, v[low:mid], swapped_v[mid:high]).astype(
                    jnp.bfloat16
                )
                sent[head + 1, 64:96] = jnp.where(mask, swapped_v[low:mid], v[mid:high]).astype(
                    jnp.bfloat16
                )

    @pl.loop(1, 32)
    def _(step):
        head_copy(step).start()

    own_head = pltpu.make_async_copy(sent.at[me], got.at[me], own_sem.at[count + 1])
    own_head.start()
    for i in range(1, count):
        owns.append(keep(i))
        handed.append(send(shards[i], targets[i].at[place], sibling))
    for c in range(first, first + 3):
        turn(crossing[c])
    hand(turned[first])
    own_head.wait()

    @pl.loop(1, 32)
    def _(step):
        head_copy(step).wait()

    keys[0:1024] = got[:, 0:32, :].reshape(1024, 128)
    keys[1024:2048] = got[:, 32:64, :].reshape(1024, 128)
    values[...] = got[:, 64:96, :].reshape(1024, 128)

    def attend_block(b):
        block = lax.rem(b + me // 4, 8)
        low_rows = pl.ds(pl.multiple_of(block * 128, 128), 128)
        high_rows = pl.ds(pl.multiple_of(1024 + block * 128, 128), 128)
        queries = swap_lanes(jnp.concatenate([keys[low_rows], keys[high_rows]], axis=0))
        queries = jnp.where(low_lanes(queries), 0.0, queries).astype(jnp.bfloat16)
        scores = lax.dot_general(
            queries, keys[...], CONTRACT_LAST, preferred_element_type=jnp.float32
        )
        top = jnp.max(scores, axis=-1, keepdims=True)
        weights = jnp.exp(scores - top)
        total = jnp.sum(weights, axis=-1, keepdims=True)
        weights = weights.astype(jnp.bfloat16)
        first = jnp.dot(weights[:, :1024], values[...], preferred_element_type=jnp.float32)
        second = jnp.dot(weights[:, 1024:], values[...], preferred_element_type=jnp.float32)
        outcome = (first + pltpu.roll(second, 64, 1)) / total
        side = pltpu.roll(outcome[128:], 64, 1)
        outcome = jnp.where(low_lanes(side), outcome[:128], side)
        context[low_rows] = outcome
        log_total = top + jnp.log(total)
        log_ref[0, low_rows] = log_total[:128]
        log_ref[1, low_rows] = log_total[128:]
        packed[pl.ds(4 * block, 4)] = outcome.astype(jnp.bfloat16).reshape(4, 32, 128)

        @pl.loop(4 * block, 4 * block + 4)
        def _(to):
            @pl.when(to != me)
            def _():
                back_copy(to).start()

    turn(crossing[first + 3])
    hand(turned[first + 1])

    @pl.loop(0, 4)
    def _(b):
        attend_block(b)

    turn(crossing[first + 4])
    hand(turned[first + 2])

    @pl.loop(4, 8)
    def _(b):
        attend_block(b)

    mine = pltpu.make_async_copy(packed.at[me], back.at[me], own_sem.at[count + 2])
    mine.start()
    owns.append(mine)
    for index in range(first + 5, len(todo)):
        turn(crossing[index])
        hand(turned[index - 2])
    hand(turned[-2])
    hand(turned[-1])

    @pl.loop(1, 32)
    def _(step):
        back_copy(lax.rem(me + step, 32)).wait()

    for copy in handed[1 + 2 * first :]:
        copy.wait_recv()
    for copy in handed:
        copy.wait_send()
    for _, _, copy in crossing + turned:
        copy.wait_send()
    for copy in owns[1:]:
        copy.wait()


def forward_heads(rows, cos_table, sin_table, gain, shards, cuts, scaling, collective_id):
    in_vmem, anywhere = pl.BlockSpec(memory_space=pltpu.VMEM), pl.BlockSpec(memory_space=pl.ANY)
    copies = 3 + len(shards) + sum(4 * pieces for _, pieces in cuts)
    low, full = jnp.bfloat16, jnp.float32
    sems = [pltpu.SemaphoreType.DMA((32,))] * 4
    proj, *rest = shards
    return pl.pallas_call(
        functools.partial(forward_kernel, cuts, scaling),
        out_shape=[
            jax.ShapeDtypeStruct(rows.shape, low),
            jax.ShapeDtypeStruct((4, *gain.shape), low),
            jax.ShapeDtypeStruct((32, 96, 128), low),
            jax.ShapeDtypeStruct((1024, 128), full),
            jax.ShapeDtypeStruct((2, 1024, 1), full),
            jax.ShapeDtypeStruct((32, 32, 128), low),
        ]
        + [jax.ShapeDtypeStruct((4, *shard.shape), low) for shard in shards],
        in_specs=[in_vmem] * (4 + len(shards)),
        out_specs=[in_vmem] * 7 + [anywhere] * len(rest),
        scratch_shapes=[
            pltpu.VMEM((32, 96, 128), low),
            pltpu.VMEM((2048, 128), low),
            pltpu.VMEM((1024, 128), low),
            pltpu.VMEM((32, 32, 128), low),
            *sems,
            pltpu.SemaphoreType.DMA((len(shards) + 3,)),
            pltpu.SemaphoreType.DMA((copies,)),
            pltpu.SemaphoreType.DMA((copies,)),
        ],
        compiler_params=pltpu.CompilerParams(
            collective_id=collective_id,
            has_side_effects=True,
            vmem_limit_bytes=56 * 1024 * 1024,
        ),
    )(rows, cos_table, sin_table, gain, *shards)


def back_kernel(kinds, cuts, scaling, *refs):
    count = len(kinds)
    sent, got, context, log_ref, cos_ref, sin_ref = refs[:6]
    parts, result = refs[6 : 6 + count], refs[6 + count]
    outs = refs[7 + count : 7 + 2 * count]
    (grads, keys, values, dq, dk, dv, packed, go_send, go_recv, back_send, back_recv, mine_sem) = refs[
        7 + 2 * count : 19 + 2 * count
    ]
    me = lax.axis_index("ctx") * 4 + lax.axis_index("fsdp")
    other = whole_mesh(me)
    greet_all(other)

    def go_copy(step):
        to, device = other(step)
        return pltpu.make_async_remote_copy(
            src_ref=sent.at[to],
            dst_ref=grads.at[me],
            send_sem=go_send.at[step],
            recv_sem=go_recv.at[step],
            device_id=device,
            device_id_type=MESH_ID,
        )

    def back_copy(to):
        step = lax.rem(to - me + 32, 32)
        return pltpu.make_async_remote_copy(
            src_ref=packed.at[to],
            dst_ref=result.at[me],
            send_sem=back_send.at[step],
            recv_sem=back_recv.at[step],
            device_id=(to // 4, lax.rem(to, 4)),
            device_id_type=MESH_ID,
        )

    @pl.loop(1, 32)
    def _(step):
        go_copy(step).start()

    mine = pltpu.make_async_copy(sent.at[me], grads.at[me], mine_sem.at[0])
    mine.start()
    start, turn, end = plane_moves(kinds, cuts, parts, outs, *refs[19 + 2 * count :])
    start(0, 1)
    keys[0:1024] = got[:, 0:32, :].reshape(1024, 128)
    keys[1024:2048] = got[:, 32:64, :].reshape(1024, 128)
    values[...] = got[:, 64:96, :].reshape(1024, 128)
    dk[...] = jnp.zeros_like(dk)
    dv[...] = jnp.zeros_like(dv)
    mine.wait()

    @pl.loop(1, 32)
    def _(step):
        go_copy(step).wait()

    start(1, 4)
    turn(2)

    def rows_of(block):
        return (
            pl.ds(pl.multiple_of(block * 128, 128), 128),
            pl.ds(pl.multiple_of(1024 + block * 128, 128), 128),
        )

    def grad_block(block):
        low_rows, high_rows = rows_of(block)
        queries = swap_lanes(jnp.concatenate([keys[low_rows], keys[high_rows]], axis=0))
        queries = jnp.where(low_lanes(queries), 0.0, queries).astype(jnp.bfloat16)
        pair = grads[pl.ds(4 * block, 4)].reshape(128, 128).astype(jnp.float32)
        side = pltpu.roll(pair, 64, 1)
        first = low_lanes(pair)
        grad = jnp.concatenate([jnp.where(first, pair, 0.0), jnp.where(first, side, 0.0)], axis=0)
        above = jnp.concatenate([jnp.where(first, 0.0, side), jnp.where(first, 0.0, pair)], axis=0)
        grad, above = grad.astype(jnp.bfloat16), above.astype(jnp.bfloat16)
        product = pair * context[low_rows]
        inner = jnp.concatenate(
            [
                jnp.sum(jnp.where(first, product, 0.0), axis=-1, keepdims=True),
                jnp.sum(jnp.where(first, 0.0, product), axis=-1, keepdims=True),
            ],
            axis=0,
        )
        log_total = jnp.concatenate([log_ref[0, low_rows], log_ref[1, low_rows]], axis=0)
        scores = lax.dot_general(
            queries, keys[...], CONTRACT_LAST, preferred_element_type=jnp.float32
        )
        probs = jnp.exp(scores - log_total)
        prob_grad = jnp.concatenate(
            [
                lax.dot_general(
                    side_grad, values[...], CONTRACT_LAST, preferred_element_type=jnp.float32
                )
                for side_grad in (grad, above)
            ],
            axis=1,
        )
        score_grad = (probs * (prob_grad - inner)).astype(jnp.bfloat16)
        dv[...] += lax.dot_general(
            probs.astype(jnp.bfloat16), grad, CONTRACT_FIRST, preferred_element_type=jnp.float32
        )
        dk[...] += lax.dot_general(
            score_grad, queries, CONTRACT_FIRST, preferred_element_type=jnp.float32
        )
        query_grad = jnp.dot(score_grad, keys[...], preferred_element_type=jnp.float32)
        dq[low_rows] = query_grad[:128]
        dq[high_rows] = query_grad[128:]

    @pl.loop(0, 4)
    def _(block):
        grad_block(block)

    start(4)
    turn(4)

    @pl.loop(4, 8)
    def _(block):
        grad_block(block)

    turn(3)

    def unrotated(rows):
        both = jnp.where(
            low_lanes(dk[rows]), pltpu.roll(dq[rows] * scaling, 64, 1), dk[rows]
        )
        sined = both * sin_ref[rows]
        lane = lax.rem(lax.broadcasted_iota(jnp.int32, both.shape, 1), 64)
        turned = jnp.where(lane < 32, pltpu.roll(sined, 96, 1), -pltpu.roll(sined, 32, 1))
        return (both * cos_ref[rows] + turned).astype(jnp.bfloat16).reshape(4, 32, 128)

    @pl.loop(0, 8)
    def _(b):
        block = lax.rem(b + me // 4, 8)
        low_rows, high_rows = rows_of(block)
        places = pl.ds(4 * block, 4)
        packed[places, 0:32, :] = unrotated(low_rows)
        packed[places, 32:64, :] = unrotated(high_rows)
        side = pltpu.roll(dv[high_rows], 64, 1)
        value_pair = jnp.where(low_lanes(side), dv[low_rows], side)
        packed[places, 64:96, :] = value_pair.astype(jnp.bfloat16).reshape(4, 32, 128)

        @pl.loop(4 * block, 4 * block + 4)
        def _(to):
            @pl.when(to != me)
            def _():
                back_copy(to).start()

    own = pltpu.make_async_copy(packed.at[me], result.at[me], mine_sem.at[1])
    own.start()
    turn(64)

    @pl.loop(1, 32)
    def _(step):
        back_copy(lax.rem(me + step, 32)).wait()

    own.wait()
    end()


def back_heads(sent, saved, tables, parts, kinds, widths, cuts, scaling, collective_id):
    in_vmem, anywhere = pl.BlockSpec(memory_space=pltpu.VMEM), pl.BlockSpec(memory_space=pl.ANY)
    low, full, rows = jnp.bfloat16, jnp.float32, parts[0].shape[-2]
    result, *outs = pl.pallas_call(
        functools.partial(back_kernel, kinds, cuts, scaling),
        out_shape=[jax.ShapeDtypeStruct((32, 96, 128), low)]
        + [jax.ShapeDtypeStruct((4, rows, width), low) for width in widths],
        in_specs=[in_vmem] * (6 + len(parts)),
        out_specs=[in_vmem] + [anywhere] * len(parts),
        scratch_shapes=[
            pltpu.VMEM((32, 32, 128), low),
            pltpu.VMEM((2048, 128), low),
            pltpu.VMEM((1024, 128), low),
            pltpu.VMEM((2048, 128), full),
            pltpu.VMEM((2048, 128), full),
            pltpu.VMEM((2048, 128), full),
            pltpu.VMEM((32, 96, 128), low),
            *[pltpu.SemaphoreType.DMA((32,))] * 4,
            pltpu.SemaphoreType.DMA((2,)),
            pltpu.SemaphoreType.DMA((3 * sum(cuts),)),
            pltpu.SemaphoreType.DMA((3 * sum(cuts),)),
            pltpu.SemaphoreType.DMA((len(parts),)),
        ],
        compiler_params=pltpu.CompilerParams(
            collective_id=collective_id,
            has_side_effects=True,
            vmem_limit_bytes=56 * 1024 * 1024,
        ),
    )(sent, *saved, *tables, *parts)
    return result, [out.reshape(4 * rows, width) for out, width in zip(outs, widths)]


def by_head_forward(mixed_rows, cos_table, sin_table, scaling):
    seq_count, row_count, _, head_count, head_size = mixed_rows.shape
    ctx_count, fsdp_count = lax.axis_size("ctx"), lax.axis_size("fsdp")
    count = ctx_count * fsdp_count
    queries = rotate(mixed_rows[:, :, 0], cos_table, sin_table).astype(jnp.bfloat16) * scaling
    key_rows = rotate(mixed_rows[:, :, 1], cos_table, sin_table).astype(jnp.bfloat16)
    value_rows = mixed_rows[:, :, 2].astype(jnp.bfloat16)
    to_head = lambda rows: rows.transpose(0, 2, 1, 3).reshape(count, row_count, head_size)
    sent = jnp.concatenate(
        [
            jnp.concatenate([to_head(queries), to_head(key_rows)], axis=-1),
            pack(to_head(value_rows)),
        ],
        axis=1,
    )
    got = exchange(sent, ctx_count, fsdp_count, 1)
    flat = lambda rows: rows.reshape(count * row_count, head_size)
    queries = flat(got[:, :row_count, :head_size])
    key_rows = flat(got[:, :row_count, head_size:])
    value_rows = flat(unpack(got[:, row_count:]))
    context, log_total = attend(queries, key_rows, value_rows, 256)
    back = exchange(
        pack(context.astype(jnp.bfloat16).reshape(count, row_count, head_size)),
        ctx_count,
        fsdp_count,
        2,
    )
    context_low = (
        unpack(back)
        .reshape(seq_count, head_count, row_count, head_size)
        .transpose(0, 2, 1, 3)
        .reshape(seq_count * row_count, head_count * head_size)
    )
    return context_low, (queries, key_rows, value_rows, context, log_total)


def by_head_back(context_grad, saved, scaling, after, planes=()):
    seq_count, row_count, head_count, head_size = context_grad.shape
    ctx_count, fsdp_count = lax.axis_size("ctx"), lax.axis_size("fsdp")
    count = ctx_count * fsdp_count
    if planes:
        sent = pack(context_grad.transpose(0, 2, 1, 3).reshape(count, row_count, head_size))
        order = jnp.arange(count * row_count, dtype=jnp.int32)
        order = order.reshape(count, 2, row_count // 2).transpose(1, 0, 2).reshape(-1)
        tables = [jnp.tile(table[:, 0], (1, 2)) for table in angles(order, head_size)]
        got, lefts = back_heads(sent, saved, tables, *planes, scaling, 2)
        parts = jnp.stack(
            [
                got[:, :row_count, :head_size],
                got[:, :row_count, head_size:],
                unpack(got[:, row_count:]),
            ]
        )
        return (
            parts.reshape(3, seq_count, head_count, row_count, head_size)
            .transpose(1, 3, 0, 2, 4)
            .reshape(seq_count * row_count, 3 * head_count * head_size)
        ), lefts
    queries, key_rows, value_rows, context, log_total = saved
    sent = pack(context_grad.transpose(0, 2, 1, 3).reshape(count, row_count, head_size))
    grad = unpack(exchange(sent, ctx_count, fsdp_count, 3)).reshape(count * row_count, head_size)
    query_grad, key_grad, value_grad = attend_back(
        queries, key_rows, value_rows, context, log_total, grad, 256
    )
    cos_all, sin_all = angles(jnp.arange(count * row_count, dtype=jnp.int32), head_size)
    cos_all, sin_all = cos_all[:, 0], sin_all[:, 0]
    query_pre = unrotate(query_grad * scaling, cos_all, sin_all).astype(jnp.bfloat16)
    key_pre = unrotate(key_grad, cos_all, sin_all).astype(jnp.bfloat16)
    split = lambda rows: rows.reshape(count, row_count, head_size)
    sent = jnp.concatenate(
        [
            jnp.concatenate([split(query_pre), split(key_pre)], axis=-1),
            pack(split(value_grad.astype(jnp.bfloat16))),
        ],
        axis=1,
    )
    if after:
        sent, after = lax.optimization_barrier((sent, after))
    got = exchange(sent, ctx_count, fsdp_count, 4)
    parts = jnp.stack(
        [got[:, :row_count, :head_size], got[:, :row_count, head_size:], unpack(got[:, row_count:])]
    )
    return (
        parts.reshape(3, seq_count, head_count, row_count, head_size)
        .transpose(1, 3, 0, 2, 4)
        .reshape(seq_count * row_count, 3 * head_count * head_size)
    ), after


def by_block_forward(mixed_rows, cos_table, sin_table, scaling):
    seq_count, row_count, _, head_count, head_size = mixed_rows.shape
    width = head_count * head_size
    queries = rotate(mixed_rows[:, :, 0], cos_table, sin_table).astype(jnp.bfloat16)
    key_flat = (
        rotate(mixed_rows[:, :, 1], cos_table, sin_table)
        .astype(jnp.bfloat16)
        .reshape(seq_count, row_count, width)
    )
    value_flat = mixed_rows[:, :, 2].astype(jnp.bfloat16).reshape(seq_count, row_count, width)
    key_block, value_block = (
        lax.all_gather(key_flat, "fsdp", axis=1, tiled=True),
        lax.all_gather(value_flat, "fsdp", axis=1, tiled=True),
    )
    start_state = empty_state(seq_count, head_count, row_count, head_size)
    running_max, denominator, weighted = forward_step(
        queries,
        scaling,
        start_state,
        (
            lax.all_gather(key_block, "ctx", axis=1, tiled=True),
            lax.all_gather(value_block, "ctx", axis=1, tiled=True),
        ),
    )
    context = (weighted / denominator[..., None]).transpose(0, 2, 1, 3)
    log_total = running_max + jnp.log(denominator)
    context_low = context.reshape(seq_count * row_count, width).astype(jnp.bfloat16)
    saved = queries, key_block, value_block, context, log_total, cos_table, sin_table
    return context_low, saved


def by_block_back(context_grad, saved, scaling, after, planes=()):
    seq_count, row_count, head_count, head_size = context_grad.shape
    width = head_count * head_size
    queries, key_block, value_block, context, log_total, cos_table, sin_table = saved
    inner = jnp.sum(context_grad.astype(jnp.float32) * context, axis=-1)
    inner_heads = inner.transpose(0, 2, 1)
    log_rows = log_total.transpose(0, 2, 1)
    query_grad = query_step(
        queries,
        context_grad,
        log_total,
        inner_heads,
        scaling,
        (
            lax.all_gather(key_block, "ctx", axis=1, tiled=True),
            lax.all_gather(value_block, "ctx", axis=1, tiled=True),
        ),
    )
    block_len = key_block.shape[1]
    query_wide = queries.reshape(seq_count, row_count, width).astype(jnp.float32)
    grad_wide = context_grad.reshape(seq_count, row_count, width).astype(jnp.float32)
    key_grad, value_grad = key_step(
        as_heads(key_block, head_size),
        as_heads(value_block, head_size),
        scaling,
        (
            lax.all_gather(query_wide, "ctx", axis=1, tiled=True),
            lax.all_gather(grad_wide, "ctx", axis=1, tiled=True),
            lax.all_gather(log_rows, "ctx", axis=1, tiled=True),
            lax.all_gather(inner, "ctx", axis=1, tiled=True),
        ),
    )
    own = lambda grad: lax.psum_scatter(
        grad.reshape(seq_count, block_len, width), "fsdp", scatter_dimension=1, tiled=True
    ).reshape(seq_count, row_count, head_count, head_size)
    query_pre = unrotate(query_grad * scaling, cos_table, sin_table)
    key_pre = unrotate(own(key_grad) * scaling, cos_table, sin_table)
    return (
        jnp.stack([query_pre, key_pre, own(value_grad)], axis=2)
        .reshape(seq_count * row_count, 3 * width)
        .astype(jnp.bfloat16)
    ), after


def group_rows(rows):
    return lax.all_gather(rows, "fsdp", axis=0, tiled=True)


def group_columns(arrays):
    count = lax.axis_size("fsdp")
    widths = [rows.shape[1] // count for rows in arrays]
    sent = jnp.stack(
        [
            jnp.concatenate(
                [rows[:, f * width : (f + 1) * width] for rows, width in zip(arrays, widths)],
                axis=1,
            )
            for f in range(count)
        ]
    )
    got = lax.all_to_all(sent, "fsdp", split_axis=0, concat_axis=0, tiled=True)
    got = got.reshape(-1, sum(widths))
    edges = [sum(widths[:i]) for i in range(len(widths) + 1)]
    return [got[:, edges[i] : edges[i + 1]] for i in range(len(widths))]


def weight_grad(left, right):
    return jnp.einsum("tw,tf->wf", left, right, preferred_element_type=jnp.float32)


def mesh_place():
    ctx, place = lax.axis_index("ctx"), lax.axis_index("fsdp")
    return ctx // 2, lax.rem(ctx, 2), place // 2, lax.rem(place, 2)


def device_at(z, y, x, core):
    return (2 * z + y, 2 * x + core)


def greet(barrier, devices):
    for device in devices:
        pl.semaphore_signal(barrier, inc=1, device_id=device, device_id_type=MESH_ID)
    pl.semaphore_wait(barrier, len(devices))


def spans(total, count):
    edges = [total * i // (count * 16) * 16 for i in range(count)] + [total]
    return list(zip(edges[:-1], edges[1:]))


def sender(send_sem, recv_sem):
    serial = iter(range(send_sem.shape[0]))

    def send(src, dst, device):
        sem = next(serial)
        copy = pltpu.make_async_remote_copy(
            src_ref=src,
            dst_ref=dst,
            send_sem=send_sem.at[sem],
            recv_sem=recv_sem.at[sem],
            device_id=device,
            device_id_type=MESH_ID,
        )
        copy.start()
        return copy

    return send


def plane_moves(kinds, cuts, ins, outs, send_sem, recv_sem, own_sem):
    z, y, x, core = mesh_place()
    to_x, to_y = device_at(z, y, 1 - x, core), device_at(z, 1 - y, x, core)
    send = sender(send_sem, recv_sem)
    firsts, seconds, owns = [], [], []

    def block(i, index):
        ref, width = ins[i], outs[i].shape[2]
        if len(ref.shape) == 3:
            return ref.at[index]
        step = ref.shape[1] - width
        return ref.at[:, pl.ds(pl.multiple_of(index * step, 128), width)]

    def start(low_part=0, high_part=len(kinds)):
        for i, kind in list(enumerate(kinds))[low_part:high_part]:
            own = block(i, y if kind else x)
            away = block(i, 1 - y if kind else 1 - x)
            for low, high in spans(outs[i].shape[1], cuts[i]):
                rows = pl.ds(low, high - low)
                by_x = send((own if kind else away).at[rows], outs[i].at[1, rows], to_x)
                by_y = send((away if kind else own).at[rows], outs[i].at[2, rows], to_y)
                firsts.append((i, rows, by_x, by_y))
        for i, kind in list(enumerate(kinds))[low_part:high_part]:
            own = block(i, y if kind else x)
            copy = pltpu.make_async_copy(own, outs[i].at[0], own_sem.at[i])
            copy.start()
            owns.append(copy)

    def turn(count):
        for i, rows, by_x, by_y in firsts[len(seconds) :][:count]:
            if kinds[i]:
                by_y.wait_recv()
                seconds.append(send(outs[i].at[2, rows], outs[i].at[3, rows], to_x))
            else:
                by_x.wait_recv()
                seconds.append(send(outs[i].at[1, rows], outs[i].at[3, rows], to_y))

    def end():
        turn(len(firsts))
        for i, rows, by_x, by_y in firsts:
            (by_x if kinds[i] else by_y).wait_recv()
            by_x.wait_send()
            by_y.wait_send()
        for copy in seconds:
            copy.wait()
        for copy in owns:
            copy.wait()

    return start, turn, end


def finish_kernel(chunks, count, *refs):
    mixed, left, gains = refs[count - 1 : count + 2]
    outs, gain_got = refs[count + 2 : 2 * count + 2], refs[2 * count + 2]
    scratch = refs[2 * count + 3 :]
    core_got, z_got, mid_got, z_sent = (scratch[i * count : (i + 1) * count] for i in range(4))
    send_sem, recv_sem, gain_send, gain_recv, own_sem, last, right = scratch[
        4 * count : 4 * count + 7
    ]
    parts = (*refs[: count - 1], last)
    z, y, x, core = mesh_place()
    me = lax.axis_index("ctx") * 4 + lax.axis_index("fsdp")
    total = len(chunks)
    barrier = pltpu.get_barrier_semaphore()

    def other(step):
        place = lax.rem(me + step, 32)
        return place, (place // 4, lax.rem(place, 4))

    @pl.loop(1, 32)
    def _(step):
        pl.semaphore_signal(barrier, inc=1, device_id=other(step)[1], device_id_type=MESH_ID)

    pl.semaphore_wait(barrier, 31)

    def send(stage, k, src, dst, device):
        return pltpu.make_async_remote_copy(
            src_ref=src,
            dst_ref=dst,
            send_sem=send_sem.at[stage * total + k],
            recv_sem=recv_sem.at[stage * total + k],
            device_id=device,
            device_id_type=MESH_ID,
        )

    def at(k):
        i, low, high = chunks[k]
        return i, pl.ds(low, high - low)

    def core_copy(k):
        i, rows = at(k)
        return send(
            0, k, parts[i].at[1 - core, rows], core_got[i].at[rows], device_at(z, y, x, 1 - core)
        )

    def inward(k):
        i, rows = at(k)
        return send(
            1, k, z_sent[i].at[rows], z_got[i].at[rows], device_at(1 + z // 2, y, x, core)
        )

    def middle(k):
        i, rows = at(k)
        return send(2, k, z_sent[i].at[rows], mid_got[i].at[rows], device_at(3 - z, y, x, core))

    def outward(k):
        i, rows = at(k)
        here = outs[i].at[y, rows]
        return send(3, k, here, here, device_at(3 * (z // 2), y, x, core))

    def across(k):
        i, rows = at(k)
        here = outs[i].at[y, rows]
        return send(4, k, here, here, device_at(z, 1 - y, x, core))

    def gain_copy(step):
        place, device = other(step)
        return pltpu.make_async_remote_copy(
            src_ref=gains.at[lax.rem(place, 4)],
            dst_ref=gain_got.at[me],
            send_sem=gain_send.at[step],
            recv_sem=gain_recv.at[step],
            device_id=device,
            device_id_type=MESH_ID,
        )

    def wide(value):
        return value.astype(jnp.float32)

    outer = (z == 0) | (z == 3)
    late = [k for k in range(total) if chunks[k][0] == count - 1][0]
    start, turn, end = plane_moves((1,), (4,), (mixed,), (right,), *scratch[4 * count + 7 :])
    for k in range(AHEAD):
        core_copy(k).start()
    start()
    own = pltpu.make_async_copy(gains.at[lax.rem(me, 4)], gain_got.at[me], own_sem)
    own.start()

    @pl.loop(1, 32)
    def _(step):
        gain_copy(step).start()

    def meet(k):
        @pl.when(outer)
        def _():
            if k >= LAG:
                outward(k - LAG).wait_recv()
                across(k - LAG).start()

        if k < 1 or k > total:
            return
        i, rows = at(k - 1)

        @pl.when(jnp.logical_not(outer))
        def _():
            middle(k - 1).wait_recv()
            value = wide(z_sent[i][rows]) + wide(mid_got[i][rows])
            outs[i][y, rows] = value.astype(jnp.bfloat16)
            outward(k - 1).start()
            across(k - 1).start()

    for k in range(total):
        i, rows = at(k)
        if 2 <= k < 6:
            turn(1)
        if k == late - AHEAD:
            end()
            for half in range(2):
                block = left[0:128, half * 256 : (half + 1) * 256]
                value = lax.dot_general(
                    block, right[0], CONTRACT_FIRST, preferred_element_type=jnp.float32
                )
                for source in range(1, 4):
                    block = left[source * 128 : (source + 1) * 128, half * 256 : (half + 1) * 256]
                    value += lax.dot_general(
                        block, right[source], CONTRACT_FIRST, preferred_element_type=jnp.float32
                    )
                last[half] = value.astype(jnp.bfloat16)
        if k + AHEAD < total:
            core_copy(k + AHEAD).start()
        core_copy(k).wait_recv()
        value = wide(parts[i][core, rows]) + wide(core_got[i][rows])

        @pl.when(outer)
        def _():
            z_sent[i][rows] = value.astype(jnp.bfloat16)
            inward(k).start()

        @pl.when(jnp.logical_not(outer))
        def _():
            inward(k).wait_recv()
            z_sent[i][rows] = (value + wide(z_got[i][rows])).astype(jnp.bfloat16)
            middle(k).start()

        meet(k)

    for k in range(total, total + LAG):
        if k > total:

            @pl.when(outer)
            def _():
                outward(k - LAG).wait_recv()
                across(k - LAG).start()
        else:
            meet(k)

    @pl.when(outer)
    def _():
        for k in range(total):
            inward(k).wait_send()

    @pl.when(jnp.logical_not(outer))
    def _():
        for k in range(total):
            middle(k).wait_send()
            outward(k).wait_send()

    for k in range(total):
        i, rows = at(k)
        there = outs[i].at[1 - y, rows]
        send(4, k, there, there, device_at(z, 1 - y, x, core)).wait_recv()
        across(k).wait_send()
        core_copy(k).wait_send()
    own.wait()

    @pl.loop(1, 32)
    def _(step):
        gain_copy(step).wait()


def finish(parts, mixed, left, gains, cuts, collective_id):
    tokens, width = mixed.shape
    shapes = [part.shape for part in parts]
    shapes.append((2, left.shape[1] // 2, width // 2))
    count = len(shapes)
    chunks = [
        (i, low, high) for i, cut in enumerate(cuts) for low, high in spans(shapes[i][1], cut)
    ]
    buffers = [pltpu.VMEM(shape[1:], jnp.bfloat16) for shape in shapes]
    in_vmem = pl.BlockSpec(memory_space=pltpu.VMEM)
    return pl.pallas_call(
        functools.partial(finish_kernel, chunks, count),
        out_shape=[jax.ShapeDtypeStruct(shape, jnp.bfloat16) for shape in shapes]
        + [jax.ShapeDtypeStruct((32, 8, gains.shape[2]), jnp.float32)],
        in_specs=[in_vmem] * (count + 2),
        out_specs=[in_vmem] * (count + 1),
        scratch_shapes=buffers * 4
        + [
            pltpu.SemaphoreType.DMA((5 * len(chunks),)),
            pltpu.SemaphoreType.DMA((5 * len(chunks),)),
            pltpu.SemaphoreType.DMA((32,)),
            pltpu.SemaphoreType.DMA((32,)),
            pltpu.SemaphoreType.DMA,
            pltpu.VMEM(shapes[-1], jnp.bfloat16),
            pltpu.VMEM((4, tokens, width // 2), jnp.bfloat16),
            pltpu.SemaphoreType.DMA((12,)),
            pltpu.SemaphoreType.DMA((12,)),
            pltpu.SemaphoreType.DMA((1,)),
        ],
        compiler_params=pltpu.CompilerParams(
            collective_id=collective_id,
            has_side_effects=True,
            vmem_limit_bytes=56 * 1024 * 1024,
        ),
    )(*parts, mixed, left, gains)


def core_blocks(left, right):
    both = weight_grad(left, right).astype(jnp.bfloat16)
    return both.reshape(2, both.shape[0] // 2, both.shape[1])


def joined_halves(out, full):
    skip = 2 * out.shape[2] - full
    return jnp.concatenate([out[0], out[1][:, skip:]], axis=1).astype(jnp.float32)


def on_device(inputs, attn_gain, attn_proj, attn_out, mlp_gain, mlp_in, mlp_out, cotangent):
    seq_count, row_count, model_width = inputs.shape
    head_size = HEAD_DIM
    head_count = HEADS
    scaling = head_size ** (-0.5)
    fsdp_count = lax.axis_size("fsdp")
    fsdp_place = lax.axis_index("fsdp")
    device_count = lax.axis_size("ctx") * fsdp_count
    one_head_each = device_count == seq_count * head_count
    start_row = (lax.axis_index("ctx") * fsdp_count + fsdp_place) * row_count
    cos_table, sin_table = angles(start_row + jnp.arange(row_count, dtype=jnp.int32), head_size)
    tokens = seq_count * row_count
    gain_width = own_rows = attn_gain.shape[0]
    ctx_count = lax.axis_size("ctx")
    small = one_head_each and fsdp_count == 4 and ctx_count == 8
    states = inputs.astype(jnp.float32)
    attention, attention_back = (
        (by_head_forward, by_head_back) if one_head_each else (by_block_forward, by_block_back)
    )
    if small:
        gain_rows = jnp.concatenate(
            [attn_gain[None], mlp_gain[None], jnp.zeros((14, gain_width), attn_gain.dtype)], axis=0
        )
        normed_low, gains, got, context, log_total, back, *fulls = forward_heads(
            inputs.reshape(tokens, model_width),
            *(
                jnp.tile(table.reshape(row_count, head_size), (seq_count, 2))
                for table in (cos_table, sin_table)
            ),
            gain_rows,
            (attn_proj, attn_out, mlp_in, mlp_out),
            CUTS,
            scaling,
            1,
        )
        saved = got, context, log_total
        context_low = (
            unpack(back)
            .reshape(seq_count, head_count, row_count, head_size)
            .transpose(0, 2, 1, 3)
            .reshape(tokens, head_count * head_size)
        )
        proj_full, out_full, lift_full, down_full = (
            full.reshape(4 * full.shape[1], full.shape[2]) for full in fulls
        )
        gain_one = gains[:, 0, :].reshape(model_width).astype(jnp.float32)
        gain_two = gains[:, 1, :].reshape(model_width).astype(jnp.float32)
        _, norm_back_one = jax.vjp(layer_norm, states, gain_one)
    else:
        gains = lax.all_gather(jnp.stack([attn_gain, mlp_gain]), "fsdp", axis=1, tiled=True)
        gain_one, gain_two = gains.astype(jnp.float32)
        proj_full, out_full, lift_full, down_full = (
            lax.all_gather(rows, "fsdp", axis=0, tiled=True)
            for rows in (attn_proj, attn_out, mlp_in, mlp_out)
        )
        normed, norm_back_one = jax.vjp(layer_norm, states, gain_one)
        normed_low = normed.astype(jnp.bfloat16).reshape(tokens, model_width)
        mixed_rows = jnp.dot(normed_low, proj_full, preferred_element_type=jnp.float32).reshape(
            seq_count, row_count, 3, head_count, head_size
        )
        context_low, saved = attention(mixed_rows, cos_table, sin_table, scaling)
    branch = jnp.dot(context_low, out_full, preferred_element_type=jnp.float32).reshape(
        seq_count, row_count, model_width
    )
    middle = states + branch
    normed_two, norm_back_two = jax.vjp(layer_norm, middle, gain_two)
    normed_two_low = normed_two.astype(jnp.bfloat16).reshape(tokens, model_width)
    lifted = jnp.dot(normed_two_low, lift_full, preferred_element_type=jnp.float32)
    gate_out, gated_back = jax.vjp(gated_unit, lifted)
    gate_low = gate_out.astype(jnp.bfloat16)
    outputs = (
        middle
        + jnp.dot(gate_low, down_full, preferred_element_type=jnp.float32).reshape(
            seq_count, row_count, model_width
        )
    ).astype(jnp.bfloat16)
    seed_rows = cotangent.reshape(tokens, model_width)
    gate_grad = jnp.einsum("td,fd->tf", seed_rows, down_full, preferred_element_type=jnp.float32)
    lifted_grad = gated_back(gate_grad)[0].astype(jnp.bfloat16)
    normed_two_grad = jnp.einsum(
        "tf,wf->tw", lifted_grad, lift_full, preferred_element_type=jnp.float32
    ).reshape(seq_count, row_count, model_width)
    middle_part, gain_two_grad = norm_back_two(normed_two_grad)
    middle_grad = cotangent.astype(jnp.float32) + middle_part
    middle_low = middle_grad.reshape(tokens, model_width).astype(jnp.bfloat16)
    context_grad = (
        jnp.einsum("tv,wv->tw", middle_low, out_full, preferred_element_type=jnp.float32)
        .astype(jnp.bfloat16)
        .reshape(seq_count, row_count, head_count, head_size)
    )
    if small:
        width, lifted_width = model_width // 2, lifted_grad.shape[1]
        hidden = gate_low.shape[1] // 2
        lift_half = -(-lifted_width // 256) * 128
        gate_halves = jnp.stack([gate_low[:, :hidden], gate_low[:, hidden:]])
        planes = (
            (lifted_grad, normed_two_low, gate_halves, context_low, normed_low, seed_rows, middle_low),
            (1, 0, 0, 0, 0, 1, 1),
            (lift_half, width, hidden, width, width, width, width),
            (4, 1, 2, 1, 1, 1, 1),
        )
        mixed_grad, sides = attention_back(context_grad, saved, scaling, (), planes)
        lift_right, normed_two_left, gate_left, context_left, normed_left, seed_right, middle_right = (
            sides
        )
        lift_part = core_blocks(normed_two_left, lift_right)
        down_part = core_blocks(gate_left, seed_right)
        out_part = core_blocks(context_left, middle_right)
    else:
        normed_two_part, gate_part, context_part, normed_part = group_columns(
            (normed_two_low, gate_low, context_low, normed_low)
        )
        seed_group = group_rows(seed_rows)
        joined = group_rows(jnp.concatenate([lifted_grad, middle_low], axis=1))
        lift_grad = weight_grad(normed_two_part, joined[:, : lifted_grad.shape[1]])
        out_grad = weight_grad(context_part, joined[:, lifted_grad.shape[1] :])
        down_grad = weight_grad(gate_part, seed_group)
        first_grads = tuple(grad.astype(jnp.bfloat16) for grad in (lift_grad, down_grad, out_grad))
        mixed_grad, first_grads = attention_back(context_grad, saved, scaling, first_grads)
        mixed_group = group_rows(mixed_grad)
        proj_grad = weight_grad(normed_part, mixed_group).astype(jnp.bfloat16)
        lift_sum, down_sum, out_sum, proj_sum = (
            total.astype(jnp.float32) for total in lax.psum((*first_grads, proj_grad), "ctx")
        )
    normed_grad = jnp.einsum(
        "tm,wm->tw", mixed_grad, proj_full, preferred_element_type=jnp.float32
    ).reshape(seq_count, row_count, model_width)
    state_part, gain_one_grad = norm_back_one(normed_grad)
    input_grad = middle_grad + state_part
    gain_grads = jnp.stack([gain_one_grad, gain_two_grad])
    if small:
        shares = gain_grads.reshape(2, fsdp_count, gain_width).transpose(1, 0, 2)
        shares = jnp.concatenate([shares, jnp.zeros((fsdp_count, 6, gain_width))], axis=1)
        lift_sum, down_sum, out_sum, proj_sum, gain_got = finish(
            (lift_part, down_part, out_part), mixed_grad, normed_left, shares, (8, 4, 2, 4), 8
        )
        lift_sum = joined_halves(lift_sum, lifted_width)
        down_sum = joined_halves(down_sum, model_width)
        out_sum = joined_halves(out_sum, model_width)
        proj_sum = joined_halves(proj_sum, mixed_grad.shape[1])
        gain_own = jnp.sum(gain_got, axis=0)
    else:
        gain_sums = lax.psum(gain_grads, ("ctx", "fsdp"))
        gain_own = lax.dynamic_slice_in_dim(gain_sums, fsdp_place * gain_width, gain_width, axis=1)
    return (
        outputs,
        input_grad,
        gain_own[0],
        proj_sum,
        out_sum,
        gain_own[1],
        lift_sum,
        down_sum,
    )


def solution(mesh):
    in_specs = (
        P(None, ("ctx", "fsdp"), None),
        P("fsdp"),
        P("fsdp", None),
        P("fsdp", None),
        P("fsdp"),
        P("fsdp", None),
        P("fsdp", None),
        P(None, ("ctx", "fsdp"), None),
    )
    out_specs = (
        P(None, ("ctx", "fsdp"), None),
        P(None, ("ctx", "fsdp"), None),
        P("fsdp"),
        P("fsdp", None),
        P("fsdp", None),
        P("fsdp"),
        P("fsdp", None),
        P("fsdp", None),
    )
    return jax.shard_map(
        on_device, mesh=mesh, in_specs=in_specs, out_specs=out_specs, check_vma=False
    )
```
